128 devices in a mesh: fsdp: 16 (over x_hi, z, core), seq: 8 (over y, x_lo).
Axes of the slice: x: 4 (x_hi: 2, x_lo: 2; x = x_hi * 2 + x_lo), y: 4, z: 4, core: 2. Of those that a mesh axis runs over, the one named last changes fastest.
Arguments:
- tokens: bfloat16 [16, 1024, 768], P('fsdp', 'seq'), may hold values from -6 to 6
- doc_lengths: int32 [16, 4], P('fsdp'), may hold values from 1 to 896, as said below
- attn_gain: bfloat16 [768], P(('fsdp', 'seq')), may hold values from 0.5 to 1.5
- w_query: bfloat16 [768, 768], P(('fsdp', 'seq')), may hold values from -0.21875 to 0.21875
- w_key: bfloat16 [768, 768], P(('fsdp', 'seq')), may hold values from -0.21875 to 0.21875
- w_value: bfloat16 [768, 768], P(('fsdp', 'seq')), may hold values from -0.21875 to 0.21875
- w_out: bfloat16 [768, 768], P(('fsdp', 'seq')), may hold values from -1.75 to 1.75
- mlp_gain: bfloat16 [768], P(('fsdp', 'seq')), may hold values from 0.5 to 1.5
- w_gate: bfloat16 [768, 3072], P(('fsdp', 'seq')), may hold values from -0.21875 to 0.21875
- w_up: bfloat16 [768, 3072], P(('fsdp', 'seq')), may hold values from -0.21875 to 0.21875
- w_down: bfloat16 [3072, 768], P(('fsdp', 'seq')), may hold values from -0.109375 to 0.109375
- cotangent: bfloat16 [16, 1024, 768], P('fsdp', 'seq'), may hold values from -6 to 6
Outputs:
- layer_out: bfloat16 [16, 1024, 768], P('fsdp', 'seq')
- input_grad: float32 [16, 1024, 768], P('fsdp', 'seq')
- grad_attn_gain: float32 [768], P(('fsdp', 'seq'))
- grad_w_query: float32 [768, 768], P(('fsdp', 'seq'))
- grad_w_key: float32 [768, 768], P(('fsdp', 'seq'))
- grad_w_value: float32 [768, 768], P(('fsdp', 'seq'))
- grad_w_out: float32 [768, 768], P(('fsdp', 'seq'))
- grad_mlp_gain: float32 [768], P(('fsdp', 'seq'))
- grad_w_gate: float32 [768, 3072], P(('fsdp', 'seq'))
- grad_w_up: float32 [768, 3072], P(('fsdp', 'seq'))
- grad_w_down: float32 [3072, 768], P(('fsdp', 'seq'))
The draws below stay inside these ranges and needn't reach their ends.
Inputs may be any that keep to these rules, and one draw needn't show every extreme that they name: `doc_lengths`: in each pack the lengths sum to 1024; exactly one document has 896 positions, and it is neither the first nor the last; the others together have 128.
All inputs are finite; a program needn't handle non-finite values.
Results may differ from the reference program's by a relative error of at most 0.019.
Values may be sent and summed in bfloat16 or wider, within the bound.
A program may use at most 192 MiB of HBM per device.

```python
import math
import jax
import jax.numpy as jnp
from jax import lax

D = 768
HEADS = 12
KV_HEADS = 12
HEAD_DIM = 64
FF = 3072
TOK_DEV = 128
DOCS = 4
GROUPS = 16
PACK = 1024


def draw_doc_lengths(key, part):
    key = jax.random.fold_in(key, 7)

    def one_group(group_key):
        cut_key, slot_key = jax.random.split(group_key)
        cut_points = jnp.sort(jax.random.permutation(cut_key, TOK_DEV - 1)[:DOCS - 2] + 1).astype(jnp.int32)
        cut_edges = jnp.concatenate([jnp.zeros((1,), jnp.int32), cut_points, jnp.full((1,), TOK_DEV, jnp.int32)])
        shorts = cut_edges[1:] - cut_edges[:-1]
        long_slot = jax.random.randint(slot_key, (), 1, DOCS - 1)
        places = jnp.arange(DOCS, dtype=jnp.int32)
        source = jnp.clip(jnp.where(places < long_slot, places, places - 1), 0, DOCS - 2)
        return jnp.where(places == long_slot, PACK - TOK_DEV, shorts[source]).astype(jnp.int32)
    return jax.vmap(one_group)(jax.random.split(key, GROUPS))


def block_scale(rng, shape, cuts, low, largest):
    def one(dim, parts):
        steps = jax.random.uniform(jax.random.fold_in(jax.random.fold_in(rng, 6), dim), (parts,), jnp.float32, low / len(cuts), largest / len(cuts))
        return jnp.repeat(jnp.exp(steps), shape[dim] // parts).reshape((-1,) + (1,) * (len(shape) - dim - 1))

    loudness = one(*cuts[0])
    for cut in cuts[1:]:
        loudness = loudness * one(*cut)
    return loudness


def scatter_about(stream_key, extent, deviation, bound, cuts=(), kind=jnp.bfloat16):
    values = deviation * jax.random.normal(stream_key, extent, jnp.float32)
    if cuts:
        values = values * block_scale(stream_key, extent, cuts, -0.22, 0.18)
    return jnp.clip(values, -bound, bound).astype(kind)


def setup_inputs(seed: int = 0) -> dict:
    splits = jax.random.split(jax.random.key(seed), 13)
    tokens = scatter_about(splits[0], (GROUPS, PACK, D), 1.0, 6.0, ((0, 16), (1, 8)))
    doc_lengths = draw_doc_lengths(jax.random.fold_in(splits[12], 71), 0)
    attn_gain = jnp.clip(1.0 + 0.1 * jax.random.normal(splits[2], (D,), jnp.float32), 0.5, 1.5).astype(jnp.bfloat16)
    w_query = scatter_about(splits[3], (D, D), D ** -0.5, 0.21875, ((0, 128),))
    w_key = scatter_about(splits[4], (D, KV_HEADS * HEAD_DIM), D ** -0.5, 0.21875, ((0, 128),))
    w_value = scatter_about(splits[5], (D, KV_HEADS * HEAD_DIM), D ** -0.5, 0.21875, ((0, 128),))
    w_out = scatter_about(splits[6], (D, D), (D // 64) ** -0.5, 1.75, ((0, 128),))
    mlp_gain = jnp.clip(1.0 + 0.1 * jax.random.normal(splits[7], (D,), jnp.float32), 0.5, 1.5).astype(jnp.bfloat16)
    w_gate = scatter_about(splits[8], (D, FF), D ** -0.5, 0.21875, ((0, 128),))
    w_up = scatter_about(splits[9], (D, FF), D ** -0.5, 0.21875, ((0, 128),))
    w_down = scatter_about(splits[10], (FF, D), FF ** -0.5, 0.109375, ((0, 128),))
    cotangent = scatter_about(splits[11], (GROUPS, PACK, D), 1.0, 6.0, ((0, 16), (1, 8)))
    return dict(tokens=tokens, doc_lengths=doc_lengths, attn_gain=attn_gain, w_query=w_query, w_key=w_key, w_value=w_value, w_out=w_out, mlp_gain=mlp_gain, w_gate=w_gate, w_up=w_up, w_down=w_down, cotangent=cotangent)


EPSILON = 1e-05
ROPE_BASE = 10000.0
MASKED_SCORE = -1e+30

@jax.custom_vjp
def low(v):
    return lax.optimization_barrier(v.astype(jnp.bfloat16)).astype(jnp.float32)

@jax.custom_vjp
def low_back(v):
    return v

def low_keep(v):
    return (low(v), None)

def low_pass(kept, grad):
    return (grad,)

def back_keep(v):
    return (v, None)

def back_low(kept, grad):
    return (low(grad),)
low.defvjp(low_keep, low_pass)
low_back.defvjp(back_keep, back_low)

def rms_norm(values, gain):
    factor = lax.rsqrt(lax.optimization_barrier(jnp.mean(values * values, axis=-1, keepdims=True)) + EPSILON)
    return values * factor * gain

def rotate(values, position, head_count):
    half_dim = HEAD_DIM // 2
    freqs = ROPE_BASE ** (-(2.0 * jnp.arange(half_dim, dtype=jnp.float32)) / HEAD_DIM)
    angles = position.astype(jnp.float32)[:, None] * freqs[None, :]
    cosine = jnp.cos(angles)[:, None, :]
    sine = jnp.sin(angles)[:, None, :]
    shaped = values.reshape(values.shape[0], head_count, HEAD_DIM)
    first_half = shaped[..., :half_dim]
    second_half = shaped[..., half_dim:]
    turned = jnp.concatenate([first_half * cosine - second_half * sine, second_half * cosine + first_half * sine], axis=-1)
    return turned.reshape(values.shape[0], head_count * HEAD_DIM)

def doc_layout(lengths, pack_len):
    ends = jnp.cumsum(lengths).astype(jnp.int32)
    where_pos = jnp.arange(pack_len, dtype=jnp.int32)
    passed = where_pos[:, None] >= ends[None, :]
    segment = lax.optimization_barrier(jnp.sum(passed.astype(jnp.int32), axis=1)).astype(jnp.int32)
    start_pos = lax.optimization_barrier(jnp.sum(jnp.where(passed, lengths[None, :], 0), axis=1)).astype(jnp.int32)
    return (segment, (where_pos - start_pos).astype(jnp.int32))

def matmul(left, right):
    return jnp.dot(left, right, precision=lax.Precision.HIGHEST, preferred_element_type=jnp.float32)

def attend(queries, key_rows, value_rows, segment):
    block_rows = min(512, PACK)
    group_size = HEADS // KV_HEADS
    key_heads = key_rows.reshape(PACK, KV_HEADS, HEAD_DIM)
    value_heads = value_rows.reshape(PACK, KV_HEADS, HEAD_DIM)
    key_index = jnp.arange(PACK, dtype=jnp.int32)
    scale_value = 1.0 / math.sqrt(HEAD_DIM)

    def one_block(query_block, segment_block, block_start):
        query_heads = query_block.reshape(block_rows, KV_HEADS, group_size, HEAD_DIM)
        scores = jnp.einsum('qhgd,khd->hgqk', query_heads, key_heads, precision=lax.Precision.HIGHEST) * scale_value
        scores = low_back(scores)
        query_index = block_start + jnp.arange(block_rows, dtype=jnp.int32)
        allowed = (segment_block[:, None] == segment[None, :]) & (key_index[None, :] <= query_index[:, None])
        scores = jnp.where(allowed[None, None], scores, MASKED_SCORE)
        probabilities = low(jax.nn.softmax(scores, axis=-1))
        mixed_values = jnp.einsum('hgqk,khd->qhgd', probabilities, value_heads, precision=lax.Precision.HIGHEST)
        return mixed_values.reshape(block_rows, HEADS * HEAD_DIM)
    checked = jax.checkpoint(one_block)

    def run_block(block_item):
        return checked(block_item[0], block_item[1], block_item[2])
    block_count = PACK // block_rows
    starts = (jnp.arange(block_count, dtype=jnp.int32) * block_rows).astype(jnp.int32)
    pieces = lax.map(run_block, (queries.reshape(block_count, block_rows, HEADS * HEAD_DIM), segment.reshape(block_count, block_rows), starts))
    return pieces.reshape(PACK, HEADS * HEAD_DIM)

def layer_forward(inputs, attn_gain, w_query, w_key, w_value, w_out, mlp_gain, w_gate, w_up, w_down, segment, position):
    normed = low(rms_norm(inputs, attn_gain))
    queries = low(rotate(low_back(matmul(normed, w_query)), position, HEADS))
    key_rows = low(rotate(low_back(matmul(normed, w_key)), position, KV_HEADS))
    value_rows = low(low_back(matmul(normed, w_value)))
    attended = low(low_back(attend(queries, key_rows, value_rows, segment)))
    hidden = inputs + low_back(matmul(attended, w_out))
    normed_two = low(rms_norm(hidden, mlp_gain))
    gate_raw = low_back(matmul(normed_two, w_gate))
    up_raw = low_back(matmul(normed_two, w_up))
    mixed = low(jax.nn.silu(gate_raw) * up_raw)
    return hidden + matmul(mixed, w_down)

def reference(tokens, doc_lengths, attn_gain, w_query, w_key, w_value, w_out, mlp_gain, w_gate, w_up, w_down, cotangent):
    weights = tuple((weight_arg.astype(jnp.float32) for weight_arg in (attn_gain, w_query, w_key, w_value, w_out, mlp_gain, w_gate, w_up, w_down)))

    def one_pack(running, pack_item):
        pack_tokens, pack_lengths, pack_cotangent = pack_item
        segment, position = doc_layout(pack_lengths, PACK)

        def forward(inputs, *params):
            return layer_forward(inputs, *params, segment, position)
        result, pullback = jax.vjp(forward, pack_tokens.astype(jnp.float32), *weights)
        gradients = pullback(pack_cotangent.astype(jnp.float32))
        running = tuple((total + grad_part for total, grad_part in zip(running, gradients[1:])))
        return (running, (result.astype(jnp.bfloat16), gradients[0]))
    start_sums = tuple((jnp.zeros(weight_arg.shape, jnp.float32) for weight_arg in weights))
    totals, outputs = lax.scan(one_pack, start_sums, (tokens, doc_lengths, cotangent))
    return (outputs[0], outputs[1], totals[0], totals[1], totals[2], totals[3], totals[4], totals[5], totals[6], totals[7], totals[8])
```

```python
import functools
import math

import jax
import jax.numpy as jnp
from jax import lax
from jax.experimental import pallas as pl
from jax.experimental.pallas import tpu as pltpu
from jax.sharding import PartitionSpec as P

HEADS = 12
HEAD_DIM = 64
EPSILON = 1e-05
ROPE_BASE = 10000.0
MASKED_SCORE = -1e30
MESH = pl.DeviceIdType.MESH
BF16 = jnp.bfloat16
F32 = jnp.float32

WIDE = ("y", "xl", "xh", "z", "c")
TALL = ("xl", "xh", "z", "c", "y")
SIZES = {"y": 4, "xl": 2, "xh": 2, "z": 4, "c": 2}
ORDERS = (("y", "z", "x"), ("z", "x", "y"), ("x", "y", "z"))
ITEMS = (
    (0, 0, ORDERS[0], WIDE, 128),
    (0, 1, ORDERS[1], WIDE, 128),
    (0, 2, ORDERS[2], WIDE, 128),
    (1, None, ORDERS[0], WIDE, 384),
    (2, None, ORDERS[1], WIDE, 384),
    (3, None, ORDERS[2], TALL, 384),
)
W_SHAPES = (
    (3,) + tuple(SIZES[n] for n in WIDE) + (48, 128),
    tuple(SIZES[n] for n in WIDE) + (48, 384),
    tuple(SIZES[n] for n in WIDE) + (48, 384),
    tuple(SIZES[n] for n in TALL) + (48, 384),
)


def place():
    f = lax.axis_index("fsdp")
    s = lax.axis_index("seq")
    return {"x": (f // 8) * 2 + s % 2, "y": s // 2, "z": (f // 2) % 4, "c": f % 2}


def device(at):
    return ((at["x"] // 2) * 8 + at["z"] * 2 + at["c"], at["y"] * 2 + at["x"] % 2)


def shifted(at, axis, k):
    return {**at, axis: (at[axis] + k) % SIZES.get(axis, 4)}


def select(names, fixed):
    index = []
    for n in names:
        if n in ("xl", "xh"):
            v = fixed.get("x")
            index.append(pl.ds(0, 2) if v is None else (v % 2 if n == "xl" else v // 2))
        else:
            v = fixed.get(n)
            index.append(pl.ds(0, SIZES[n]) if v is None else v)
    return tuple(index)


def expand(axes):
    return [n for a in axes for n in (("xl", "xh") if a == "x" else (a,))]


def kept(names, axes):
    some = expand(axes)
    return tuple(n for n in names if n in some)


def remote(src, dst, send, recv, to):
    return pltpu.make_async_remote_copy(
        src_ref=src, dst_ref=dst, send_sem=send, recv_sem=recv, device_id=to, device_id_type=MESH
    )


def greet(at):
    f = lax.axis_index("fsdp")
    s = lax.axis_index("seq")
    bar = pltpu.get_barrier_semaphore()
    peers = [(f, (s + k) % 8) for k in range(1, 8)]
    peers += [device(shifted(at, "z", k)) for k in (1, 2, 3)]
    peers += [device(shifted(at, "c", 1))]
    peers += [device({**at, "x": (at["x"] + 2) % 4})]
    peers += [device({**at, "x": (at["x"] // 2 * 2 + 2) % 4 + (1 - at["x"] % 2)})]
    for p in peers:
        pl.semaphore_signal(bar, inc=1, device_id=p, device_id_type=MESH)
    pl.semaphore_wait(bar, len(peers))


def pick_rows(rows, slots, per, offset):
    i = lax.broadcasted_iota(jnp.int32, (rows, slots), 0)
    j = lax.broadcasted_iota(jnp.int32, (rows, slots), 1)
    return (j == (i // per) * 32 + offset + i % per).astype(BF16)


def gather_kernel(
    s0, d0, vh, wa, wg, wu, wd, xa, r0, rd0, sem0s, sem0r, semds, semdr, semxs, semxr, sems, semr, semcs, semcr
):
    at = place()
    f = lax.axis_index("fsdp")
    s = lax.axis_index("seq")
    arrays = (wa, wg, wu, wd)
    greet(at)

    def first(k):
        to, frm = (s + k) % 8, (s - k + 8) % 8
        out = remote(s0.at[to], r0.at[s], sem0s.at[k - 1], sem0r.at[k - 1], (f, to))
        inn = remote(s0.at[to], r0.at[frm], sem0s.at[k - 1], sem0r.at[k - 1], (f, to))
        return out, inn

    firsts = [first(k) for k in range(1, 8)]
    xl = at["x"] % 2
    beside = (f, at["y"] * 2 + 1 - xl)
    down_out = remote(d0.at[1 - xl], rd0.at[xl], semds, semdr, beside)
    down_in = remote(d0.at[1 - xl], rd0.at[1 - xl], semds, semdr, beside)
    for out, _ in firsts:
        out.start()
    down_out.start()

    def token_copy(to):
        return remote(vh, xa.at[s], semxs.at[to], semxr.at[s], (f, to))

    def token_in(frm):
        return remote(vh, xa.at[frm], semxs.at[frm], semxr.at[frm], (f, frm))

    for to in range(1, 8):
        pl.when(to > s)(lambda to=to: token_copy(to).start())

    r0[s] = s0[s]
    rd0[xl] = d0[xl]
    xa[s] = vh[...]
    for _, inn in firsts:
        inn.wait_recv()
    down_in.wait_recv()

    def block(item, fixed):
        array, third, _, names, _ = item
        ref = arrays[array]
        lead = () if third is None else (third,)
        return ref.at[lead + select(names, fixed)]

    def put(item, value):
        array, third, _, names, _ = item
        lead = () if third is None else (third,)
        arrays[array][lead + select(names, at)] = value

    flat = r0[...].reshape(256, 384)
    attn = jnp.dot(pick_rows(48, 256, 6, 12), flat, preferred_element_type=F32).astype(BF16)
    for t in range(3):
        put(ITEMS[t], attn[:, t * 128 : (t + 1) * 128])

    def ring(i, phase, k):
        item = ITEMS[i]
        order = item[2]
        axis = order[phase]
        gone = order[:phase]
        fixed = {n: at[n] for n in ("x", "y", "z", "c") if n not in gone}
        theirs = {**fixed, axis: (at[axis] - k + 4) % 4}
        to = device(shifted(at, axis, k))
        out = remote(block(item, fixed), block(item, fixed), sems.at[i, phase, k - 1], semr.at[i, phase, k - 1], to)
        inn = remote(block(item, theirs), block(item, theirs), sems.at[i, phase, k - 1], semr.at[i, phase, k - 1], to)
        return out, inn

    sibling = device(shifted(at, "c", 1))

    def across(i, k):
        item = ITEMS[i]
        axis = item[2][2]
        mine = {axis: (at[axis] - k + 4) % 4, "c": at["c"]}
        theirs = {axis: (at[axis] - k + 4) % 4, "c": 1 - at["c"]}
        out = remote(block(item, mine), block(item, mine), semcs.at[i, k], semcr.at[i, k], sibling)
        inn = remote(block(item, theirs), block(item, theirs), semcs.at[i, k], semcr.at[i, k], sibling)
        return out, inn

    def start(items, phase):
        for k in (1, 3, 2):
            for i in items:
                ring(i, phase, k)[0].start()

    def arrive(items, phase):
        for k in (1, 3, 2):
            for i in items:
                ring(i, phase, k)[1].wait_recv()

    small, large = (0, 1, 2), (3, 4, 5)
    start(small, 0)
    put(ITEMS[3], jnp.dot(pick_rows(48, 256, 6, 0), flat, preferred_element_type=F32).astype(BF16))
    put(ITEMS[4], jnp.dot(pick_rows(48, 256, 6, 6), flat, preferred_element_type=F32).astype(BF16))
    down = jnp.dot(pick_rows(48, 64, 24, 0), rd0[...].reshape(64, 384), preferred_element_type=F32)
    put(ITEMS[5], down.astype(BF16))
    start(large, 0)
    arrive(small, 0)
    start(small, 1)
    arrive(large, 0)
    start(large, 1)
    arrive(small, 1)
    start(small, 2)
    for i in small:
        across(i, 0)[0].start()
    arrive(large, 1)
    start(large, 2)
    for i in large:
        across(i, 0)[0].start()
    for items in (small, large):
        for k in (1, 3, 2):
            for i in items:
                ring(i, 2, k)[1].wait_recv()
                across(i, k)[0].start()
    for frm in range(0, 7):
        pl.when(frm < s)(lambda frm=frm: token_in(frm).wait_recv())
    for i in range(6):
        for k in range(4):
            across(i, k)[1].wait_recv()
    for out, _ in firsts:
        out.wait_send()
    down_out.wait_send()
    for to in range(1, 8):
        pl.when(to > s)(lambda to=to: token_copy(to).wait_send())
    for i in range(6):
        for phase in range(3):
            for k in (1, 2, 3):
                ring(i, phase, k)[0].wait_send()
        for k in range(4):
            across(i, k)[0].wait_send()


VMEM_SPEC = pl.BlockSpec(memory_space=pltpu.VMEM)
DMA = pltpu.SemaphoreType.DMA


def gather(s0, d0, vh):
    return pl.pallas_call(
        gather_kernel,
        out_shape=[jax.ShapeDtypeStruct(w, BF16) for w in W_SHAPES] + [jax.ShapeDtypeStruct((8, 128, 768), BF16)],
        in_specs=[VMEM_SPEC] * 3,
        out_specs=[VMEM_SPEC] * 5,
        scratch_shapes=[
            pltpu.VMEM((8, 32, 384), BF16),
            pltpu.VMEM((2, 32, 384), BF16),
            DMA((7,)), DMA((7,)), DMA, DMA, DMA((8,)), DMA((8,)),
            DMA((6, 3, 3)), DMA((6, 3, 3)), DMA((6, 4)), DMA((6, 4)),
        ],
        compiler_params=pltpu.CompilerParams(
            collective_id=0, has_side_effects=True, vmem_limit_bytes=60 * 2**20
        ),
        name="gather_weights",
    )(s0, d0, vh)


def scatter_kernel(
    ga, gg, gu, gd, dn, fo, fd, dno,
    ra, rg, ru, rd,
    t3a0, t3a1, t3a2, t3g, t3u, t3d,
    t2a0, t2a1, t2a2, t2g, t2u, t2d,
    t1a, t1m, s3s, f0, fd0, rdn,
    semcs, semcr, sems, semr, sem0s, sem0r, semds, semdr, semxs, semxr,
):
    at = place()
    f = lax.axis_index("fsdp")
    s = lax.axis_index("seq")
    grads = (ga, gg, gu, gd)
    sums = (ra, rg, ru, rd)
    t3 = (t3a0, t3a1, t3a2, t3g, t3u, t3d)
    t2 = (t2a0, t2a1, t2a2, t2g, t2u, t2d)
    greet(at)
    sibling = device(shifted(at, "c", 1))

    def token_out(to):
        return remote(dn.at[to], rdn.at[s], semxs.at[to], semxr.at[s], (f, to))

    def token_in(frm):
        return remote(dn.at[frm], rdn.at[frm], semxs.at[frm], semxr.at[frm], (f, frm))

    def grad_ref(i):
        array, third = ITEMS[i][:2]
        return grads[array] if third is None else grads[array].at[third]

    def sum_ref(i):
        array, third = ITEMS[i][:2]
        return sums[array] if third is None else sums[array].at[third]

    def names_of(i, left):
        return kept(ITEMS[i][3], ITEMS[i][2][:left])

    def across(i):
        return remote(
            grad_ref(i).at[select(ITEMS[i][3], {"c": 1 - at["c"]})], sum_ref(i), semcs.at[i], semcr.at[i], sibling
        )

    large, small = (5, 3, 4), (0, 1, 2)
    for i in large + small:
        across(i).start()
    for to in range(0, 7):
        pl.when(to < s)(lambda to=to: token_out(to).start())

    def digits(names, n):
        out = {}
        for name in reversed(names):
            out[name] = n % SIZES[name]
            n = n // SIZES[name]
        return out

    def full_index(names, fixed, free, n):
        got = digits(free, n)
        index = []
        for name in names:
            if name in free:
                index.append(got[name])
            elif name in ("xl", "xh"):
                index.append(fixed["x"] % 2 if name == "xl" else fixed["x"] // 2)
            else:
                index.append(fixed[name])
        return tuple(index)

    def count(names):
        return math.prod(SIZES[n] for n in names)

    def add_core(i):
        names = ITEMS[i][3]
        free = tuple(n for n in names if n != "c")
        g, r = grad_ref(i), sum_ref(i)

        def body(n, carry):
            gi = full_index(names, {"c": at["c"]}, free, n)
            ri = full_index(free, {}, free, n)
            r[ri] = (r[ri].astype(F32) + g[gi].astype(F32)).astype(BF16)
            return carry

        lax.fori_loop(0, count(free), body, 0)

    def hop(i, left, k):
        axis = ITEMS[i][2][left - 1]
        names = names_of(i, left)
        if left == 3:
            src = sum_ref(i).at[select(names, {axis: (at[axis] + k) % 4})]
            dst = t3[i].at[k - 1]
        else:
            base = stage_ref(i, left)
            src = base.at[select(names, {axis: (at[axis] + k) % 4})]
            dst = t2[i].at[k - 1] if left == 2 else (t1a.at[i, k - 1] if i < 3 else t1m.at[i - 3, k - 1])
        return remote(src, dst, sems.at[i, left - 1, k - 1], semr.at[i, left - 1, k - 1], device(shifted(at, axis, k)))

    def stage_ref(i, left):
        return t3[i].at[0] if left == 2 else t2[i].at[0]

    def add_ring(i, left):
        axis = ITEMS[i][2][left - 1]
        names = names_of(i, left)
        free = names_of(i, left - 1)
        own = sum_ref(i) if left == 3 else stage_ref(i, left)
        inn = t3[i] if left == 3 else t2[i]
        fixed = {axis: at[axis]}

        def body(n, carry):
            oi = full_index(names, fixed, free, n)
            fi = full_index(free, {}, free, n)
            total = own[oi].astype(F32)
            for k in range(3):
                total = total + inn[(k,) + fi].astype(F32)
            inn[(0,) + fi] = total.astype(BF16)
            return carry

        lax.fori_loop(0, count(free), body, 0)

    def start(items, left):
        for k in (1, 3, 2):
            for i in items:
                hop(i, left, k).start()

    def arrive(i, left):
        for k in (1, 3, 2):
            hop(i, left, k).wait_recv()

    for i in large + small:
        across(i).wait_recv()
        add_core(i)
        for k in (1, 3, 2):
            hop(i, 3, k).start()
    for left in (3, 2):
        for i in large + small:
            arrive(i, left)
            add_ring(i, left)
            for k in (1, 3, 2):
                hop(i, left - 1, k).start()

    def last(i):
        arrive(i, 1)
        axis = ITEMS[i][2][0]
        names = names_of(i, 1)
        own = stage_ref(i, 1)
        total = own[select(names, {axis: at[axis]})].astype(F32)
        inn = t1a if i < 3 else t1m
        for k in range(3):
            total = total + inn[i if i < 3 else i - 3, k].astype(F32)
        return total.astype(BF16)

    down = last(5)
    gate = last(3)
    up = last(4)
    attn = jnp.concatenate([last(0), last(1), last(2)], axis=1)

    def unpick(rows, slots, per, offset):
        j = lax.broadcasted_iota(jnp.int32, (slots, rows), 0)
        i = lax.broadcasted_iota(jnp.int32, (slots, rows), 1)
        return (j == (i // per) * 32 + offset + i % per).astype(BF16)

    mixed = jnp.dot(unpick(48, 256, 6, 0), gate, preferred_element_type=F32)
    mixed += jnp.dot(unpick(48, 256, 6, 6), up, preferred_element_type=F32)
    mixed += jnp.dot(unpick(48, 256, 6, 12), attn, preferred_element_type=F32)
    f0[...] = mixed.astype(BF16).reshape(8, 32, 384)
    fd0[...] = jnp.dot(unpick(48, 64, 24, 0), down, preferred_element_type=F32).astype(BF16).reshape(2, 32, 384)

    xl = at["x"] % 2
    beside = (f, at["y"] * 2 + 1 - xl)

    def final(k):
        to, frm = (s + k) % 8, (s - k + 8) % 8
        out = remote(f0.at[to], fo.at[s], sem0s.at[k - 1], sem0r.at[k - 1], (f, to))
        inn = remote(f0.at[to], fo.at[frm], sem0s.at[k - 1], sem0r.at[k - 1], (f, to))
        return out, inn

    down_out = remote(fd0.at[1 - xl], fd.at[xl], semds, semdr, beside)
    down_in = remote(fd0.at[1 - xl], fd.at[1 - xl], semds, semdr, beside)
    for k in range(1, 8):
        final(k)[0].start()
    down_out.start()
    fo[s] = f0[s]
    fd[xl] = fd0[xl]

    dno[...] = dn[s].astype(F32)
    for frm in range(1, 8):

        def add(frm=frm):
            token_in(frm).wait_recv()
            dno[...] += rdn[frm].astype(F32)

        pl.when(frm > s)(add)
    for k in range(1, 8):
        final(k)[1].wait_recv()
    down_in.wait_recv()
    for k in range(1, 8):
        final(k)[0].wait_send()
    down_out.wait_send()
    for to in range(0, 7):
        pl.when(to < s)(lambda to=to: token_out(to).wait_send())
    for i in range(6):
        across(i).wait_send()
        for left in (3, 2, 1):
            for k in (1, 2, 3):
                hop(i, left, k).wait_send()


def dims(i, left):
    return tuple(SIZES[n] for n in kept(ITEMS[i][3], ITEMS[i][2][:left]))


def scatter(ga, gg, gu, gd, dn):
    no_core = lambda shape, names, lead: shape[: names.index("c") + lead] + shape[names.index("c") + lead + 1 :]
    sums = [
        no_core(W_SHAPES[0], WIDE, 1),
        no_core(W_SHAPES[1], WIDE, 0),
        no_core(W_SHAPES[2], WIDE, 0),
        no_core(W_SHAPES[3], TALL, 0),
    ]
    scratch = [pltpu.VMEM(x, BF16) for x in sums]
    for left in (2, 1):
        for i in range(6):
            scratch.append(pltpu.VMEM((3,) + dims(i, left) + (48, ITEMS[i][4]), BF16))
    scratch += [
        pltpu.VMEM((3, 3, 48, 128), BF16),
        pltpu.VMEM((3, 3, 48, 384), BF16),
        pltpu.VMEM((8, 128), F32),
        pltpu.VMEM((8, 32, 384), BF16),
        pltpu.VMEM((2, 32, 384), BF16),
        pltpu.VMEM((8, 128, 768), BF16),
    ]
    return pl.pallas_call(
        scatter_kernel,
        out_shape=[
            jax.ShapeDtypeStruct((8, 32, 384), BF16),
            jax.ShapeDtypeStruct((2, 32, 384), BF16),
            jax.ShapeDtypeStruct((128, 768), F32),
        ],
        in_specs=[VMEM_SPEC] * 5,
        out_specs=[VMEM_SPEC] * 3,
        scratch_shapes=scratch
        + [
            DMA((6,)), DMA((6,)), DMA((6, 3, 3)), DMA((6, 3, 3)),
            DMA((7,)), DMA((7,)), DMA, DMA, DMA((8,)), DMA((8,)),
        ],
        compiler_params=pltpu.CompilerParams(
            collective_id=1, has_side_effects=True, vmem_limit_bytes=60 * 2**20
        ),
        name="scatter_grads",
    )(ga, gg, gu, gd, dn)


def rotate(values, position, sign):
    half_dim = HEAD_DIM // 2
    freqs = ROPE_BASE ** (-(2.0 * jnp.arange(half_dim, dtype=F32)) / HEAD_DIM)
    angles = position.astype(F32)[:, None] * freqs[None, :]
    cosine = jnp.cos(angles)[:, None, :]
    sine = sign * jnp.sin(angles)[:, None, :]
    shaped = values.reshape(values.shape[0], HEADS, HEAD_DIM)
    a = shaped[..., :half_dim]
    b = shaped[..., half_dim:]
    turned = jnp.concatenate([a * cosine - b * sine, b * cosine + a * sine], axis=-1)
    return turned.reshape(values.shape[0], HEADS * HEAD_DIM)


def doc_layout(lengths, pack_len):
    ends = jnp.cumsum(lengths)
    where_pos = jnp.arange(pack_len, dtype=jnp.int32)
    passed = where_pos[:, None] >= ends[None, :]
    segment = jnp.sum(passed.astype(jnp.int32), axis=1)
    start_pos = jnp.sum(jnp.where(passed, lengths[None, :], 0), axis=1)
    return (segment, where_pos - start_pos)


def product(form, left, right):
    return jnp.einsum(form, left, right, preferred_element_type=F32)


def norm_factor(values):
    return lax.rsqrt(jnp.mean(values * values, axis=-1, keepdims=True) + EPSILON)


def norm_back(values, factor, e):
    return factor * e - values * factor**3 * jnp.mean(e * values, axis=-1, keepdims=True)


def pieces(w):
    return w.reshape(6, 8, 384).transpose(1, 0, 2)


def per_device(tokens, doc_lengths, attn_gain, w_query, w_key, w_value, w_out, mlp_gain, w_gate, w_up, w_down, cotangent):
    tok_rows = tokens.shape[1]
    s = lax.axis_index("seq")
    pack_len = tok_rows * 8
    scale_value = 1.0 / math.sqrt(HEAD_DIM)
    gain_one = attn_gain.astype(F32)[:, None]
    gain_two = mlp_gain.astype(F32)[:, None]
    fold = lambda w, g: (w.astype(F32) * g).astype(BF16)

    inputs = tokens[0].astype(F32)
    factor_one = norm_factor(inputs)
    vhat = (inputs * factor_one).astype(BF16)

    attn = jnp.concatenate([fold(w_query, gain_one), fold(w_key, gain_one), fold(w_value, gain_one), w_out], axis=1)
    s0 = jnp.concatenate(
        [pieces(fold(w_gate, gain_two)), pieces(fold(w_up, gain_two)), pieces(attn), jnp.zeros((8, 14, 384), BF16)], axis=1
    )
    d0 = jnp.pad(w_down.reshape(24, 2, 384).transpose(1, 0, 2), ((0, 0), (0, 8), (0, 0)))
    wa, wg, wu, wd, xa = gather(s0, d0, vhat)
    full = wa.reshape(3, 8, 768, 128).transpose(2, 1, 0, 3).reshape(768, 3072)
    full_query, full_key, full_value, full_out = (full[:, i * 768 : (i + 1) * 768] for i in range(4))
    full_gate = wg.reshape(8, 768, 384)
    full_up = wu.reshape(8, 768, 384)
    full_down = wd.reshape(2, 3072, 384)
    before = jnp.arange(8) <= s
    vhat_all = jnp.where(before[:, None, None], xa, 0).reshape(pack_len, 768)

    first_row = s * tok_rows
    segment_all, position_all = doc_layout(doc_lengths[0], pack_len)
    segment_mine = lax.dynamic_slice_in_dim(segment_all, first_row, tok_rows)
    position_mine = lax.dynamic_slice_in_dim(position_all, first_row, tok_rows)
    query_index = first_row + jnp.arange(tok_rows, dtype=jnp.int32)

    queries = rotate(product("td,de->te", vhat, full_query), position_mine, 1.0).astype(BF16)
    key_rows = rotate(product("td,de->te", vhat_all, full_key), position_all, 1.0).astype(BF16)
    value_rows = product("td,de->te", vhat_all, full_value).astype(BF16)
    q = queries.reshape(tok_rows, HEADS, HEAD_DIM)
    k = key_rows.reshape(pack_len, HEADS, HEAD_DIM)
    v = value_rows.reshape(pack_len, HEADS, HEAD_DIM)
    scores = product("qhd,khd->hqk", q, k) * scale_value
    key_index = jnp.arange(pack_len, dtype=jnp.int32)
    allowed = (segment_mine[:, None] == segment_all[None, :]) & (key_index[None, :] <= query_index[:, None])
    probs = jax.nn.softmax(jnp.where(allowed[None], scores, MASKED_SCORE), axis=-1)
    probs_low = probs.astype(BF16)
    attended = product("hqk,khd->qhd", probs_low, v).reshape(tok_rows, 768).astype(BF16)
    hidden = inputs + product("td,de->te", attended, full_out)

    factor_two = norm_factor(hidden)
    vhat_two = (hidden * factor_two).astype(BF16)
    gate_raw = product("td,cdf->tcf", vhat_two, full_gate)
    up_raw = product("td,cdf->tcf", vhat_two, full_up)
    sig = 1.0 / (1.0 + jnp.exp(-gate_raw))
    silu = gate_raw * sig
    mixed = (silu * up_raw).astype(BF16).reshape(tok_rows, 3072)
    mlp_out = product("tf,cfd->tcd", mixed, full_down).reshape(tok_rows, 768)
    layer_out = (hidden + mlp_out).astype(BF16)

    upstream = cotangent[0]
    up_c = upstream.reshape(tok_rows, 2, 384)
    d_mixed = product("tcd,cfd->tf", up_c, full_down).reshape(tok_rows, 8, 384)
    d_gate = (d_mixed * up_raw * sig * (1.0 + gate_raw * (1.0 - sig))).astype(BF16)
    d_up = (d_mixed * silu).astype(BF16)
    e_two = product("tcf,cdf->td", d_gate, full_gate) + product("tcf,cdf->td", d_up, full_up)
    d_hidden = upstream.astype(F32) + norm_back(hidden, factor_two, e_two)
    grad_down = product("tf,tcd->cfd", mixed, up_c).astype(BF16).reshape(W_SHAPES[3])
    grad_gate = product("td,tcf->cdf", vhat_two, d_gate).astype(BF16).reshape(W_SHAPES[1])
    grad_up = product("td,tcf->cdf", vhat_two, d_up).astype(BF16).reshape(W_SHAPES[2])

    d_hidden_low = d_hidden.astype(BF16)
    d_attended = product("te,de->td", d_hidden_low, full_out).astype(BF16)
    da = d_attended.reshape(tok_rows, HEADS, HEAD_DIM)
    d_probs = product("qhd,khd->hqk", da, v)
    d_scores = (probs * (d_probs - jnp.sum(probs * d_probs, axis=-1, keepdims=True))).astype(BF16)
    d_queries = (product("hqk,khd->qhd", d_scores, k) * scale_value).reshape(tok_rows, 768)
    d_keys = (product("hqk,qhd->khd", d_scores, q) * scale_value).reshape(pack_len, 768)
    d_values = product("hqk,qhd->khd", probs_low, da).reshape(pack_len, 768)
    d_query_raw = rotate(d_queries, position_mine, -1.0).astype(BF16)
    d_key_raw = rotate(d_keys, position_all, -1.0).astype(BF16)
    d_value_raw = d_values.astype(BF16)
    e_part = product("te,de->td", d_key_raw, full_key) + product("te,de->td", d_value_raw, full_value)
    e_mine = product("te,de->td", d_query_raw, full_query)
    g_attn = jnp.concatenate(
        [
            product("td,te->de", vhat, d_query_raw),
            product("td,te->de", vhat_all, d_key_raw),
            product("td,te->de", vhat_all, d_value_raw),
            product("td,te->de", attended, d_hidden_low),
        ],
        axis=1,
    ).astype(BF16)
    g_attn = g_attn.reshape(768, 8, 3, 128).transpose(2, 1, 0, 3).reshape(W_SHAPES[0])
    fo, fd, dno = scatter(g_attn, grad_gate, grad_up, grad_down, e_part.astype(BF16).reshape(8, tok_rows, 768))
    e_one = dno + e_mine
    input_grad = d_hidden + norm_back(inputs, factor_one, e_one)

    whole = lambda i: fo[:, i * 6 : i * 6 + 6].astype(F32).transpose(1, 0, 2).reshape(6, 3072)
    h_gate, h_up, h_attn = whole(0), whole(1), whole(2)
    own = lambda h, w: jnp.sum(h * w.astype(F32), axis=1)
    hq, hk, hv, ho = (h_attn[:, i * 768 : (i + 1) * 768] for i in range(4))
    grad_gain_one = own(hq, w_query) + own(hk, w_key) + own(hv, w_value)
    grad_gain_two = own(h_gate, w_gate) + own(h_up, w_up)
    g_down = fd[:, :24].astype(F32).transpose(1, 0, 2).reshape(24, 768)
    return (
        layer_out[None],
        input_grad[None],
        grad_gain_one,
        hq * gain_one,
        hk * gain_one,
        hv * gain_one,
        ho,
        grad_gain_two,
        h_gate * gain_two,
        h_up * gain_two,
        g_down,
    )


def solution(mesh):
    rows = P(("fsdp", "seq"), None)
    gain = P(("fsdp", "seq"))
    toks = P("fsdp", "seq", None)
    return jax.shard_map(
        per_device,
        mesh=mesh,
        in_specs=(toks, P("fsdp", None), gain, rows, rows, rows, rows, gain, rows, rows, rows, toks),
        out_specs=(toks, toks, gain, rows, rows, rows, rows, gain, rows, rows, rows),
        check_vma=False,
    )
```

```python
import math

import jax
import jax.numpy as jnp
from jax import lax
from jax.experimental import pallas as pl
from jax.experimental.pallas import tpu as pltpu
from jax.sharding import PartitionSpec as P

HEADS = 12
HEAD_DIM = 64
EPSILON = 1e-05
ROPE_BASE = 10000.0
MASKED_SCORE = -1e30
VMEM_LIMIT = 62 * 2**20
MESH = pl.DeviceIdType.MESH
BF16 = jnp.bfloat16
F32 = jnp.float32

WIDE = ("y", "xl", "xh", "z", "c")
TALL = ("xl", "xh", "z", "c", "y")
SIZES = {"y": 4, "xl": 2, "xh": 2, "z": 4, "c": 2}
ORDERS = (("y", "z", "x"), ("z", "x", "y"), ("x", "y", "z"))
ITEMS = (
    (0, 0, ORDERS[0], WIDE, 128),
    (0, 1, ORDERS[1], WIDE, 128),
    (0, 2, ORDERS[2], WIDE, 128),
    (1, None, ORDERS[0], WIDE, 384),
    (2, None, ORDERS[1], WIDE, 384),
    (3, None, ORDERS[2], TALL, 384),
)
W_SHAPES = (
    (3,) + tuple(SIZES[n] for n in WIDE) + (48, 128),
    tuple(SIZES[n] for n in WIDE) + (48, 384),
    tuple(SIZES[n] for n in WIDE) + (48, 384),
    tuple(SIZES[n] for n in TALL) + (48, 384),
)


def place():
    f = lax.axis_index("fsdp")
    s = lax.axis_index("seq")
    return {"x": (f // 8) * 2 + s % 2, "y": s // 2, "z": (f // 2) % 4, "c": f % 2}


def device(at):
    return ((at["x"] // 2) * 8 + at["z"] * 2 + at["c"], at["y"] * 2 + at["x"] % 2)


def shifted(at, axis, k):
    return {**at, axis: (at[axis] + k) % SIZES.get(axis, 4)}


def select(names, fixed):
    index = []
    for n in names:
        if n in ("xl", "xh"):
            v = fixed.get("x")
            index.append(pl.ds(0, 2) if v is None else (v % 2 if n == "xl" else v // 2))
        else:
            v = fixed.get(n)
            index.append(pl.ds(0, SIZES[n]) if v is None else v)
    return tuple(index)


def expand(axes):
    return [n for a in axes for n in (("xl", "xh") if a == "x" else (a,))]


def kept(names, axes):
    some = expand(axes)
    return tuple(n for n in names if n in some)


def remote(src, dst, send, recv, to):
    return pltpu.make_async_remote_copy(
        src_ref=src, dst_ref=dst, send_sem=send, recv_sem=recv, device_id=to, device_id_type=MESH
    )


def greet(at):
    f = lax.axis_index("fsdp")
    s = lax.axis_index("seq")
    bar = pltpu.get_barrier_semaphore()
    peers = [(f, (s + k) % 8) for k in range(1, 8)]
    peers += [device(shifted(at, "z", k)) for k in (1, 2, 3)]
    peers += [device(shifted(at, "c", 1))]
    peers += [device({**at, "x": (at["x"] + 2) % 4})]
    peers += [device({**at, "x": (at["x"] // 2 * 2 + 2) % 4 + (1 - at["x"] % 2)})]
    for p in peers:
        pl.semaphore_signal(bar, inc=1, device_id=p, device_id_type=MESH)
    pl.semaphore_wait(bar, len(peers))


def one_hot(rows, slots, per, offset, flip=False):
    shape = (slots, rows) if flip else (rows, slots)
    i = lax.broadcasted_iota(jnp.int32, shape, 1 if flip else 0)
    j = lax.broadcasted_iota(jnp.int32, shape, 0 if flip else 1)
    return (j == (i // per) * 32 + offset + i % per).astype(BF16)


def nn(a, b):
    return jnp.dot(a, b, preferred_element_type=F32)


def nt(a, b):
    return lax.dot_general(a, b, (((1,), (1,)), ((), ())), preferred_element_type=F32)


def tn(a, b):
    return lax.dot_general(a, b, (((0,), (0,)), ((), ())), preferred_element_type=F32)


def norm_factor(values):
    return lax.rsqrt(jnp.mean(values * values, axis=-1, keepdims=True) + EPSILON)


def norm_back(values, factor, e):
    return factor * e - values * (factor * factor * factor * jnp.mean(e * values, axis=-1, keepdims=True))


def swap_halves(v):
    lane = lax.broadcasted_iota(jnp.int32, v.shape, 1)
    return jnp.where(lane % 64 < 32, pltpu.roll(v, 96, 1), pltpu.roll(v, 32, 1))


def digits(names, n):
    out = {}
    for name in reversed(names):
        out[name] = n % SIZES[name]
        n = n // SIZES[name]
    return out


def full_index(names, fixed, free, n):
    got = digits(free, n)
    index = []
    for name in names:
        if name in free:
            index.append(got[name])
        elif name in ("xl", "xh"):
            index.append(fixed["x"] % 2 if name == "xl" else fixed["x"] // 2)
        else:
            index.append(fixed[name])
    return tuple(index)


def count(names):
    return math.prod(SIZES[n] for n in names)


def layer_kernel(
    lens, gains, tok, cot, w_query, w_key, w_value, w_out, w_gate, w_up, w_down,
    out_o, in_o, ga1_o, gq_o, gk_o, gv_o, go_o, ga2_o, gg_o, gu_o, gd_o,
    wa, wg, wu, wd, ga, gg, gu, gd, xa, xat, r0, rd0, s0, d0,
    ks, vs, qs, ps, att, hid, oacc, eacc, dhid, dqs, cosine, sine, bias, rdn, fo, fd0,
    t2a0, t2a1, t2a2, t2g, t2u, t2d, t1a, t1m,
    sem0s, sem0r, semds, semdr, semxs, semxr, sems, semr, semcs, semcr,
    bem0s, bem0r, bemds, bemdr, bemxs, bemxr, bems, bemr, bemcs, bemcr, free_large, free_small,
):
    at = place()
    f = lax.axis_index("fsdp")
    s = lax.axis_index("seq")
    weights = (wa, wg, wu, wd)
    grads = (ga, gg, gu, gd)
    t2 = (t2a0, t2a1, t2a2, t2g, t2u, t2d)
    sibling = device(shifted(at, "c", 1))
    xl = at["x"] % 2
    beside = (f, at["y"] * 2 + 1 - xl)
    small, large = (0, 1, 2), (5, 3, 4)

    row = lax.broadcasted_iota(jnp.int32, (6, 1), 0)

    def gain_column(which):
        col = jnp.zeros((6, 1), F32)
        for r in range(6):
            col = jnp.where(row == r, gains[which, r], col)
        return col

    gain_one, gain_two = gain_column(0), gain_column(1)
    inputs = tok[...].astype(F32)
    factor_one = norm_factor(inputs)
    xa[s] = (inputs * factor_one).astype(BF16)
    s0[...] = jnp.zeros_like(s0)
    d0[...] = jnp.zeros_like(d0)
    for b in range(8):
        lanes = pl.ds(b * 384, 384)
        half = pl.ds((b % 2) * 384, 384)
        s0[b, 0:6] = w_gate[:, lanes].astype(F32) * gain_two
        s0[b, 8:14] = w_up[:, lanes].astype(F32) * gain_two
        if b < 6:
            s0[b, 16:22] = (w_query, w_key, w_value)[b // 2][:, half].astype(F32) * gain_one
        else:
            s0[b, 16:22] = w_out[:, half].astype(F32)
    for b in range(2):
        d0[b, 0:24] = w_down[:, b * 384 : (b + 1) * 384].astype(F32)
    s0b, d0b = fo, fd0
    s0b[...] = s0[...].astype(BF16)
    d0b[...] = d0[...].astype(BF16)

    greet(at)

    def first(k):
        to, frm = (s + k) % 8, (s - k + 8) % 8
        out = remote(s0b.at[to], r0.at[s], sem0s.at[k - 1], sem0r.at[k - 1], (f, to))
        inn = remote(s0b.at[to], r0.at[frm], sem0s.at[k - 1], sem0r.at[k - 1], (f, to))
        return out, inn

    def down_copy(slot):
        return remote(d0b.at[1 - xl], rd0.at[slot], semds, semdr, beside)

    def token_out(to):
        return remote(xa.at[s], xa.at[s], semxs.at[to], semxr.at[s], (f, to))

    def token_in(frm):
        return remote(xa.at[frm], xa.at[frm], semxs.at[frm], semxr.at[frm], (f, frm))

    for k in range(1, 8):
        first(k)[0].start()
    down_copy(xl).start()
    for to in range(1, 8):
        pl.when(to > s)(lambda to=to: token_out(to).start())
    r0[s] = s0b[s]
    rd0[xl] = d0b[xl]

    def item_ref(arrays, i):
        array, third = ITEMS[i][:2]
        return arrays[array] if third is None else arrays[array].at[third]

    def block(i, fixed):
        return item_ref(weights, i).at[select(ITEMS[i][3], fixed)]

    def put(i, value):
        array, third, _, names, _ = ITEMS[i]
        lead = () if third is None else (third,)
        weights[array][lead + select(names, at)] = value

    def ring(i, phase, k):
        order = ITEMS[i][2]
        axis = order[phase]
        fixed = {n: at[n] for n in ("x", "y", "z", "c") if n not in order[:phase]}
        theirs = {**fixed, axis: (at[axis] - k + 4) % 4}
        to = device(shifted(at, axis, k))
        send, recv = sems.at[i, phase, k - 1], semr.at[i, phase, k - 1]
        return remote(block(i, fixed), block(i, fixed), send, recv, to), remote(
            block(i, theirs), block(i, theirs), send, recv, to
        )

    def across(i, k):
        axis = ITEMS[i][2][2]
        mine = {axis: (at[axis] - k + 4) % 4, "c": at["c"]}
        theirs = {**mine, "c": 1 - at["c"]}
        send, recv = semcs.at[i, k], semcr.at[i, k]
        return remote(block(i, mine), block(i, mine), send, recv, sibling), remote(
            block(i, theirs), block(i, theirs), send, recv, sibling
        )

    def start(items, phase):
        for k in (1, 3, 2):
            for i in items:
                ring(i, phase, k)[0].start()

    def arrive(items, phase):
        for k in (1, 3, 2):
            for i in items:
                ring(i, phase, k)[1].wait_recv()

    for k in range(1, 8):
        first(k)[1].wait_recv()
    flat = r0[...].reshape(256, 384)
    piece = nn(one_hot(48, 256, 6, 16), flat).astype(BF16)
    for t in range(3):
        put(t, piece[:, t * 128 : (t + 1) * 128])
    start(small, 0)
    put(3, nn(one_hot(48, 256, 6, 0), flat).astype(BF16))
    put(4, nn(one_hot(48, 256, 6, 8), flat).astype(BF16))
    down_copy(1 - xl).wait_recv()
    put(5, nn(one_hot(48, 64, 24, 0), rd0[...].reshape(64, 384)).astype(BF16))
    start(large, 0)
    arrive(small, 0)
    start(small, 1)
    arrive(large, 0)
    start(large, 1)

    ends = [lens[0, 0], lens[0, 0] + lens[0, 1], lens[0, 0] + lens[0, 1] + lens[0, 2]]
    freq_lane = (lax.broadcasted_iota(jnp.int32, (1, 128), 1) % 32).astype(F32)
    freqs = jnp.exp(freq_lane * (-2.0 * math.log(ROPE_BASE) / HEAD_DIM))
    lane = lax.broadcasted_iota(jnp.int32, (128, 128), 1)

    def segment_of(index):
        return sum((index >= e).astype(jnp.int32) for e in ends)

    def table(u, carry):
        index = u * 128 + lax.broadcasted_iota(jnp.int32, (128, 1), 0)
        begin = jnp.zeros_like(index)
        for e in ends:
            begin = jnp.where(index >= e, e, begin)
        angle = (index - begin).astype(F32) * freqs
        rows = pl.ds(pl.multiple_of(u * 128, 128), 128)
        cosine[rows, :] = jnp.cos(angle)
        sine[rows, :] = jnp.where(lane % 64 < 32, -1.0, 1.0) * jnp.sin(angle)
        mine = s * 128 + lax.broadcasted_iota(jnp.int32, (1, 128), 1)
        allowed = (segment_of(index) == segment_of(mine)) & (index <= mine)
        bias[rows, :] = jnp.where(allowed, 0.0, MASKED_SCORE)
        return carry

    lax.fori_loop(0, 8, table, 0)

    arrive(small, 1)
    start(small, 2)
    for i in small:
        across(i, 0)[0].start()
    arrive(large, 1)
    start(large, 2)
    for i in large:
        across(i, 0)[0].start()
    for u in range(1, 8):

        def clear(u=u):
            xa[u] = jnp.zeros((128, 768), BF16)

        pl.when(u > s)(clear)
    for frm in range(0, 7):
        pl.when(frm < s)(lambda frm=frm: token_in(frm).wait_recv())

    def transpose_tokens(u, carry):
        xat[:, pl.ds(pl.multiple_of(u * 128, 128), 128)] = xa[u].T
        return carry

    lax.fori_loop(0, 8, transpose_tokens, 0)
    for k in (1, 3, 2):
        for i in small:
            ring(i, 2, k)[1].wait_recv()
            across(i, k)[0].start()
    for k in range(4):
        for i in small:
            across(i, k)[1].wait_recv()

    for k in range(1, 8):
        first(k)[0].wait_send()
    down_copy(xl).wait_send()
    for to in range(1, 8):
        pl.when(to > s)(lambda to=to: token_out(to).wait_send())

    mine = pl.ds(pl.multiple_of(s * 128, 128), 128)
    cos_mine, sin_mine = cosine[mine, :], sine[mine, :]
    left = lax.broadcasted_iota(jnp.int32, (128, 128), 1) < 64

    def attn_weight(kind, p):
        return wa[p % 3, kind, p // 3].reshape(768, 128)

    def attn_full(kind):
        return jnp.concatenate([attn_weight(kind, p) for p in range(6)], axis=1)

    def stacked(v):
        zero = jnp.zeros_like(v)
        return jnp.concatenate([jnp.where(left, v, zero), jnp.where(left, zero, v)], axis=0)

    def unstacked(v):
        return jnp.concatenate([v[:64, :128], v[64:, 128:]], axis=0).T

    def pair_lanes(p):
        return pl.ds(pl.multiple_of(p * 128, 128), 128)

    def attend(p, carry):
        tokens_all = xa[...].reshape(1024, 768)
        w_kv = jnp.concatenate([attn_weight(1, p), attn_weight(2, p)], axis=1)
        kv = nn(tokens_all, w_kv)
        k_raw = kv[:, :128]
        k = (k_raw * cosine[...] + swap_halves(k_raw) * sine[...]).astype(BF16)
        v = kv[:, 128:].astype(BF16)
        q_raw = nn(xa[s], attn_weight(0, p))
        q = ((q_raw * cos_mine + swap_halves(q_raw) * sin_mine).astype(BF16) * (1.0 / math.sqrt(HEAD_DIM))).astype(BF16)
        qq = stacked(q)
        ks[p] = k
        vs[p] = v
        qs[p] = qq
        masks = bias[...]
        scores = nt(k, qq) + jnp.concatenate([masks, masks], axis=1)
        top = jnp.max(scores, axis=0, keepdims=True)
        e = jnp.exp(scores - top)
        total = jnp.sum(e, axis=0, keepdims=True)
        probs = (e * (1.0 / total)).astype(BF16)
        ps[p] = probs
        att[:, pair_lanes(p)] = unstacked(tn(v, probs)).astype(BF16)
        return carry

    lax.fori_loop(0, 6, attend, 0)

    hidden = tok[...].astype(F32) + nn(att[...], attn_full(3))
    hid[...] = hidden
    factor_two = norm_factor(hidden)
    v2 = (hidden * factor_two).astype(BF16)
    v2t = v2.T
    oacc[...] = jnp.zeros_like(oacc)
    eacc[...] = jnp.zeros_like(eacc)

    for k in (1, 3, 2):
        for i in large:
            ring(i, 2, k)[1].wait_recv()
            across(i, k)[0].start()
    for k in range(4):
        for i in large:
            across(i, k)[1].wait_recv()

    def feed(b, carry):
        y, h = b // 2, b % 2
        g_w = wg[y, h].reshape(768, 384)
        u_w = wu[y, h].reshape(768, 384)
        d_w = jnp.concatenate([wd[0, b // 4, b % 4].reshape(384, 384), wd[1, b // 4, b % 4].reshape(384, 384)], axis=1)
        c = cot[...]
        gate = nn(v2, g_w)
        up = nn(v2, u_w)
        sig = 1.0 / (1.0 + jnp.exp(-gate))
        silu = gate * sig
        mixed = (silu * up).astype(BF16)
        oacc[...] += nn(mixed, d_w)
        d_mixed = nt(c, d_w)
        d_gate = (d_mixed * up * sig * (1.0 + gate * (1.0 - sig))).astype(BF16)
        d_up = (d_mixed * silu).astype(BF16)
        eacc[...] += nt(d_gate, g_w) + nt(d_up, u_w)
        gg[y, h] = nn(v2t, d_gate).astype(BF16).reshape(2, 4, 2, 48, 384)
        gu[y, h] = nn(v2t, d_up).astype(BF16).reshape(2, 4, 2, 48, 384)
        g_d = tn(mixed, c).astype(BF16)
        gd[0, b // 4, b % 4] = g_d[:, :384].reshape(2, 4, 48, 384)
        gd[1, b // 4, b % 4] = g_d[:, 384:].reshape(2, 4, 48, 384)
        return carry

    lax.fori_loop(0, 8, feed, 0)

    def give(sem):
        peers = [sibling] + [device(shifted(at, a, k)) for a in ("x", "y", "z") for k in (1, 2, 3)]
        for p in peers:
            pl.semaphore_signal(sem, inc=1, device_id=p, device_id_type=MESH)
        pl.semaphore_wait(sem, len(peers))

    def sent(items):
        for i in items:
            for phase in range(3):
                for k in (1, 2, 3):
                    ring(i, phase, k)[0].wait_send()
            for k in range(4):
                across(i, k)[0].wait_send()

    def chunk(i, l, core):
        return item_ref(grads, i).at[select(ITEMS[i][3], {ITEMS[i][2][2]: l, "c": core})]

    def store(i, l, core):
        return item_ref(weights, i).at[select(ITEMS[i][3], {ITEMS[i][2][2]: l, "c": core})]

    def share(i, k):
        l = (at[ITEMS[i][2][2]] + k) % 4
        return remote(chunk(i, l, 1 - at["c"]), store(i, l, 0), bemcs.at[i, k], bemcr.at[i, k], sibling)

    def hop(i, left, k):
        order = ITEMS[i][2]
        axis = order[left - 1]
        there = (at[axis] + k) % 4
        if left == 3:
            src, dst = store(i, there, 0), store(i, k - 1, 1)
        else:
            fixed = {order[2]: at[order[2]], "c": 0, axis: there}
            if left == 1:
                fixed[order[1]] = at[order[1]]
            src = item_ref(weights, i).at[select(ITEMS[i][3], fixed)]
            dst = t2[i].at[k - 1] if left == 2 else (t1a.at[i, k - 1] if i < 3 else t1m.at[i - 3, k - 1])
        send, recv = bems.at[i, left - 1, k - 1], bemr.at[i, left - 1, k - 1]
        return remote(src, dst, send, recv, device(shifted(at, axis, k)))

    def add_core(i, k):
        names, order = ITEMS[i][3], ITEMS[i][2]
        free = kept(names, order[:2])
        axis = order[2]
        l = (at[axis] + k) % 4
        g, r = item_ref(grads, i), item_ref(weights, i)

        def body(n, carry):
            gi = full_index(names, {axis: l, "c": at["c"]}, free, n)
            ri = full_index(names, {axis: l, "c": 0}, free, n)
            r[ri] = (r[ri].astype(F32) + g[gi].astype(F32)).astype(BF16)
            return carry

        lax.fori_loop(0, count(free), body, 0)

    def add_ring(i, left):
        names, order = ITEMS[i][3], ITEMS[i][2]
        axis = order[left - 1]
        free = kept(names, order[: left - 1])
        r = item_ref(weights, i)
        fixed = {order[2]: at[order[2]], "c": 0, axis: at[axis]}

        def body(n, carry):
            oi = full_index(names, fixed, free, n)
            total = r[oi].astype(F32)
            for k in range(3):
                if left == 3:
                    total = total + r[full_index(names, {axis: k, "c": 1}, free, n)].astype(F32)
                else:
                    total = total + t2[i][(k,) + full_index(free, {}, free, n)].astype(F32)
            r[oi] = total.astype(BF16)
            return carry

        lax.fori_loop(0, count(free), body, 0)

    def hop_arrive(i, left):
        for k in (1, 3, 2):
            hop(i, left, k).wait_recv()

    def last(i):
        hop_arrive(i, 1)
        fixed = {**at, "c": 0}
        total = item_ref(weights, i)[select(ITEMS[i][3], fixed)].astype(F32)
        for k in range(3):
            total = total + (t1a[i, k] if i < 3 else t1m[i - 3, k]).astype(F32)
        return total.astype(BF16)

    sent(large)
    give(free_large)
    for k in (1, 3, 2, 0):
        for i in large:
            share(i, k).start()

    hidden = hid[...]
    factor_two = norm_factor(hidden)
    out_o[...] = (hidden + oacc[...]).astype(BF16)
    d_hidden = cot[...].astype(F32) + norm_back(hidden, factor_two, eacc[...])
    dhid[...] = d_hidden
    dh = d_hidden.astype(BF16)
    d_att = nt(dh, attn_full(3)).astype(BF16)
    att_t = att[...].T
    for j in range(2):
        g_o = nn(att_t, dh[:, j * 384 : (j + 1) * 384]).astype(BF16)
        for t in range(3):
            ga[t, 3, j] = g_o[:, t * 128 : (t + 1) * 128].reshape(2, 4, 2, 48, 128)
    att[...] = d_att

    def attend_back(p, carry):
        da = stacked(att[:, pair_lanes(p)])
        k, v, qq, probs = ks[p], vs[p], qs[p], ps[p]
        d_probs = nt(v, da)
        probs_f = probs.astype(F32)
        d_sum = jnp.sum(probs_f * d_probs, axis=0, keepdims=True)
        d_scores = (probs_f * (d_probs - d_sum)).astype(BF16)
        d_v = nn(probs, da).astype(BF16)
        d_k = nn(d_scores, qq)
        d_k = (d_k * cosine[...] - swap_halves(d_k) * sine[...]).astype(BF16)
        d_q = unstacked(tn(k, d_scores)) * (1.0 / math.sqrt(HEAD_DIM))
        d_q = (d_q * cos_mine - swap_halves(d_q) * sin_mine).astype(BF16)
        ks[p] = d_k
        vs[p] = d_v
        dqs[:, pair_lanes(p)] = d_q
        g_kv = nn(xat[...], jnp.concatenate([d_k, d_v], axis=1)).astype(BF16)
        g_q = nn(xat[:, mine], d_q).astype(BF16)
        t, h = p % 3, p // 3
        ga[t, 0, h] = g_q.reshape(2, 4, 2, 48, 128)
        ga[t, 1, h] = g_kv[:, :128].reshape(2, 4, 2, 48, 128)
        ga[t, 2, h] = g_kv[:, 128:].reshape(2, 4, 2, 48, 128)
        return carry

    for j, k in enumerate((1, 3, 2)):
        lax.fori_loop(2 * j, 2 * j + 2, attend_back, 0)
        for i in large:
            share(i, k).wait_recv()
            add_core(i, k)
            hop(i, 3, k).start()

    w_kv = jnp.concatenate([attn_full(1), attn_full(2)], axis=1)

    def tokens_back(u, carry):
        rows = pl.ds(pl.multiple_of(u * 128, 128), 128)
        d_kv = jnp.concatenate([ks[p, rows, :] for p in range(6)] + [vs[p, rows, :] for p in range(6)], axis=1)
        xa[u] = nt(d_kv, w_kv).astype(BF16)
        return carry

    lax.fori_loop(0, 8, tokens_back, 0)

    def grad_out(to):
        return remote(xa.at[to], rdn.at[s], bemxs.at[to], bemxr.at[s], (f, to))

    def grad_in(frm):
        return remote(xa.at[frm], rdn.at[frm], bemxs.at[frm], bemxr.at[frm], (f, frm))

    for to in range(0, 7):
        pl.when(to < s)(lambda to=to: grad_out(to).start())
    eacc[...] = nt(dqs[...], attn_full(0))

    sent(small)
    give(free_small)
    for k in (1, 3, 2, 0):
        for i in small:
            share(i, k).start()

    for i in large:
        share(i, 0).wait_recv()
        add_core(i, 0)
    for k in (1, 3, 2):
        for i in small:
            share(i, k).wait_recv()
            add_core(i, k)
            hop(i, 3, k).start()
    for i in small:
        share(i, 0).wait_recv()
        add_core(i, 0)
    for i in large:
        hop_arrive(i, 3)
        add_ring(i, 3)
        for k in (1, 3, 2):
            hop(i, 2, k).start()
    for i in small:
        hop_arrive(i, 3)
        add_ring(i, 3)
        for k in (1, 3, 2):
            hop(i, 2, k).start()
    for i in large + small:
        hop_arrive(i, 2)
        add_ring(i, 2)
        for k in (1, 3, 2):
            hop(i, 1, k).start()

    eacc[...] += xa[s].astype(F32)
    for frm in range(1, 8):

        def add(frm=frm):
            grad_in(frm).wait_recv()
            eacc[...] += rdn[frm].astype(F32)

        pl.when(frm > s)(add)
    inputs = tok[...].astype(F32)
    in_o[...] = dhid[...] + norm_back(inputs, norm_factor(inputs), eacc[...])

    down, gate, up = last(5), last(3), last(4)
    attn = jnp.concatenate([last(0), last(1), last(2)], axis=1)
    rows = nn(one_hot(48, 256, 6, 0, True), gate)
    rows += nn(one_hot(48, 256, 6, 8, True), up)
    rows += nn(one_hot(48, 256, 6, 16, True), attn)
    fo[...] = rows.astype(BF16).reshape(8, 32, 384)
    fd0[...] = nn(one_hot(48, 64, 24, 0, True), down).astype(BF16).reshape(2, 32, 384)

    def final(k):
        to, frm = (s + k) % 8, (s - k + 8) % 8
        out = remote(fo.at[to], r0.at[s], bem0s.at[k - 1], bem0r.at[k - 1], (f, to))
        inn = remote(fo.at[to], r0.at[frm], bem0s.at[k - 1], bem0r.at[k - 1], (f, to))
        return out, inn

    def final_down(slot):
        return remote(fd0.at[1 - xl], rd0.at[slot], bemds, bemdr, beside)

    for k in range(1, 8):
        final(k)[0].start()
    final_down(xl).start()
    r0[s] = fo[s]
    rd0[xl] = fd0[xl]
    for k in range(1, 8):
        final(k)[1].wait_recv()
    final_down(1 - xl).wait_recv()

    s0[...] = r0[...].astype(F32)
    d0[...] = rd0[...].astype(F32)
    gain_sum_one = jnp.zeros((6, 1), F32)
    gain_sum_two = jnp.zeros((6, 1), F32)
    for b in range(8):
        lanes = pl.ds(b * 384, 384)
        half = pl.ds((b % 2) * 384, 384)
        h_gate, h_up, h_attn = s0[b, 0:6], s0[b, 8:14], s0[b, 16:22]
        gg_o[:, lanes] = h_gate * gain_two
        gu_o[:, lanes] = h_up * gain_two
        gain_sum_two += jnp.sum(h_gate * w_gate[:, lanes].astype(F32), axis=1, keepdims=True)
        gain_sum_two += jnp.sum(h_up * w_up[:, lanes].astype(F32), axis=1, keepdims=True)
        if b < 6:
            (gq_o, gk_o, gv_o)[b // 2][:, half] = h_attn * gain_one
            raw = (w_query, w_key, w_value)[b // 2][:, half].astype(F32)
            gain_sum_one += jnp.sum(h_attn * raw, axis=1, keepdims=True)
        else:
            go_o[:, half] = h_attn
    for b in range(2):
        gd_o[:, b * 384 : (b + 1) * 384] = d0[b, 0:24]
    ga1_o[...] = gain_sum_one
    ga2_o[...] = gain_sum_two

    for k in range(1, 8):
        final(k)[0].wait_send()
    final_down(xl).wait_send()
    for to in range(0, 7):
        pl.when(to < s)(lambda to=to: grad_out(to).wait_send())
    for i in range(6):
        for k in range(4):
            share(i, k).wait_send()
        for left in (3, 2, 1):
            for k in (1, 2, 3):
                hop(i, left, k).wait_send()


VMEM_SPEC = pl.BlockSpec(memory_space=pltpu.VMEM)
SMEM_SPEC = pl.BlockSpec(memory_space=pltpu.SMEM)
DMA = pltpu.SemaphoreType.DMA
REGULAR = pltpu.SemaphoreType.REGULAR


def layer(lens, gains, *arrays):
    outs = [
        ((128, 768), BF16), ((128, 768), F32), ((6, 1), F32),
        ((6, 768), F32), ((6, 768), F32), ((6, 768), F32), ((6, 768), F32),
        ((6, 1), F32), ((6, 3072), F32), ((6, 3072), F32), ((24, 768), F32),
    ]
    scratch = [(w, BF16) for w in W_SHAPES] * 2
    scratch += [
        ((8, 128, 768), BF16), ((768, 1024), BF16), ((8, 32, 384), BF16), ((2, 32, 384), BF16),
        ((8, 32, 384), F32), ((2, 32, 384), F32),
        ((6, 1024, 128), BF16), ((6, 1024, 128), BF16), ((6, 256, 128), BF16), ((6, 1024, 256), BF16),
        ((128, 768), BF16), ((128, 768), F32), ((128, 768), F32), ((128, 768), F32), ((128, 768), F32), ((128, 768), BF16),
        ((1024, 128), F32), ((1024, 128), F32), ((1024, 128), F32), ((8, 128, 768), BF16),
        ((8, 32, 384), BF16), ((2, 32, 384), BF16),
    ]
    for i in range(6):
        kept_dims = tuple(SIZES[n] for n in kept(ITEMS[i][3], ITEMS[i][2][:1]))
        scratch.append(((3,) + kept_dims + (48, ITEMS[i][4]), BF16))
    scratch += [((3, 3, 48, 128), BF16), ((3, 3, 48, 384), BF16)]
    copies = [
        DMA((7,)), DMA((7,)), DMA, DMA, DMA((8,)), DMA((8,)),
        DMA((6, 3, 3)), DMA((6, 3, 3)), DMA((6, 4)), DMA((6, 4)),
    ]
    return pl.pallas_call(
        layer_kernel,
        out_shape=[jax.ShapeDtypeStruct(shape, kind) for shape, kind in outs],
        in_specs=[SMEM_SPEC] * 2 + [VMEM_SPEC] * 9,
        out_specs=[VMEM_SPEC] * len(outs),
        scratch_shapes=[pltpu.VMEM(shape, kind) for shape, kind in scratch] + copies + copies + [REGULAR, REGULAR],
        compiler_params=pltpu.CompilerParams(collective_id=0, has_side_effects=True, vmem_limit_bytes=VMEM_LIMIT),
        name="layer",
    )(lens, gains, *arrays)


def per_device(tokens, doc_lengths, attn_gain, w_query, w_key, w_value, w_out, mlp_gain, w_gate, w_up, w_down, cotangent):
    gains = jnp.stack([attn_gain, mlp_gain]).astype(F32)
    out = layer(
        doc_lengths, gains, tokens[0], cotangent[0], w_query, w_key, w_value, w_out, w_gate, w_up, w_down
    )
    return (out[0][None], out[1][None], out[2][:, 0]) + tuple(out[3:7]) + (out[7][:, 0],) + tuple(out[8:])


def solution(mesh):
    rows = P(("fsdp", "seq"), None)
    gain = P(("fsdp", "seq"))
    toks = P("fsdp", "seq", None)
    return jax.shard_map(
        per_device,
        mesh=mesh,
        in_specs=(toks, P("fsdp", None), gain, rows, rows, rows, rows, gain, rows, rows, rows, toks),
        out_specs=(toks, toks, gain, rows, rows, rows, rows, gain, rows, rows, rows),
        check_vma=False,
    )
```

```python
import math

import jax
import jax.numpy as jnp
from jax import lax
from jax.experimental import pallas as pl
from jax.experimental.pallas import tpu as pltpu
from jax.sharding import PartitionSpec as P

HEADS = 12
HEAD_DIM = 64
EPSILON = 1e-05
ROPE_BASE = 10000.0
MASKED_SCORE = -1e30
VMEM_LIMIT = 62 * 2**20
MESH = pl.DeviceIdType.MESH
BF16 = jnp.bfloat16
F32 = jnp.float32

WIDE = ("y", "xl", "xh", "z")
TALL = ("xl", "xh", "z", "y")
SIZES = {"y": 4, "xl": 2, "xh": 2, "z": 4, "c": 2}
ORDERS = (("y", "z", "x"), ("z", "x", "y"), ("x", "y", "z"))
ITEMS = (
    (0, (0,), (), ORDERS[0], WIDE, (48, 128)),
    (0, (1,), (), ORDERS[1], WIDE, (48, 128)),
    (0, (2,), (), ORDERS[2], WIDE, (48, 128)),
    (1, (), (), ORDERS[0], WIDE, (96, 128)),
    (2, (), (), ORDERS[1], WIDE, (96, 128)),
    (3, (), (), ORDERS[2], TALL, (32, 384)),
    (4, (), (0,), ORDERS[0], WIDE, (48, 128)),
    (4, (), (1,), ORDERS[1], WIDE, (48, 128)),
    (5, (), (), ORDERS[2], TALL, (16, 384)),
)
W_SHAPES = (
    (3, 4, 2, 2, 4, 2, 48, 128),
    (4, 2, 2, 4, 96, 128),
    (4, 2, 2, 4, 96, 128),
    (2, 2, 4, 4, 32, 384),
    (4, 2, 2, 4, 2, 48, 128),
    (2, 2, 4, 4, 16, 384),
)


def place():
    f = lax.axis_index("fsdp")
    s = lax.axis_index("seq")
    return {"x": (f // 8) * 2 + s % 2, "y": s // 2, "z": (f // 2) % 4, "c": f % 2}


def device(at):
    return ((at["x"] // 2) * 8 + at["z"] * 2 + at["c"], at["y"] * 2 + at["x"] % 2)


def shifted(at, axis, k):
    return {**at, axis: (at[axis] + k) % SIZES.get(axis, 4)}


def select(names, fixed):
    index = []
    for n in names:
        if n in ("xl", "xh"):
            v = fixed.get("x")
            index.append(pl.ds(0, 2) if v is None else (v % 2 if n == "xl" else v // 2))
        else:
            v = fixed.get(n)
            index.append(pl.ds(0, SIZES[n]) if v is None else v)
    return tuple(index)


def expand(axes):
    return [n for a in axes for n in (("xl", "xh") if a == "x" else (a,))]


def kept(names, axes):
    some = expand(axes)
    return tuple(n for n in names if n in some)


def remote(src, dst, send, recv, to):
    return pltpu.make_async_remote_copy(
        src_ref=src, dst_ref=dst, send_sem=send, recv_sem=recv, device_id=to, device_id_type=MESH
    )


def greet(at):
    f = lax.axis_index("fsdp")
    s = lax.axis_index("seq")
    bar = pltpu.get_barrier_semaphore()
    peers = [(f, (s + k) % 8) for k in range(1, 8)]
    peers += [(f + 1 - 2 * (f % 2), (s + k) % 8) for k in range(8)]
    peers += [device(shifted(at, "z", k)) for k in (1, 2, 3)]
    peers += [device({**at, "x": (at["x"] + 2) % 4})]
    peers += [device({**at, "x": (at["x"] // 2 * 2 + 2) % 4 + (1 - at["x"] % 2)})]
    for p in peers:
        pl.semaphore_signal(bar, inc=1, device_id=p, device_id_type=MESH)
    pl.semaphore_wait(bar, len(peers))


def one_hot(rows, slots, per, size, offset, flip=False):
    shape = (slots * size, rows) if flip else (rows, slots * size)
    i = lax.broadcasted_iota(jnp.int32, shape, 1 if flip else 0)
    j = lax.broadcasted_iota(jnp.int32, shape, 0 if flip else 1)
    return (j == (i // per) * size + offset + i % per).astype(BF16)


def units(core, up, flip=False):
    i = lax.broadcasted_iota(jnp.int32, (384, 384), 1 if flip else 0)
    j = lax.broadcasted_iota(jnp.int32, (384, 384), 0 if flip else 1)
    y, r = (i % 192) // 48, i % 48
    early = y * 32 + r + (128 if up else 0)
    late = y * 16 + r - 32 + (320 if up else 256)
    return ((i // 192 == core) & (j == jnp.where(r < 32, early, late))).astype(BF16)


def nn(a, b):
    return jnp.dot(a, b, preferred_element_type=F32)


def nt(a, b):
    return lax.dot_general(a, b, (((1,), (1,)), ((), ())), preferred_element_type=F32)


def tn(a, b):
    return lax.dot_general(a, b, (((0,), (0,)), ((), ())), preferred_element_type=F32)


def norm_factor(values):
    return lax.rsqrt(jnp.mean(values * values, axis=-1, keepdims=True) + EPSILON)


def norm_back(values, factor, e):
    return factor * e - values * (factor * factor * factor * jnp.mean(e * values, axis=-1, keepdims=True))


def swap_halves(v):
    lane = lax.broadcasted_iota(jnp.int32, v.shape, 1)
    return jnp.where(lane % 64 < 32, pltpu.roll(v, 96, 1), pltpu.roll(v, 32, 1))


def digits(names, n):
    out = {}
    for name in reversed(names):
        out[name] = n % SIZES[name]
        n = n // SIZES[name]
    return out


def full_index(names, fixed, free, n):
    got = digits(free, n)
    index = []
    for name in names:
        if name in free:
            index.append(got[name])
        elif name in ("xl", "xh"):
            index.append(fixed["x"] % 2 if name == "xl" else fixed["x"] // 2)
        else:
            index.append(fixed[name])
    return tuple(index)


def count(names):
    return math.prod(SIZES[n] for n in names)


def layer_kernel(
    lens, gains, tok, cot, w_query, w_key, w_value, w_out, w_gate, w_up, w_down,
    out_o, in_o, ga1_o, gq_o, gk_o, gv_o, go_o, ga2_o, gg_o, gu_o, gd_o,
    wa, wg, wu, wd, wm, we, ga, gg, gu, gd, gm, ge,
    xa, xat, r0, rd0, s0, d0, s0b, d0b, ks, vs, qs, ps, att, hid, dhid, dqs, cosine, sine, bias, rdn,
    v2s, cs, oacc, eacc, osum, esum, ra, *rest
):
    at = place()
    f = lax.axis_index("fsdp")
    s = lax.axis_index("seq")
    t3, t2, t1 = rest[:9], rest[9:18], rest[18:27]
    sem0s, sem0r, semds, semdr, semxs, semxr, sems, semr, semcs, semcr, semps, sempr = rest[27:39]
    bem0s, bem0r, bemds, bemdr, bems, bemr, bemcs, bemcr = rest[39:]
    weights = (wa, wg, wu, wd, wm, we)
    grads = (ga, gg, gu, gd, gm, ge)
    sibling = device(shifted(at, "c", 1))
    xl = at["x"] % 2
    beside = (f, at["y"] * 2 + 1 - xl)
    small, early, late = (0, 1, 2), (5, 3, 4), (8, 6, 7)
    large = early + late

    row = lax.broadcasted_iota(jnp.int32, (6, 1), 0)

    def gain_column(which):
        col = jnp.zeros((6, 1), F32)
        for r in range(6):
            col = jnp.where(row == r, gains[which, r], col)
        return col

    gain_one, gain_two = gain_column(0), gain_column(1)
    inputs = tok[...].astype(F32)
    factor_one = norm_factor(inputs)
    xa[s] = (inputs * factor_one).astype(BF16)
    cs[at["c"]] = cot[...]
    s0[...] = jnp.zeros_like(s0)
    d0[...] = jnp.zeros_like(d0)
    for b in range(8):
        lanes = pl.ds(b * 384, 384)
        half = pl.ds((b % 2) * 384, 384)
        s0[0, b, 0:6] = w_gate[:, lanes].astype(F32) * gain_two
        s0[1, b, 0:6] = w_up[:, lanes].astype(F32) * gain_two
        if b < 6:
            s0[2, b, 0:6] = (w_query, w_key, w_value)[b // 2][:, half].astype(F32) * gain_one
        else:
            s0[2, b, 0:6] = w_out[:, half].astype(F32)
    for b in range(2):
        d0[b, 0:24] = w_down[:, b * 384 : (b + 1) * 384].astype(F32)
    d0b[...] = d0[...].astype(BF16)
    gate_rows = s0[0].reshape(64, 384).astype(BF16)
    up_rows = s0[1].reshape(64, 384).astype(BF16)
    for core in range(2):
        rows = nn(gate_rows, units(core, False)) + nn(up_rows, units(core, True))
        s0b[core] = jnp.concatenate([rows.reshape(8, 8, 384), s0[2]], axis=1).astype(BF16)

    greet(at)

    def group(k, src, dst, sends, recvs):
        me = at["c"] * 8 + s
        to, frm = (me + k) % 16, (me - k + 16) % 16
        peer = (f - at["c"] + to // 8, to % 8)
        send, recv = sends.at[k - 1], recvs.at[k - 1]
        out = remote(src.at[to // 8, to % 8], dst.at[me], send, recv, peer)
        inn = remote(src.at[to // 8, to % 8], dst.at[frm], send, recv, peer)
        return out, inn

    def first(k):
        return group(k, s0b, r0, sem0s, sem0r)

    def swap(buf, n):
        c = at["c"]
        return remote(buf.at[c], buf.at[c], semps.at[n], sempr.at[n], sibling)

    def swapped(buf, n):
        c = at["c"]
        return remote(buf.at[c], buf.at[1 - c], semps.at[n], sempr.at[n], sibling)

    def down_copy(slot):
        return remote(d0b.at[1 - xl], rd0.at[slot], semds, semdr, beside)

    def token_out(to):
        return remote(xa.at[s], xa.at[s], semxs.at[to], semxr.at[s], (f, to))

    def token_in(frm):
        return remote(xa.at[frm], xa.at[frm], semxs.at[frm], semxr.at[frm], (f, frm))

    for k in range(1, 16):
        first(k)[0].start()
    down_copy(xl).start()
    swap(cs, 0).start()
    r0[at["c"] * 8 + s] = s0b[at["c"], s]
    rd0[xl] = d0b[xl]

    def cored(i, core):
        return (core,) if i < 3 else ()

    def block(i, fixed, core):
        array, lead, tail, _, names, _ = ITEMS[i]
        return weights[array].at[lead + select(names, fixed) + cored(i, core) + tail]

    def put(i, value):
        array, lead, tail, _, names, _ = ITEMS[i]
        weights[array][lead + select(names, at) + cored(i, at["c"]) + tail] = value

    def ring(i, phase, k):
        order = ITEMS[i][3]
        axis = order[phase]
        fixed = {n: at[n] for n in ("x", "y", "z") if n not in order[:phase]}
        theirs = {**fixed, axis: (at[axis] - k + 4) % 4}
        to = device(shifted(at, axis, k))
        mine, other = block(i, fixed, at["c"]), block(i, theirs, at["c"])
        send, recv = sems.at[i, phase, k - 1], semr.at[i, phase, k - 1]
        return remote(mine, mine, send, recv, to), remote(other, other, send, recv, to)

    def across(i, k):
        axis = ITEMS[i][3][2]
        where = {axis: (at[axis] - k + 4) % 4}
        mine, other = block(i, where, at["c"]), block(i, where, 1 - at["c"])
        send, recv = semcs.at[i, k], semcr.at[i, k]
        return remote(mine, mine, send, recv, sibling), remote(other, other, send, recv, sibling)

    def start(items, phase):
        for k in (1, 3, 2):
            for i in items:
                ring(i, phase, k)[0].start()

    def arrive(items, phase):
        for k in (1, 3, 2):
            for i in items:
                ring(i, phase, k)[1].wait_recv()

    for k in range(1, 16):
        first(k)[1].wait_recv()
    flat = r0[...].reshape(256, 384)
    piece = nn(one_hot(48, 16, 6, 16, at["c"] * 128 + 8), flat).astype(BF16)
    for j in range(3):
        put(j, piece[:, j * 128 : (j + 1) * 128])
    start(small, 0)
    piece = nn(one_hot(96, 16, 6, 16, 0), flat).astype(BF16)
    put(3, piece[:, :128])
    put(4, piece[:, 128:256])
    put(6, piece[:48, 256:])
    put(7, piece[48:, 256:])
    down_copy(1 - xl).wait_recv()
    piece = nn(one_hot(48, 2, 24, 32, 0), rd0[...].reshape(64, 384)).astype(BF16)
    put(5, piece[:32])
    put(8, piece[32:])
    start(large, 0)
    arrive(small, 0)
    start(small, 1)
    arrive(large, 0)
    start(large, 1)

    ends = [lens[0, 0], lens[0, 0] + lens[0, 1], lens[0, 0] + lens[0, 1] + lens[0, 2]]
    freq_lane = (lax.broadcasted_iota(jnp.int32, (1, 128), 1) % 32).astype(F32)
    freqs = jnp.exp(freq_lane * (-2.0 * math.log(ROPE_BASE) / HEAD_DIM))
    lane = lax.broadcasted_iota(jnp.int32, (128, 128), 1)

    def segment_of(index):
        return sum((index >= e).astype(jnp.int32) for e in ends)

    def table(u, carry):
        index = u * 128 + lax.broadcasted_iota(jnp.int32, (128, 1), 0)
        begin = jnp.zeros_like(index)
        for e in ends:
            begin = jnp.where(index >= e, e, begin)
        angle = (index - begin).astype(F32) * freqs
        rows = pl.ds(pl.multiple_of(u * 128, 128), 128)
        cosine[rows, :] = jnp.cos(angle)
        sine[rows, :] = jnp.where(lane % 64 < 32, -1.0, 1.0) * jnp.sin(angle)
        mine = s * 128 + lax.broadcasted_iota(jnp.int32, (1, 128), 1)
        allowed = (segment_of(index) == segment_of(mine)) & (index <= mine)
        bias[rows, :] = jnp.where(allowed, 0.0, MASKED_SCORE)
        return carry

    lax.fori_loop(0, 8, table, 0)

    arrive(small, 1)
    start(small, 2)
    for i in small:
        across(i, 0)[0].start()
    for to in range(1, 8):
        pl.when(to > s)(lambda to=to: token_out(to).start())
    arrive(large, 1)
    start(early, 2)
    start(late, 2)
    for u in range(1, 8):

        def clear(u=u):
            xa[u] = jnp.zeros((128, 768), BF16)

        pl.when(u > s)(clear)
    for frm in range(0, 7):
        pl.when(frm < s)(lambda frm=frm: token_in(frm).wait_recv())

    def transpose_tokens(u, carry):
        xat[:, pl.ds(pl.multiple_of(u * 128, 128), 128)] = xa[u].T
        return carry

    lax.fori_loop(0, 8, transpose_tokens, 0)
    for k in (1, 3, 2):
        for i in small:
            ring(i, 2, k)[1].wait_recv()
            across(i, k)[0].start()
    for k in range(4):
        for i in small:
            across(i, k)[1].wait_recv()

    for k in range(1, 16):
        first(k)[0].wait_send()
    down_copy(xl).wait_send()
    for to in range(1, 8):
        pl.when(to > s)(lambda to=to: token_out(to).wait_send())

    mine = pl.ds(pl.multiple_of(s * 128, 128), 128)
    cos_mine, sin_mine = cosine[mine, :], sine[mine, :]
    left = lax.broadcasted_iota(jnp.int32, (128, 128), 1) < 64

    def attn_weight(kind, p):
        return wa[p % 3, kind, p // 3].reshape(768, 128)

    def attn_full(kind):
        return jnp.concatenate([attn_weight(kind, p) for p in range(6)], axis=1)

    def stacked(v):
        zero = jnp.zeros_like(v)
        return jnp.concatenate([jnp.where(left, v, zero), jnp.where(left, zero, v)], axis=0)

    def unstacked(v):
        return jnp.concatenate([v[:64, :128], v[64:, 128:]], axis=0).T

    def pair_lanes(p):
        return pl.ds(pl.multiple_of(p * 128, 128), 128)

    def attend(p, carry):
        tokens_all = xa[...].reshape(1024, 768)
        w_kv = jnp.concatenate([attn_weight(1, p), attn_weight(2, p)], axis=1)
        kv = nn(tokens_all, w_kv)
        k_raw = kv[:, :128]
        k = (k_raw * cosine[...] + swap_halves(k_raw) * sine[...]).astype(BF16)
        v = kv[:, 128:].astype(BF16)
        q_raw = nn(xa[s], attn_weight(0, p))
        q = ((q_raw * cos_mine + swap_halves(q_raw) * sin_mine).astype(BF16) * (1.0 / math.sqrt(HEAD_DIM))).astype(BF16)
        qq = stacked(q)
        ks[p] = k
        vs[p] = v
        qs[p] = qq
        masks = bias[...]
        scores = nt(k, qq) + jnp.concatenate([masks, masks], axis=1)
        top = jnp.max(scores, axis=0, keepdims=True)
        e = jnp.exp(scores - top)
        total = jnp.sum(e, axis=0, keepdims=True)
        probs = (e * (1.0 / total)).astype(BF16)
        ps[p] = probs
        att[:, pair_lanes(p)] = unstacked(tn(v, probs)).astype(BF16)
        return carry

    lax.fori_loop(0, 6, attend, 0)

    hidden = tok[...].astype(F32) + nn(att[...], attn_full(3))
    hid[...] = hidden
    factor_two = norm_factor(hidden)
    v2s[at["c"]] = (hidden * factor_two).astype(BF16)
    swap(v2s, 1).start()
    oacc[...] = jnp.zeros_like(oacc)
    eacc[...] = jnp.zeros_like(eacc)
    swapped(cs, 0).wait()
    swapped(v2s, 1).wait()
    v2 = v2s[...].reshape(256, 768)
    v2t = v2.T

    def pair(a, b):
        return jnp.concatenate([a, b], axis=1)

    def gated(gate, up, d_w):
        c = cs[...].reshape(256, 768)
        sig = 1.0 / (1.0 + jnp.exp(-gate))
        silu = gate * sig
        mixed = (silu * up).astype(BF16)
        oacc[...] += nn(mixed, d_w).reshape(2, 128, 768)
        d_mixed = nt(c, d_w)
        d_gate = d_mixed * up * sig * (1.0 + gate * (1.0 - sig))
        d_up = d_mixed * silu
        return d_gate, d_up, tn(mixed, c).astype(BF16)

    def feed_early(y, carry):
        g_w = pair(wg[y, 0].reshape(768, 128), wg[y, 1].reshape(768, 128))
        u_w = pair(wu[y, 0].reshape(768, 128), wu[y, 1].reshape(768, 128))
        xh, z = y // 2, (y % 2) * 2
        d_w = jnp.concatenate(
            [pair(wd[0, xh, z + b].reshape(128, 384), wd[1, xh, z + b].reshape(128, 384)) for b in range(2)], axis=0
        )
        d_gate, d_up, g_d = gated(nn(v2, g_w), nn(v2, u_w), d_w)
        d_gate, d_up = d_gate.astype(BF16), d_up.astype(BF16)
        eacc[...] += (nt(d_gate, g_w) + nt(d_up, u_w)).reshape(2, 128, 768)
        g_g = nn(v2t, d_gate).astype(BF16)
        g_u = nn(v2t, d_up).astype(BF16)
        for b in range(2):
            lanes = slice(b * 128, (b + 1) * 128)
            gg[y, b] = g_g[:, lanes].reshape(2, 4, 96, 128)
            gu[y, b] = g_u[:, lanes].reshape(2, 4, 96, 128)
            for h in range(2):
                gd[h, xh, z + b] = g_d[lanes, h * 384 : (h + 1) * 384].reshape(4, 32, 384)
        return carry

    def feed_late(y, carry):
        w = pair(wm[y, 0].reshape(768, 128), wm[y, 1].reshape(768, 128))
        xh, z = y // 2, (y % 2) * 2
        d_w = jnp.concatenate(
            [pair(we[0, xh, z + b].reshape(64, 384), we[1, xh, z + b].reshape(64, 384)) for b in range(2)], axis=0
        )
        both = nn(v2, w)
        low = lax.broadcasted_iota(jnp.int32, (256, 128), 1) < 64

        def mix(a, b):
            return jnp.where(low, a, pltpu.roll(b, 64, 1)), jnp.where(low, pltpu.roll(a, 64, 1), b)

        gate, up = mix(both[:, :128], both[:, 128:])
        d_gate, d_up, g_d = gated(gate, up, d_w)
        d_both = pair(*mix(d_gate, d_up)).astype(BF16)
        eacc[...] += nt(d_both, w).reshape(2, 128, 768)
        g = nn(v2t, d_both).astype(BF16)
        for b in range(2):
            gm[y, b] = g[:, b * 128 : (b + 1) * 128].reshape(2, 4, 2, 48, 128)
            for h in range(2):
                ge[h, xh, z + b] = g_d[b * 64 : (b + 1) * 64, h * 384 : (h + 1) * 384].reshape(4, 16, 384)
        return carry

    def home(i):
        array, lead, tail = ITEMS[i][:3]
        return (ra, lead, ()) if i < 3 else (grads[array], lead, tail)

    def home_at(i, index):
        ref, lead, tail = home(i)
        return ref.at[lead + index + tail]

    def share(i, k):
        axis = ITEMS[i][3][2]
        where = select(ITEMS[i][4], {axis: (at[axis] + k) % 4})
        part = ga.at[ITEMS[i][1] + where + (1 - at["c"],)]
        return remote(part, home_at(i, where), bemcs.at[i, k], bemcr.at[i, k], sibling)

    def hop(i, left, k):
        order, names = ITEMS[i][3:5]
        axis = order[left - 1]
        fixed = {a: at[a] for a in order[left:]}
        src = home_at(i, select(names, {**fixed, axis: (at[axis] + k) % 4}))
        dst = (t1, t2, t3)[left - 1][i].at[k - 1]
        send, recv = bems.at[i, left - 1, k - 1], bemr.at[i, left - 1, k - 1]
        return remote(src, dst, send, recv, device(shifted(at, axis, k)))

    def add_core(i, k):
        order, names = ITEMS[i][3:5]
        free = kept(names, order[:2])
        axis = order[2]
        fixed = {axis: (at[axis] + k) % 4}

        def body(n, carry):
            index = ITEMS[i][1] + full_index(names, fixed, free, n)
            ra[index] = (ra[index].astype(F32) + ga[index + (at["c"],)].astype(F32)).astype(BF16)
            return carry

        lax.fori_loop(0, count(free), body, 0, unroll=4)

    def add_ring(i, left):
        order, names = ITEMS[i][3:5]
        free = kept(names, order[: left - 1])
        fixed = {a: at[a] for a in order[left - 1 :]}
        ref, lead, tail = home(i)
        came = (t1, t2, t3)[left - 1][i]

        def body(n, carry):
            index = lead + full_index(names, fixed, free, n) + tail
            total = ref[index].astype(F32)
            for k in range(3):
                total = total + came[(k,) + full_index(free, {}, free, n)].astype(F32)
            ref[index] = total.astype(BF16)
            return carry

        lax.fori_loop(0, count(free), body, 0, unroll=4)

    def hop_start(items, left):
        for k in (1, 3, 2):
            for i in items:
                hop(i, left, k).start()

    def hop_on(i, left):
        for k in (1, 3, 2):
            hop(i, left, k).wait_recv()
        add_ring(i, left)
        hop_start((i,), left - 1)

    def last(i):
        for k in (1, 3, 2):
            hop(i, 1, k).wait_recv()
        ref, lead, tail = home(i)
        total = ref[lead + select(ITEMS[i][4], at) + tail].astype(F32)
        for k in range(3):
            total = total + t1[i][k].astype(F32)
        return total.astype(BF16)

    def sent(items):
        for i in items:
            for phase in range(3):
                for k in (1, 2, 3):
                    ring(i, phase, k)[0].wait_send()
            if i < 3:
                for k in range(4):
                    across(i, k)[0].wait_send()

    arrive(early, 2)
    lax.fori_loop(0, 4, feed_early, 0)
    sent(large)
    hop_start(early, 3)
    arrive(late, 2)
    lax.fori_loop(0, 4, feed_late, 0)
    sum_o = remote(oacc.at[1 - at["c"]], osum, semps.at[2], sempr.at[2], sibling)
    sum_e = remote(eacc.at[1 - at["c"]], esum, semps.at[3], sempr.at[3], sibling)
    sum_e.start()
    sum_o.start()
    hop_start(late, 3)
    sum_e.wait()

    hidden = hid[...]
    factor_two = norm_factor(hidden)
    d_hidden = cot[...].astype(F32) + norm_back(hidden, factor_two, eacc[at["c"]] + esum[...])
    dhid[...] = d_hidden
    dh = d_hidden.astype(BF16)
    d_att = nt(dh, attn_full(3)).astype(BF16)
    att_t = att[...].T
    for j in range(2):
        g_o = nn(att_t, dh[:, j * 384 : (j + 1) * 384]).astype(BF16)
        for t in range(3):
            ga[t, 3, j] = g_o[:, t * 128 : (t + 1) * 128].reshape(2, 4, 2, 48, 128)
    att[...] = d_att

    def attend_back(p, carry):
        da = stacked(att[:, pair_lanes(p)])
        k, v, qq, probs = ks[p], vs[p], qs[p], ps[p]
        d_probs = nt(v, da)
        probs_f = probs.astype(F32)
        d_sum = jnp.sum(probs_f * d_probs, axis=0, keepdims=True)
        d_scores = (probs_f * (d_probs - d_sum)).astype(BF16)
        d_v = nn(probs, da).astype(BF16)
        d_k = nn(d_scores, qq)
        d_k = (d_k * cosine[...] - swap_halves(d_k) * sine[...]).astype(BF16)
        d_q = unstacked(tn(k, d_scores)) * (1.0 / math.sqrt(HEAD_DIM))
        d_q = (d_q * cos_mine - swap_halves(d_q) * sin_mine).astype(BF16)
        ks[p] = d_k
        vs[p] = d_v
        dqs[:, pair_lanes(p)] = d_q
        g_kv = nn(xat[...], jnp.concatenate([d_k, d_v], axis=1)).astype(BF16)
        g_q = nn(xat[:, mine], d_q).astype(BF16)
        t, h = p % 3, p // 3
        ga[t, 0, h] = g_q.reshape(2, 4, 2, 48, 128)
        ga[t, 1, h] = g_kv[:, :128].reshape(2, 4, 2, 48, 128)
        ga[t, 2, h] = g_kv[:, 128:].reshape(2, 4, 2, 48, 128)
        return carry

    def back_on(t):
        for k in (1, 3, 2, 0):
            share(t, k).wait_recv()
            add_core(t, k)
            if k:
                hop(t, 3, k).start()

    for t in range(3):

        def third_back(h, carry, t=t):
            return attend_back(t + 3 * h, carry)

        lax.fori_loop(0, 2, third_back, 0)
        for k in (1, 3, 2, 0):
            share(t, k).start()
        if t:
            back_on(t - 1)

    w_kv = jnp.concatenate([attn_full(1), attn_full(2)], axis=1)

    def tokens_back(u, carry):
        rows = pl.ds(pl.multiple_of(u * 128, 128), 128)
        d_kv = jnp.concatenate([ks[p, rows, :] for p in range(6)] + [vs[p, rows, :] for p in range(6)], axis=1)
        xa[u] = nt(d_kv, w_kv).astype(BF16)
        return carry

    lax.fori_loop(0, 8, tokens_back, 0)

    def grad_out(to):
        return remote(xa.at[to], rdn.at[s], semxs.at[to], semxr.at[s], (f, to))

    def grad_in(frm):
        return remote(xa.at[frm], rdn.at[frm], semxs.at[frm], semxr.at[frm], (f, frm))

    for to in range(0, 7):
        pl.when(to < s)(lambda to=to: grad_out(to).start())
    sum_o.wait()
    out_o[...] = (hid[...] + oacc[at["c"]] + osum[...]).astype(BF16)
    esum[...] = nt(dqs[...], attn_full(0))

    back_on(2)
    for i in early + late:
        hop_on(i, 3)
    for i in small:
        hop_on(i, 3)
    for i in early + late + small:
        hop_on(i, 2)

    esum[...] += xa[s].astype(F32)
    for frm in range(1, 8):

        def add(frm=frm):
            grad_in(frm).wait_recv()
            esum[...] += rdn[frm].astype(F32)

        pl.when(frm > s)(add)
    inputs = tok[...].astype(F32)
    in_o[...] = dhid[...] + norm_back(inputs, norm_factor(inputs), esum[...])

    down = jnp.concatenate([last(5), last(8)], axis=0)
    both = jnp.concatenate([last(3), last(4), jnp.concatenate([last(6), last(7)], axis=0)], axis=1)
    attn = jnp.concatenate([last(t) for t in small], axis=1)
    rows = nn(one_hot(96, 16, 6, 16, 0, True), both)
    rows += nn(one_hot(48, 16, 6, 16, at["c"] * 128 + 8, True), attn)
    s0b[...] = rows.astype(BF16).reshape(2, 8, 16, 384)
    d0b[...] = nn(one_hot(48, 2, 24, 32, 0, True), down).astype(BF16).reshape(2, 32, 384)

    def final(k):
        return group(k, s0b, r0, bem0s, bem0r)

    def final_down(slot):
        return remote(d0b.at[1 - xl], rd0.at[slot], bemds, bemdr, beside)

    for k in range(1, 16):
        final(k)[0].start()
    final_down(xl).start()
    r0[at["c"] * 8 + s] = s0b[at["c"], s]
    rd0[xl] = d0b[xl]
    for k in range(1, 16):
        final(k)[1].wait_recv()
    final_down(1 - xl).wait_recv()

    got = r0[...].reshape(2, 8, 16, 384)
    halves = [got[core, :, :8].reshape(64, 384) for core in range(2)]
    for which in range(2):
        natural = nn(halves[0], units(0, which == 1, True)) + nn(halves[1], units(1, which == 1, True))
        s0[which] = natural.reshape(8, 8, 384)
    s0[2] = r0[pl.ds(at["c"] * 8, 8), 8:, :].astype(F32)
    d0[...] = rd0[...].astype(F32)
    gain_sum_one = jnp.zeros((6, 1), F32)
    gain_sum_two = jnp.zeros((6, 1), F32)
    for b in range(8):
        lanes = pl.ds(b * 384, 384)
        half = pl.ds((b % 2) * 384, 384)
        h_gate, h_up, h_attn = s0[0, b, 0:6], s0[1, b, 0:6], s0[2, b, 0:6]
        gg_o[:, lanes] = h_gate * gain_two
        gu_o[:, lanes] = h_up * gain_two
        gain_sum_two += jnp.sum(h_gate * w_gate[:, lanes].astype(F32), axis=1, keepdims=True)
        gain_sum_two += jnp.sum(h_up * w_up[:, lanes].astype(F32), axis=1, keepdims=True)
        if b < 6:
            (gq_o, gk_o, gv_o)[b // 2][:, half] = h_attn * gain_one
            raw = (w_query, w_key, w_value)[b // 2][:, half].astype(F32)
            gain_sum_one += jnp.sum(h_attn * raw, axis=1, keepdims=True)
        else:
            go_o[:, half] = h_attn
    for b in range(2):
        gd_o[:, b * 384 : (b + 1) * 384] = d0[b, 0:24]
    ga1_o[...] = gain_sum_one
    ga2_o[...] = gain_sum_two

    for k in range(1, 16):
        final(k)[0].wait_send()
    final_down(xl).wait_send()
    for to in range(0, 7):
        pl.when(to < s)(lambda to=to: grad_out(to).wait_send())
    sent(small)
    for i in range(9):
        if i < 3:
            for k in range(4):
                share(i, k).wait_send()
        for left in (3, 2, 1):
            for k in (1, 2, 3):
                hop(i, left, k).wait_send()


VMEM_SPEC = pl.BlockSpec(memory_space=pltpu.VMEM)
SMEM_SPEC = pl.BlockSpec(memory_space=pltpu.SMEM)
DMA = pltpu.SemaphoreType.DMA


def layer(lens, gains, *arrays):
    outs = [
        ((128, 768), BF16), ((128, 768), F32), ((6, 1), F32),
        ((6, 768), F32), ((6, 768), F32), ((6, 768), F32), ((6, 768), F32),
        ((6, 1), F32), ((6, 3072), F32), ((6, 3072), F32), ((24, 768), F32),
    ]
    scratch = [(w, BF16) for w in W_SHAPES] * 2
    scratch += [
        ((8, 128, 768), BF16), ((768, 1024), BF16), ((16, 16, 384), BF16), ((2, 32, 384), BF16),
        ((3, 8, 8, 384), F32), ((2, 32, 384), F32), ((2, 8, 16, 384), BF16), ((2, 32, 384), BF16),
        ((6, 1024, 128), BF16), ((6, 1024, 128), BF16), ((6, 256, 128), BF16), ((6, 1024, 256), BF16),
        ((128, 768), BF16), ((128, 768), F32), ((128, 768), F32), ((128, 768), BF16),
        ((1024, 128), F32), ((1024, 128), F32), ((1024, 128), F32), ((8, 128, 768), BF16),
        ((2, 128, 768), BF16), ((2, 128, 768), BF16), ((2, 128, 768), F32), ((2, 128, 768), F32),
        ((128, 768), F32), ((128, 768), F32), ((3, 4, 2, 2, 4, 48, 128), BF16),
    ]
    for rings in (2, 1, 0):
        for item in ITEMS:
            left = tuple(SIZES[n] for n in kept(item[4], item[3][:rings]))
            scratch.append(((3,) + left + item[5], BF16))
    copies = [
        DMA((15,)), DMA((15,)), DMA, DMA, DMA((8,)), DMA((8,)),
        DMA((9, 3, 3)), DMA((9, 3, 3)), DMA((3, 4)), DMA((3, 4)), DMA((4,)), DMA((4,)),
        DMA((15,)), DMA((15,)), DMA, DMA, DMA((9, 3, 3)), DMA((9, 3, 3)), DMA((3, 4)), DMA((3, 4)),
    ]
    return pl.pallas_call(
        layer_kernel,
        out_shape=[jax.ShapeDtypeStruct(shape, kind) for shape, kind in outs],
        in_specs=[SMEM_SPEC] * 2 + [VMEM_SPEC] * 9,
        out_specs=[VMEM_SPEC] * len(outs),
        scratch_shapes=[pltpu.VMEM(shape, kind) for shape, kind in scratch] + copies,
        compiler_params=pltpu.CompilerParams(collective_id=0, has_side_effects=True, vmem_limit_bytes=VMEM_LIMIT),
        name="layer",
    )(lens, gains, *arrays)


def per_device(tokens, doc_lengths, attn_gain, w_query, w_key, w_value, w_out, mlp_gain, w_gate, w_up, w_down, cotangent):
    gains = jnp.stack([attn_gain, mlp_gain]).astype(F32)
    out = layer(
        doc_lengths, gains, tokens[0], cotangent[0], w_query, w_key, w_value, w_out, w_gate, w_up, w_down
    )
    return (out[0][None], out[1][None], out[2][:, 0]) + tuple(out[3:7]) + (out[7][:, 0],) + tuple(out[8:])


def solution(mesh):
    rows = P(("fsdp", "seq"), None)
    gain = P(("fsdp", "seq"))
    toks = P("fsdp", "seq", None)
    return jax.shard_map(
        per_device,
        mesh=mesh,
        in_specs=(toks, P("fsdp", None), gain, rows, rows, rows, rows, gain, rows, rows, rows, toks),
        out_specs=(toks, toks, gain, rows, rows, rows, rows, gain, rows, rows, rows),
        check_vma=False,
    )
```

```python
import math

import jax
import jax.numpy as jnp
from jax import lax
from jax.experimental import pallas as pl
from jax.experimental.pallas import tpu as pltpu
from jax.sharding import PartitionSpec as P

HEADS = 12
HEAD_DIM = 64
EPSILON = 1e-05
ROPE_BASE = 10000.0
MASKED_SCORE = -1e30
VMEM_LIMIT = 62 * 2**20
MESH = pl.DeviceIdType.MESH
BF16 = jnp.bfloat16
F32 = jnp.float32

NAMES = ("y", "xl", "xh", "z")
SIZES = {"y": 4, "xl": 2, "xh": 2, "z": 4, "c": 2}
ORDERS = (("y", "z", "x"), ("z", "x", "y"), ("x", "y", "z"))
ROWS = (208, 144, 224)
FULL = (1, 0, 2)
ATTN = {0: (0, 48), 1: (0, 48), 2: (0, 48)}
EARLY = {0: (48, 96), 1: (48, 96), 2: (48, 96)}
LATE = {0: (144, 64), 2: (144, 80)}
PARTS = (ATTN, EARLY, LATE)


def place():
    f = lax.axis_index("fsdp")
    s = lax.axis_index("seq")
    return {"x": (f // 8) * 2 + s % 2, "y": s // 2, "z": (f // 2) % 4, "c": f % 2}


def device(at):
    return ((at["x"] // 2) * 8 + at["z"] * 2 + at["c"], at["y"] * 2 + at["x"] % 2)


def shifted(at, axis, k):
    return {**at, axis: (at[axis] + k) % SIZES.get(axis, 4)}


def select(names, fixed, half=None):
    index = []
    for n in names:
        size = SIZES[n]
        if half is not None and n == half[0]:
            index.append(pl.ds(half[1] * (size // 2), size // 2))
        elif n in ("xl", "xh"):
            v = fixed.get("x")
            index.append(pl.ds(0, 2) if v is None else (v % 2 if n == "xl" else v // 2))
        else:
            v = fixed.get(n)
            index.append(pl.ds(0, size) if v is None else v)
    return tuple(index)


def expand(axes):
    return [n for a in axes for n in (("xl", "xh") if a == "x" else (a,))]


def kept(names, axes):
    some = expand(axes)
    return tuple(n for n in names if n in some)


def remote(src, dst, send, recv, to):
    return pltpu.make_async_remote_copy(
        src_ref=src, dst_ref=dst, send_sem=send, recv_sem=recv, device_id=to, device_id_type=MESH
    )


def greeting(at):
    f = lax.axis_index("fsdp")
    s = lax.axis_index("seq")
    bar = pltpu.get_barrier_semaphore()
    peers = [(f, (s + k) % 8) for k in range(1, 8)]
    peers += [(f + 1 - 2 * (f % 2), (s + k) % 8) for k in range(8)]
    peers += [device(shifted(at, "z", k)) for k in (1, 2, 3)]
    peers += [device({**at, "x": (at["x"] + 2) % 4})]
    peers += [device({**at, "x": (at["x"] // 2 * 2 + 2) % 4 + (1 - at["x"] % 2)})]
    for p in peers:
        pl.semaphore_signal(bar, inc=1, device_id=p, device_id_type=MESH)
    return bar, len(peers)


def one_hot(rows, slots, per, size, offset, flip=False):
    shape = (slots * size, rows) if flip else (rows, slots * size)
    i = lax.broadcasted_iota(jnp.int32, shape, 1 if flip else 0)
    j = lax.broadcasted_iota(jnp.int32, shape, 0 if flip else 1)
    return (j == (i // per) * size + offset + i % per).astype(BF16)


def units(core, up, flip=False):
    i = lax.broadcasted_iota(jnp.int32, (384, 384), 1 if flip else 0)
    j = lax.broadcasted_iota(jnp.int32, (384, 384), 0 if flip else 1)
    y, r = (i % 192) // 48, i % 48
    early = y * 32 + r + (128 if up else 0)
    late = y * 16 + r - 32 + (320 if up else 256)
    return ((i // 192 == core) & (j == jnp.where(r < 32, early, late))).astype(BF16)


def nn(a, b):
    return jnp.dot(a, b, preferred_element_type=F32)


def nt(a, b):
    return lax.dot_general(a, b, (((1,), (1,)), ((), ())), preferred_element_type=F32)


def tn(a, b):
    return lax.dot_general(a, b, (((0,), (0,)), ((), ())), preferred_element_type=F32)


def norm_factor(values):
    return lax.rsqrt(jnp.mean(values * values, axis=-1, keepdims=True) + EPSILON)


def norm_back(values, factor, e):
    return factor * e - values * (factor * factor * factor * jnp.mean(e * values, axis=-1, keepdims=True))


def swap_halves(v):
    lane = lax.broadcasted_iota(jnp.int32, v.shape, 1)
    return jnp.where(lane % 64 < 32, pltpu.roll(v, 96, 1), pltpu.roll(v, 32, 1))


def digits(names, n):
    out = {}
    for name in reversed(names):
        out[name] = n % SIZES[name]
        n = n // SIZES[name]
    return out


def full_index(names, fixed, free, n):
    got = digits(free, n)
    index = []
    for name in names:
        if name in free:
            index.append(got[name])
        elif name in ("xl", "xh"):
            index.append(fixed["x"] % 2 if name == "xl" else fixed["x"] // 2)
        else:
            index.append(fixed[name])
    return tuple(index)


def count(names):
    return math.prod(SIZES[n] for n in names)


def layer_kernel(
    lens, gains, tok, cot, w_query, w_key, w_value, w_out, w_gate, w_up, w_down,
    out_o, in_o, rows_o, down_o,
    a0, a1, a2, w0, w1, w2, g0, g1, g2, h0, h1, h2,
    xa, xat, r0, rd0, s0, d0, s0b, d0b, ks, vs, qs, ps, att, hid, dhid, dqs, cosine, sine, bias, rdn,
    v2s, cs, oacc, eacc, osum, esum, rdc, toks, out_s, in_s, lens_out, lens_in, *rest
):
    at = place()
    f = lax.axis_index("fsdp")
    s = lax.axis_index("seq")
    xl = at["x"] % 2
    here = at["y"] * 2 + at["c"]
    stays = at["c"] == xl
    partner = (f - at["c"] + xl, here)
    t3, t2, t1 = rest[:3], rest[3:6], rest[6:9]
    sem0s, sem0r, semds, semdr, semxs, semxr, sems, semr, semls, semlr, semcs, semcr, semps, sempr = rest[9:23]
    bem0s, bem0r, bemds, bemdr, bems, bemr, bemls, bemlr, bemcs, bemcr = rest[23:33]
    semms, semmr, semys, semyr, semzs, semzr, semws, semwr = rest[33:]
    attn_weights = (a0, a1, a2)
    weights = (w0, w1, w2)
    own_grads = (g0, g1, g2)
    homes = (h0, h1, h2)
    sibling = device(shifted(at, "c", 1))
    xl = at["x"] % 2
    beside = (f, at["y"] * 2 + 1 - xl)
    bar, others = greeting(at)
    row = lax.broadcasted_iota(jnp.int32, (6, 1), 0)

    def gain_column(which):
        col = jnp.zeros((6, 1), F32)
        for r in range(6):
            col = jnp.where(row == r, gains[which, r], col)
        return col

    gain_one, gain_two = gain_column(0), gain_column(1)
    for r in range(4):
        lens_out[r : r + 1] = jnp.full((1, 128), lens[0, r], jnp.int32).astype(F32)
    lens_out[4:8] = jnp.zeros((4, 128), F32)
    s0[...] = jnp.zeros_like(s0)
    d0[...] = jnp.zeros_like(d0)
    for b in range(8):
        lanes = pl.ds(b * 384, 384)
        half = pl.ds((b % 2) * 384, 384)
        s0[0, b, 0:6] = w_gate[:, lanes].astype(F32) * gain_two
        s0[1, b, 0:6] = w_up[:, lanes].astype(F32) * gain_two
        if b < 6:
            s0[2, b, 0:6] = (w_query, w_key, w_value)[b // 2][:, half].astype(F32) * gain_one
        else:
            s0[2, b, 0:6] = w_out[:, half].astype(F32)
    for b in range(2):
        d0[b, 0:24] = w_down[:, b * 384 : (b + 1) * 384].astype(F32)
    d0b[...] = d0[...].astype(BF16)
    gate_rows = s0[0].reshape(64, 384).astype(BF16)
    up_rows = s0[1].reshape(64, 384).astype(BF16)
    for core in range(2):
        rows = nn(gate_rows, units(core, False)) + nn(up_rows, units(core, True))
        s0b[core] = jnp.concatenate([rows.reshape(8, 8, 384), s0[2]], axis=1).astype(BF16)

    pl.semaphore_wait(bar, others)

    def group(k, src, dst, sends, recvs):
        me = at["c"] * 8 + s
        to, frm = (me + k) % 16, (me - k + 16) % 16
        peer = (f - at["c"] + to // 8, to % 8)
        send, recv = sends.at[k - 1], recvs.at[k - 1]
        out = remote(src.at[to // 8, to % 8], dst.at[me], send, recv, peer)
        inn = remote(src.at[to // 8, to % 8], dst.at[frm], send, recv, peer)
        return out, inn

    def first(k):
        return group(k, s0b, r0, sem0s, sem0r)

    def swap(buf, n):
        c = at["c"]
        return remote(buf.at[c], buf.at[c], semps.at[n], sempr.at[n], sibling)

    def swapped(buf, n):
        c = at["c"]
        return remote(buf.at[c], buf.at[1 - c], semps.at[n], sempr.at[n], sibling)

    def down_copy(slot):
        return remote(d0b.at[1 - xl], rd0.at[slot], semds, semdr, beside)

    def moves(n):
        src = (tok, cot, lens_out)[n]
        dst = (toks, cs.at[xl], lens_in)[n]
        return remote(src, dst, semms.at[n], semmr.at[n], partner)

    def token_out(y):
        return remote(xa.at[here], xa.at[here], semxs.at[y], semxr.at[at["y"]], (f, y * 2 + xl))

    def token_in(y):
        block = xa.at[y * 2 + at["c"]]
        return remote(block, block, semxs.at[y], semxr.at[y], (f, y * 2 + xl))

    def token_across(y):
        mine, other = xa.at[y * 2 + at["c"]], xa.at[y * 2 + 1 - at["c"]]
        send, recv = semys.at[y], semyr.at[y]
        return remote(mine, mine, send, recv, sibling), remote(other, other, send, recv, sibling)

    for k in range(1, 16):
        first(k)[0].start()
    down_copy(xl).start()

    def move():
        for n in (0, 2, 1):
            moves(n).start()
        for n in range(3):
            moves(n).wait()

    def stay():
        toks[...] = tok[...]
        cs[xl] = cot[...]
        lens_in[...] = lens_out[...]

    pl.when(jnp.logical_not(stays))(move)
    pl.when(stays)(stay)
    swap(cs, 0).start()
    inputs = toks[...].astype(F32)
    xa[here] = (inputs * norm_factor(inputs)).astype(BF16)
    for y in range(1, 4):
        pl.when(y > at["y"])(lambda y=y: token_out(y).start())
    pl.when(at["c"] == 0)(lambda: token_across(at["y"])[0].start())
    r0[at["c"] * 8 + s] = s0b[at["c"], s]
    rd0[xl] = d0b[xl]

    def rest(i, part):
        return pl.ds(0, 48) if part == 0 else pl.ds(48, ROWS[i] - 48)

    def block(i, fixed, core, rows):
        where = select(NAMES, fixed)
        if rows.start < 48:
            return attn_weights[i].at[where + (core,)]
        return weights[i].at[where + (pl.ds(rows.start - 48, rows.size),)]

    def put(i, first_row, value):
        where = select(NAMES, at)
        if first_row < 48:
            attn_weights[i][where + (at["c"],)] = value
        else:
            weights[i][where + (slice(first_row - 48, first_row - 48 + value.shape[0]),)] = value

    def ring(i, part, phase, k):
        order = ORDERS[i]
        axis = order[phase]
        fixed = {n: at[n] for n in ("x", "y", "z") if n not in order[:phase]}
        theirs = {**fixed, axis: (at[axis] - k + 4) % 4}
        mine, other = block(i, fixed, at["c"], rest(i, part)), block(i, theirs, at["c"], rest(i, part))
        slot = 2 * part + phase
        send, recv = sems.at[i, slot, k - 1], semr.at[i, slot, k - 1]
        to = device(shifted(at, axis, k))
        return remote(mine, mine, send, recv, to), remote(other, other, send, recv, to)

    def direct(i, part, k):
        axis = ORDERS[i][2]
        rows = pl.ds(*PARTS[part][i])
        mine = block(i, {axis: at[axis]}, at["c"], rows)
        other = block(i, {axis: (at[axis] - k + 4) % 4}, at["c"], rows)
        send, recv = semls.at[i, part, k - 1], semlr.at[i, part, k - 1]
        to = device(shifted(at, axis, k))
        return remote(mine, mine, send, recv, to), remote(other, other, send, recv, to)

    def across(i, k):
        axis = ORDERS[i][2]
        where = {axis: (at[axis] + k) % 4}
        mine, other = block(i, where, at["c"], rest(i, 0)), block(i, where, 1 - at["c"], rest(i, 0))
        send, recv = semcs.at[i, k], semcr.at[i, k]
        return remote(mine, mine, send, recv, sibling), remote(other, other, send, recv, sibling)

    def start(part, phase):
        for k in (1, 3, 2):
            for i in FULL:
                ring(i, part, phase, k)[0].start()

    def arrive(part, phase):
        for k in (1, 3, 2):
            for i in FULL:
                ring(i, part, phase, k)[1].wait_recv()

    def start_last(part):
        for k in (1, 3, 2):
            for i in PARTS[part]:
                direct(i, part, k)[0].start()

    def arrive_last(part):
        for k in (1, 3, 2):
            for i in PARTS[part]:
                direct(i, part, k)[1].wait_recv()
                if part == 0:
                    across(i, (4 - k) % 4)[0].start()

    def sent(part):
        for i in PARTS[part]:
            for k in (1, 2, 3):
                direct(i, part, k)[0].wait_send()

    for k in range(1, 16):
        first(k)[1].wait_recv()
    flat = r0[...].reshape(256, 384)
    piece = nn(one_hot(48, 16, 6, 16, at["c"] * 128 + 8), flat).astype(BF16)
    for i in range(3):
        put(i, 0, piece[:, i * 128 : (i + 1) * 128])
    start(0, 0)
    piece = nn(one_hot(96, 16, 6, 16, 0), flat).astype(BF16)
    put(0, 48, piece[:, :128])
    put(0, 144, piece[:64, 256:])
    put(1, 48, piece[:, 128:256])
    put(2, 192, piece[64:, 256:])
    down_copy(1 - xl).wait_recv()
    piece = nn(one_hot(48, 2, 24, 32, 0), rd0[...].reshape(64, 384)).astype(BF16)
    for b in range(3):
        lanes = slice(b * 128, (b + 1) * 128)
        put(2, 48 + 32 * b, piece[:32, lanes])
        put(2, 144 + 16 * b, piece[32:, lanes])
    start(1, 0)
    arrive(0, 0)
    start(0, 1)
    arrive(0, 1)
    start_last(0)
    for i in ATTN:
        across(i, 0)[0].start()
    arrive(1, 0)
    start(1, 1)

    ends = [lens_in[0:1, :]]
    for r in (1, 2):
        ends.append(ends[-1] + lens_in[r : r + 1, :])
    freq_lane = (lax.broadcasted_iota(jnp.int32, (1, 128), 1) % 32).astype(F32)
    freqs = jnp.exp(freq_lane * (-2.0 * math.log(ROPE_BASE) / HEAD_DIM))
    lane = lax.broadcasted_iota(jnp.int32, (128, 128), 1)

    def segment_of(index):
        return sum(jnp.where(index >= e, 1.0, 0.0) for e in ends)

    def table(u, carry):
        index = (u * 128 + lax.broadcasted_iota(jnp.int32, (128, 128), 0)).astype(F32)
        begin = jnp.zeros_like(index)
        for e in ends:
            begin = jnp.where(index >= e, e, begin)
        angle = (index - begin) * freqs
        rows = pl.ds(pl.multiple_of(u * 128, 128), 128)
        cosine[rows, :] = jnp.cos(angle)
        sine[rows, :] = jnp.where(lane % 64 < 32, -1.0, 1.0) * jnp.sin(angle)
        mine = (here * 128 + lax.broadcasted_iota(jnp.int32, (1, 128), 1)).astype(F32)
        allowed = (segment_of(index) == segment_of(mine)) & (index <= mine)
        bias[rows, :] = jnp.where(allowed, 0.0, MASKED_SCORE)
        return carry

    lax.fori_loop(0, 8, table, 0)

    arrive(1, 1)
    start_last(1)
    for u in range(1, 8):

        def clear(u=u):
            xa[u] = jnp.zeros((128, 768), BF16)

        pl.when(u > here)(clear)
    for y in range(3):

        def pass_on(y=y):
            token_in(y).wait_recv()
            token_across(y)[0].start()

        pl.when(y < at["y"])(pass_on)
    for y in range(3):
        pl.when(y < at["y"])(lambda y=y: token_across(y)[1].wait_recv())
    pl.when(at["c"] == 1)(lambda: token_across(at["y"])[1].wait_recv())

    def transpose_tokens(u, carry):
        xat[:, pl.ds(pl.multiple_of(u * 128, 128), 128)] = xa[u].T
        return carry

    lax.fori_loop(0, 8, transpose_tokens, 0)
    arrive_last(0)
    for k in range(4):
        for i in ATTN:
            across(i, k)[1].wait_recv()

    for k in range(1, 16):
        first(k)[0].wait_send()
    down_copy(xl).wait_send()
    for y in range(1, 4):
        pl.when(y > at["y"])(lambda y=y: token_out(y).wait_send())
    for y in range(3):
        pl.when(y < at["y"])(lambda y=y: token_across(y)[0].wait_send())
    pl.when(at["c"] == 0)(lambda: token_across(at["y"])[0].wait_send())

    mine = pl.ds(pl.multiple_of(here * 128, 128), 128)
    cos_mine, sin_mine = cosine[mine, :], sine[mine, :]
    left = lax.broadcasted_iota(jnp.int32, (128, 128), 1) < 64

    def attn_weight(kind, t, h):
        return attn_weights[t][kind, h].reshape(768, 128)

    def put_grad(kind, t, h, value):
        own_grads[t][kind, h] = value.reshape(2, 4, 2, 48, 128)

    def attn_full(kind):
        return jnp.concatenate([attn_weight(kind, p % 3, p // 3) for p in range(6)], axis=1)

    def stacked(v):
        zero = jnp.zeros_like(v)
        return jnp.concatenate([jnp.where(left, v, zero), jnp.where(left, zero, v)], axis=0)

    def unstacked(v):
        return jnp.concatenate([v[:64, :128], v[64:, 128:]], axis=0).T

    def pair_lanes(p):
        return pl.ds(pl.multiple_of(p * 128, 128), 128)

    def attend(t, h):
        p = t + 3 * h
        tokens_all = xa[...].reshape(1024, 768)
        w_kv = jnp.concatenate([attn_weight(1, t, h), attn_weight(2, t, h)], axis=1)
        kv = nn(tokens_all, w_kv)
        k_raw = kv[:, :128]
        k = (k_raw * cosine[...] + swap_halves(k_raw) * sine[...]).astype(BF16)
        v = kv[:, 128:].astype(BF16)
        q_raw = nn(xa[here], attn_weight(0, t, h))
        q = ((q_raw * cos_mine + swap_halves(q_raw) * sin_mine).astype(BF16) * (1.0 / math.sqrt(HEAD_DIM))).astype(BF16)
        qq = stacked(q)
        ks[p] = k
        vs[p] = v
        qs[p] = qq
        masks = bias[...]
        scores = nt(k, qq) + jnp.concatenate([masks, masks], axis=1)
        top = jnp.max(scores, axis=0, keepdims=True)
        e = jnp.exp(scores - top)
        total = jnp.sum(e, axis=0, keepdims=True)
        probs = (e * (1.0 / total)).astype(BF16)
        ps[p] = probs
        att[:, pair_lanes(p)] = unstacked(tn(v, probs)).astype(BF16)

    for t in range(3):

        def attend_third(h, carry, t=t):
            attend(t, h)
            return carry

        lax.fori_loop(0, 2, attend_third, 0)
        if t == 0:
            start_last(2)


    hidden = toks[...].astype(F32) + nn(att[...], attn_full(3))
    hid[...] = hidden
    factor_two = norm_factor(hidden)
    v2s[at["c"]] = (hidden * factor_two).astype(BF16)
    swap(v2s, 1).start()
    oacc[...] = jnp.zeros_like(oacc)
    eacc[...] = jnp.zeros_like(eacc)
    swapped(cs, 0).wait()
    swapped(v2s, 1).wait()
    v2 = v2s[...].reshape(256, 768)
    v2t = v2.T

    def pair(a, b):
        return jnp.concatenate([a, b], axis=1)

    def gated(gate, up, d_w):
        c = cs[...].reshape(256, 768)
        sig = 1.0 / (1.0 + jnp.exp(-gate))
        silu = gate * sig
        mixed = (silu * up).astype(BF16)
        oacc[...] += nn(mixed, d_w).reshape(2, 128, 768)
        d_mixed = nt(c, d_w)
        d_gate = d_mixed * up * sig * (1.0 + gate * (1.0 - sig))
        d_up = d_mixed * silu
        return d_gate, d_up, tn(mixed, c).astype(BF16)

    def down_rows(xh, z, first_row, rows):
        def part(b, h, n):
            some = pl.ds(first_row - 48 + n * rows, rows)
            return w2[:, h, xh, z + b, some].reshape(4 * rows, 128)

        return jnp.concatenate(
            [jnp.concatenate([part(b, h, n) for h in range(2) for n in range(3)], axis=1) for b in range(2)], axis=0
        )

    def put_down(xh, z, first_row, rows, g):
        for b in range(2):
            for h in range(2):
                for n in range(3):
                    some = pl.ds(first_row + n * rows, rows)
                    lanes = slice(h * 384 + n * 128, h * 384 + (n + 1) * 128)
                    h2[:, h, xh, z + b, some] = g[b * 4 * rows : (b + 1) * 4 * rows, lanes].reshape(4, rows, 128)

    def feed_early(y, carry):
        g_w = pair(*(w0[y, b, :, :, 0:96].reshape(768, 128) for b in range(2)))
        u_w = pair(*(w1[y, b].reshape(768, 128) for b in range(2)))
        xh, z = y // 2, (y % 2) * 2
        d_w = down_rows(xh, z, 48, 32)
        d_gate, d_up, g_d = gated(nn(v2, g_w), nn(v2, u_w), d_w)
        d_gate, d_up = d_gate.astype(BF16), d_up.astype(BF16)
        eacc[...] += (nt(d_gate, g_w) + nt(d_up, u_w)).reshape(2, 128, 768)
        g_g = nn(v2t, d_gate).astype(BF16)
        g_u = nn(v2t, d_up).astype(BF16)
        for b in range(2):
            lanes = slice(b * 128, (b + 1) * 128)
            h0[y, b, :, :, 48:144] = g_g[:, lanes].reshape(2, 4, 96, 128)
            h1[y, b, :, :, 48:144] = g_u[:, lanes].reshape(2, 4, 96, 128)
        put_down(xh, z, 48, 32, g_d)
        return carry

    def feed_late(y, carry):
        def weight(b):
            low_rows, high_rows = w0[y, b, :, :, 96:160], w2[y, b, :, :, 144:176]
            return jnp.concatenate([low_rows, high_rows], axis=2).reshape(768, 128)

        w = pair(weight(0), weight(1))
        xh, z = y // 2, (y % 2) * 2
        d_w = down_rows(xh, z, 144, 16)
        both = nn(v2, w)
        low = lax.broadcasted_iota(jnp.int32, (256, 128), 1) < 64

        def mix(a, b):
            return jnp.where(low, a, pltpu.roll(b, 64, 1)), jnp.where(low, pltpu.roll(a, 64, 1), b)

        gate, up = mix(both[:, :128], both[:, 128:])
        d_gate, d_up, g_d = gated(gate, up, d_w)
        d_both = pair(*mix(d_gate, d_up)).astype(BF16)
        eacc[...] += nt(d_both, w).reshape(2, 128, 768)
        g = nn(v2t, d_both).astype(BF16)
        for b in range(2):
            rows = g[:, b * 128 : (b + 1) * 128].reshape(2, 4, 96, 128)
            h0[y, b, :, :, 144:208] = rows[:, :, :64]
            h2[y, b, :, :, 192:224] = rows[:, :, 64:]
        put_down(xh, z, 144, 16, g_d)
        return carry

    def home(i, fixed, part=None, half=None):
        first_row, rows = (0, ROWS[i]) if part is None else PARTS[part][i]
        return homes[i].at[select(NAMES, fixed, half) + (pl.ds(first_row, rows),)]

    def share(i, k):
        where = {ORDERS[i][2]: (at[ORDERS[i][2]] + k) % 4}
        part = own_grads[i].at[select(NAMES, where) + (1 - at["c"],)]
        return remote(part, home(i, where, 0), bemcs.at[i, k], bemcr.at[i, k], sibling)

    def add_core(i, k):
        order = ORDERS[i]
        free = kept(NAMES, order[:2])
        fixed = {order[2]: (at[order[2]] + k) % 4}
        rows = pl.ds(*ATTN[i])

        def body(n, carry):
            index = full_index(NAMES, fixed, free, n)
            total = homes[i][index + (rows,)].astype(F32) + own_grads[i][index + (at["c"],)].astype(F32)
            homes[i][index + (rows,)] = total.astype(BF16)
            return carry

        lax.fori_loop(0, count(free), body, 0, unroll=4)

    def split(i):
        return "z" if ORDERS[i][2] == "y" else "y"

    def halfway(i, part, way):
        axis = ORDERS[i][2]
        half = (split(i), way)
        src = home(i, {axis: (at[axis] + 2) % 4}, part, half)
        dst = t3[i].at[(1,) + select(kept(NAMES, ORDERS[i][:2]), {}, half) + (pl.ds(*PARTS[part][i]),)]
        send, recv = bemls.at[i, part, way], bemlr.at[i, part, way]
        return remote(src, dst, send, recv, device(shifted(at, axis, (1, 3)[way])))

    def whole(i, part, way):
        axis = ORDERS[i][2]
        src = home(i, {axis: (at[axis] + (1, 3)[way]) % 4}, part)
        dst = t3[i].at[2 * way, :, :, :, pl.ds(*PARTS[part][i])] if ORDERS[i][2] != "x" else t3[i].at[
            2 * way, :, :, pl.ds(*PARTS[part][i])
        ]
        send, recv = bemls.at[i, part, 2 + way], bemlr.at[i, part, 2 + way]
        return remote(src, dst, send, recv, device(shifted(at, axis, (1, 3)[way])))

    def add_half(i, part, way):
        order = ORDERS[i]
        where = split(i)
        free = kept(NAMES, order[:2])
        turned = (where,) + tuple(m for m in free if m != where)
        fixed = {order[2]: (at[order[2]] + (1, 3)[way]) % 4}
        rows = pl.ds(*PARTS[part][i])

        def body(n, carry):
            got = digits(turned, n)
            got[where] = got[where] + way * (SIZES[where] // 2)
            n = 0
            for m in free:
                n = n * SIZES[m] + got[m]
            index = full_index(NAMES, fixed, free, n) + (rows,)
            came = t3[i][(1,) + tuple(got[m] for m in free) + (rows,)]
            homes[i][index] = (homes[i][index].astype(F32) + came.astype(F32)).astype(BF16)
            return carry

        lax.fori_loop(0, count(free) // 2, body, 0, unroll=4)

    def add_whole(i, part):
        order = ORDERS[i]
        free = kept(NAMES, order[:2])
        fixed = {order[2]: at[order[2]]}
        rows = pl.ds(*PARTS[part][i])

        def body(n, carry):
            index = full_index(NAMES, fixed, free, n) + (rows,)
            there = full_index(free, {}, free, n) + (rows,)
            total = homes[i][index].astype(F32) + t3[i][(0,) + there].astype(F32) + t3[i][(2,) + there].astype(F32)
            homes[i][index] = total.astype(BF16)
            return carry

        lax.fori_loop(0, count(free), body, 0, unroll=4)

    def hop(i, part, left, k):
        order = ORDERS[i]
        axis = order[left - 1]
        fixed = {a: at[a] for a in order[left:]}
        rows = rest(i, part)
        src = homes[i].at[select(NAMES, {**fixed, axis: (at[axis] + k) % 4}) + (rows,)]
        if left == 1:
            dst = t1[i].at[k - 1, rows]
        else:
            dst = t2[i].at[(k - 1,) + select(kept(NAMES, order[:1]), {}) + (rows,)]
        slot = 2 * part + left - 1
        send, recv = bems.at[i, slot, k - 1], bemr.at[i, slot, k - 1]
        return remote(src, dst, send, recv, device(shifted(at, axis, k)))

    def add_ring(i, part):
        order = ORDERS[i]
        free = kept(NAMES, order[:1])
        fixed = {a: at[a] for a in order[1:]}
        rows = rest(i, part)

        def body(n, carry):
            index = full_index(NAMES, fixed, free, n) + (rows,)
            total = homes[i][index].astype(F32)
            for k in range(3):
                total = total + t2[i][(k,) + full_index(free, {}, free, n) + (rows,)].astype(F32)
            homes[i][index] = total.astype(BF16)
            return carry

        lax.fori_loop(0, count(free), body, 0)

    def hop_start(part):
        for k in (1, 3, 2):
            for i in FULL:
                hop(i, part, 2, k).start()

    def hop_on(part):
        for i in FULL:
            for k in (1, 3, 2):
                hop(i, part, 2, k).wait_recv()
            add_ring(i, part)
            for k in (1, 3, 2):
                hop(i, part, 1, k).start()

    def last(i, part):
        for k in (1, 3, 2):
            hop(i, part, 1, k).wait_recv()
        rows = rest(i, part)
        total = homes[i][select(NAMES, at) + (rows,)].astype(F32)
        for k in range(3):
            total = total + t1[i][k, rows].astype(F32)
        return total.astype(BF16)

    def half_start(part, items=FULL):
        for way in range(2):
            for i in items:
                if i in PARTS[part]:
                    halfway(i, part, way).start()

    def half_on(part, items=FULL):
        for way in range(2):
            for i in items:
                if i in PARTS[part]:
                    halfway(i, part, way).wait_recv()
                    add_half(i, part, way)
                    whole(i, part, way).start()

    def whole_on(part):
        for i in PARTS[part]:
            for way in range(2):
                whole(i, part, way).wait_recv()
            add_whole(i, part)

    for i in FULL:
        for part in range(2):
            if i in FULL:
                for phase in range(2):
                    for k in (1, 2, 3):
                        ring(i, part, phase, k)[0].wait_send()
    arrive_last(1)
    lax.fori_loop(0, 4, feed_early, 0)
    half_start(1)
    arrive_last(2)
    lax.fori_loop(0, 4, feed_late, 0)
    sum_o = remote(oacc.at[1 - at["c"]], osum, semps.at[2], sempr.at[2], sibling)
    sum_e = remote(eacc.at[1 - at["c"]], esum, semps.at[3], sempr.at[3], sibling)
    sum_e.start()
    sum_o.start()
    half_start(2)
    half_on(1)
    sum_e.wait()

    hidden = hid[...]
    factor_two = norm_factor(hidden)
    d_hidden = cs[at["c"]].astype(F32) + norm_back(hidden, factor_two, eacc[at["c"]] + esum[...])
    dhid[...] = d_hidden
    dh = d_hidden.astype(BF16)
    d_att = nt(dh, attn_full(3)).astype(BF16)
    att_t = att[...].T
    for j in range(2):
        g_o = nn(att_t, dh[:, j * 384 : (j + 1) * 384]).astype(BF16)
        for t in range(3):
            put_grad(3, t, j, g_o[:, t * 128 : (t + 1) * 128])
    att[...] = d_att

    def attend_back(t, h):
        p = t + 3 * h
        da = stacked(att[:, pair_lanes(p)])
        k, v, qq, probs = ks[p], vs[p], qs[p], ps[p]
        d_probs = nt(v, da)
        probs_f = probs.astype(F32)
        d_sum = jnp.sum(probs_f * d_probs, axis=0, keepdims=True)
        d_scores = (probs_f * (d_probs - d_sum)).astype(BF16)
        d_v = nn(probs, da).astype(BF16)
        d_k = nn(d_scores, qq)
        d_k = (d_k * cosine[...] - swap_halves(d_k) * sine[...]).astype(BF16)
        d_q = unstacked(tn(k, d_scores)) * (1.0 / math.sqrt(HEAD_DIM))
        d_q = (d_q * cos_mine - swap_halves(d_q) * sin_mine).astype(BF16)
        ks[p] = d_k
        vs[p] = d_v
        dqs[:, pair_lanes(p)] = d_q
        g_kv = nn(xat[...], jnp.concatenate([d_k, d_v], axis=1)).astype(BF16)
        g_q = nn(xat[:, mine], d_q).astype(BF16)
        put_grad(0, t, h, g_q)
        put_grad(1, t, h, g_kv[:, :128])
        put_grad(2, t, h, g_kv[:, 128:])

    def share_on(i):
        for k in (2, 1, 3, 0):
            share(i, k).wait_recv()
            add_core(i, k)
            if k == 2:
                half_start(0, (i,))

    half_on(2)
    def third_back(h, carry):
        attend_back(0, h)
        return carry

    lax.fori_loop(0, 2, third_back, 0)

    def share_start(i):
        for k in (2, 1, 3, 0):
            share(i, k).start()

    share_start(0)
    attend_back(1, 0)
    share_on(0)
    attend_back(1, 1)
    share_start(1)
    half_on(0, (0,))
    attend_back(2, 0)
    share_on(1)
    attend_back(2, 1)
    share_start(2)
    whole_on(1)
    half_on(0, (1,))
    share_on(2)
    whole_on(2)
    hop_start(1)

    w_kv = jnp.concatenate([attn_full(1), attn_full(2)], axis=1)

    def tokens_back(u, carry):
        rows = pl.ds(pl.multiple_of(u * 128, 128), 128)
        d_kv = jnp.concatenate([ks[p, rows, :] for p in range(6)] + [vs[p, rows, :] for p in range(6)], axis=1)
        xa[u] = nt(d_kv, w_kv).astype(BF16)
        return carry

    lax.fori_loop(0, 8, tokens_back, 0)

    def grad_across(y):
        mine = xa.at[y * 2 + 1 - at["c"]]
        return remote(mine, rdc.at[y], semzs.at[y], semzr.at[y], sibling)

    def grad_out(y):
        return remote(xa.at[y * 2 + at["c"]], rdn.at[at["y"]], semws.at[y], semwr.at[at["y"]], (f, y * 2 + xl))

    def grad_in(y):
        return remote(xa.at[y * 2 + at["c"]], rdn.at[y], semws.at[y], semwr.at[y], (f, y * 2 + xl))

    for y in range(3):
        pl.when(y < at["y"])(lambda y=y: grad_across(y).start())
    pl.when(at["c"] == 1)(lambda: grad_across(at["y"]).start())
    for y in range(3):

        def add_across(y=y):
            grad_across(y).wait_recv()
            block = xa[y * 2 + at["c"]].astype(F32) + rdc[y].astype(F32)
            xa[y * 2 + at["c"]] = block.astype(BF16)
            grad_out(y).start()

        pl.when(y < at["y"])(add_across)
    half_on(0, (2,))
    sum_o.wait()
    out_s[...] = (hid[...] + oacc[at["c"]] + osum[...]).astype(BF16)

    def out_move():
        return remote(out_s, out_o, semms.at[3], semmr.at[3], partner)

    def out_stay():
        out_o[...] = out_s[...]

    pl.when(jnp.logical_not(stays))(lambda: out_move().start())
    pl.when(stays)(out_stay)
    esum[...] = nt(dqs[...], attn_full(0))

    hop_on(1)
    whole_on(0)
    hop_start(0)
    sum0, sum1, sum2 = last(0, 1), last(1, 1), last(2, 1)
    down = jnp.concatenate(
        [
            jnp.concatenate([sum2[a + b * n : a + b * (n + 1)] for n in range(3)], axis=1)
            for a, b in ((0, 32), (96, 16))
        ],
        axis=0,
    )
    mixed_units = jnp.concatenate([sum0[96:160], sum2[144:176]], axis=0)
    both = jnp.concatenate([sum0[0:96], sum1[0:96], mixed_units], axis=1)
    rows_mlp = nn(one_hot(96, 16, 6, 16, 0, True), both)
    d0b[...] = nn(one_hot(48, 2, 24, 32, 0, True), down).astype(BF16).reshape(2, 32, 384)
    hop_on(0)

    esum[...] += xa[here].astype(F32)

    def add_own():
        grad_across(at["y"]).wait_recv()
        esum[...] += rdc[at["y"]].astype(F32)

    pl.when(at["c"] == 0)(add_own)
    for y in range(1, 4):

        def add(y=y):
            grad_in(y).wait_recv()
            esum[...] += rdn[y].astype(F32)

        pl.when(y > at["y"])(add)
    inputs = toks[...].astype(F32)
    in_s[...] = dhid[...] + norm_back(inputs, norm_factor(inputs), esum[...])

    def in_move():
        return remote(in_s, in_o, semms.at[4], semmr.at[4], partner)

    def in_stay():
        in_o[...] = in_s[...]

    pl.when(jnp.logical_not(stays))(lambda: in_move().start())
    pl.when(stays)(in_stay)
    attn = jnp.concatenate([last(i, 0) for i in range(3)], axis=1)
    rows = rows_mlp + nn(one_hot(48, 16, 6, 16, at["c"] * 128 + 8, True), attn)
    s0b[...] = rows.astype(BF16).reshape(2, 8, 16, 384)

    def final(k):
        return group(k, s0b, r0, bem0s, bem0r)

    def final_down(slot):
        return remote(d0b.at[1 - xl], rd0.at[slot], bemds, bemdr, beside)

    for k in range(1, 16):
        final(k)[0].start()
    final_down(xl).start()
    r0[at["c"] * 8 + s] = s0b[at["c"], s]
    rd0[xl] = d0b[xl]
    for k in range(1, 16):
        final(k)[1].wait_recv()
    final_down(1 - xl).wait_recv()

    rows_o[...] = r0[...]
    down_o[...] = rd0[...]
    for k in range(1, 16):
        final(k)[0].wait_send()
    final_down(xl).wait_send()
    for y in range(3):

        def across_sent(y=y):
            grad_across(y).wait_send()
            grad_out(y).wait_send()

        pl.when(y < at["y"])(across_sent)
    pl.when(at["c"] == 1)(lambda: grad_across(at["y"]).wait_send())

    def moved():
        out_move().wait()
        in_move().wait()

    pl.when(jnp.logical_not(stays))(moved)
    for part in range(3):
        sent(part)
    for i in ATTN:
        for k in range(4):
            across(i, k)[0].wait_send()
            share(i, k).wait_send()
    for part in range(3):
        for i in PARTS[part]:
            for way in range(2):
                halfway(i, part, way).wait_send()
                whole(i, part, way).wait_send()
    for part in range(2):
        for i in FULL:
            for left in (2, 1):
                for k in (1, 2, 3):
                    hop(i, part, left, k).wait_send()


def finish_kernel(gains, w_query, w_key, w_value, w_gate, w_up, rows_i, down_i, out_i, in_i,
                  out_o, in_o, ga1_o, gq_o, gk_o, gv_o, go_o, ga2_o, gg_o, gu_o, gd_o, s0):
    out_o[...] = out_i[...]
    in_o[...] = in_i[...]
    row = lax.broadcasted_iota(jnp.int32, (6, 1), 0)

    def gain_column(which):
        col = jnp.zeros((6, 1), F32)
        for r in range(6):
            col = jnp.where(row == r, gains[which, r], col)
        return col

    def as_row(col):
        lane = lax.broadcasted_iota(jnp.int32, (6, 6), 1)
        side = lax.broadcasted_iota(jnp.int32, (6, 6), 0)
        return jnp.sum(jnp.where(lane == side, col, 0.0), axis=0, keepdims=True)

    gain_one, gain_two = gain_column(0), gain_column(1)
    c = lax.axis_index("fsdp") % 2
    got = rows_i[...].reshape(2, 8, 16, 384)
    halves = [got[core, :, :8].reshape(64, 384) for core in range(2)]
    for which in range(2):
        natural = nn(halves[0], units(0, which == 1, True)) + nn(halves[1], units(1, which == 1, True))
        s0[which] = natural.reshape(8, 8, 384)
    s0[2] = rows_i[pl.ds(c * 8, 8), 8:, :].astype(F32)
    down = down_i[...].astype(F32)
    gain_sum_one = jnp.zeros((6, 1), F32)
    gain_sum_two = jnp.zeros((6, 1), F32)
    for b in range(8):
        lanes = pl.ds(b * 384, 384)
        half = pl.ds((b % 2) * 384, 384)
        h_gate, h_up, h_attn = s0[0, b, 0:6], s0[1, b, 0:6], s0[2, b, 0:6]
        gg_o[:, lanes] = h_gate * gain_two
        gu_o[:, lanes] = h_up * gain_two
        gain_sum_two += jnp.sum(h_gate * w_gate[:, lanes].astype(F32), axis=1, keepdims=True)
        gain_sum_two += jnp.sum(h_up * w_up[:, lanes].astype(F32), axis=1, keepdims=True)
        if b < 6:
            (gq_o, gk_o, gv_o)[b // 2][:, half] = h_attn * gain_one
            raw = (w_query, w_key, w_value)[b // 2][:, half].astype(F32)
            gain_sum_one += jnp.sum(h_attn * raw, axis=1, keepdims=True)
        else:
            go_o[:, half] = h_attn
    for b in range(2):
        gd_o[:, b * 384 : (b + 1) * 384] = down[b, 0:24]
    ga1_o[...] = as_row(gain_sum_one)
    ga2_o[...] = as_row(gain_sum_two)


VMEM_SPEC = pl.BlockSpec(memory_space=pltpu.VMEM)
SMEM_SPEC = pl.BlockSpec(memory_space=pltpu.SMEM)
DMA = pltpu.SemaphoreType.DMA


def layer(lens, gains, *arrays):
    outs = [((128, 768), BF16), ((128, 768), F32), ((16, 16, 384), BF16), ((2, 32, 384), BF16)]
    sizes = tuple(SIZES[n] for n in NAMES)
    scratch = [(sizes + (2, 48, 128), BF16) for _ in ROWS] + [(sizes + (r - 48, 128), BF16) for r in ROWS]
    scratch += [(sizes + (2, 48, 128), BF16) for _ in ROWS]
    scratch += [(sizes + (r, 128), BF16) for r in ROWS]
    scratch += [
        ((8, 128, 768), BF16), ((768, 1024), BF16), ((16, 16, 384), BF16), ((2, 32, 384), BF16),
        ((3, 8, 8, 384), F32), ((2, 32, 384), F32), ((2, 8, 16, 384), BF16), ((2, 32, 384), BF16),
        ((6, 1024, 128), BF16), ((6, 1024, 128), BF16), ((6, 256, 128), BF16), ((6, 1024, 256), BF16),
        ((128, 768), BF16), ((128, 768), F32), ((128, 768), F32), ((128, 768), BF16),
        ((1024, 128), F32), ((1024, 128), F32), ((1024, 128), F32), ((4, 128, 768), BF16),
        ((2, 128, 768), BF16), ((2, 128, 768), BF16), ((2, 128, 768), F32), ((2, 128, 768), F32),
        ((128, 768), F32), ((128, 768), F32), ((4, 128, 768), BF16), ((128, 768), BF16), ((128, 768), BF16), ((128, 768), F32),
        ((8, 128), F32), ((8, 128), F32),
    ]
    for rings in (2, 1, 0):
        for i in range(3):
            left = tuple(SIZES[n] for n in kept(NAMES, ORDERS[i][:rings]))
            scratch.append(((3,) + left + (ROWS[i], 128), BF16))
    copies = [
        DMA((15,)), DMA((15,)), DMA, DMA, DMA((4,)), DMA((4,)),
        DMA((3, 4, 3)), DMA((3, 4, 3)), DMA((3, 3, 4)), DMA((3, 3, 4)), DMA((3, 4)), DMA((3, 4)), DMA((4,)), DMA((4,)),
        DMA((15,)), DMA((15,)), DMA, DMA,
        DMA((3, 4, 3)), DMA((3, 4, 3)), DMA((3, 3, 4)), DMA((3, 3, 4)), DMA((3, 4)), DMA((3, 4)),
        DMA((5,)), DMA((5,)), DMA((4,)), DMA((4,)), DMA((4,)), DMA((4,)), DMA((4,)), DMA((4,)),
    ]
    return pl.pallas_call(
        layer_kernel,
        out_shape=[jax.ShapeDtypeStruct(shape, kind) for shape, kind in outs],
        in_specs=[SMEM_SPEC] * 2 + [VMEM_SPEC] * 9,
        out_specs=[VMEM_SPEC] * len(outs),
        scratch_shapes=[pltpu.VMEM(shape, kind) for shape, kind in scratch] + copies,
        compiler_params=pltpu.CompilerParams(collective_id=0, has_side_effects=True, vmem_limit_bytes=VMEM_LIMIT),
        name="layer",
    )(lens, gains, *arrays)


def finish(gains, *arrays):
    outs = [
        ((128, 768), BF16), ((128, 768), F32), ((1, 6), F32),
        ((6, 768), F32), ((6, 768), F32), ((6, 768), F32), ((6, 768), F32),
        ((1, 6), F32), ((6, 3072), F32), ((6, 3072), F32), ((24, 768), F32),
    ]
    return pl.pallas_call(
        finish_kernel,
        out_shape=[jax.ShapeDtypeStruct(shape, kind) for shape, kind in outs],
        in_specs=[SMEM_SPEC] + [VMEM_SPEC] * 9,
        out_specs=[VMEM_SPEC] * len(outs),
        scratch_shapes=[pltpu.VMEM((3, 8, 8, 384), F32)],
        name="finish",
    )(gains, *arrays)


def per_device(tokens, doc_lengths, attn_gain, w_query, w_key, w_value, w_out, mlp_gain, w_gate, w_up, w_down, cotangent):
    gains = jnp.stack([attn_gain, mlp_gain]).astype(F32)
    layer_out, input_grad, rows, down = layer(
        doc_lengths, gains, tokens[0], cotangent[0], w_query, w_key, w_value, w_out, w_gate, w_up, w_down
    )
    out = finish(gains, w_query, w_key, w_value, w_gate, w_up, rows, down, layer_out, input_grad)
    return (out[0][None], out[1][None], out[2][0]) + tuple(out[3:7]) + (out[7][0],) + tuple(out[8:])


def solution(mesh):
    rows = P(("fsdp", "seq"), None)
    gain = P(("fsdp", "seq"))
    toks = P("fsdp", "seq", None)
    return jax.shard_map(
        per_device,
        mesh=mesh,
        in_specs=(toks, P("fsdp", None), gain, rows, rows, rows, rows, gain, rows, rows, rows, toks),
        out_specs=(toks, toks, gain, rows, rows, rows, rows, gain, rows, rows, rows),
        check_vma=False,
    )
```

```python
import math

import jax
import jax.numpy as jnp
from jax import lax
from jax.experimental import pallas as pl
from jax.experimental.pallas import tpu as pltpu
from jax.sharding import PartitionSpec as P

HEADS = 12
HEAD_DIM = 64
EPSILON = 1e-05
ROPE_BASE = 10000.0
MASKED_SCORE = -1e30
VMEM_LIMIT = 62 * 2**20
MESH = pl.DeviceIdType.MESH
BF16 = jnp.bfloat16
F32 = jnp.float32

NAMES = ("y", "xl", "xh", "z")
SIZES = {"y": 4, "xl": 2, "xh": 2, "z": 4, "c": 2}
ORDERS = (("y", "z", "x"), ("z", "x", "y"), ("x", "y", "z"))
ROWS = (208, 176, 192)
FULL = (1, 0, 2)
ATTN = {0: (0, 48), 1: (0, 48), 2: (0, 48)}
EARLY = {0: (48, 96), 1: (48, 96), 2: (48, 96)}
LATE = {0: (144, 64), 1: (144, 32), 2: (144, 48)}
PARTS = (ATTN, EARLY, LATE)


def place():
    f = lax.axis_index("fsdp")
    s = lax.axis_index("seq")
    return {"x": (f // 8) * 2 + s % 2, "y": s // 2, "z": (f // 2) % 4, "c": f % 2}


def device(at):
    return ((at["x"] // 2) * 8 + at["z"] * 2 + at["c"], at["y"] * 2 + at["x"] % 2)


def shifted(at, axis, k):
    return {**at, axis: (at[axis] + k) % SIZES.get(axis, 4)}


def select(names, fixed, half=None):
    index = []
    for n in names:
        size = SIZES[n]
        if half is not None and n == half[0]:
            index.append(pl.ds(half[1] * (size // 2), size // 2))
        elif n in ("xl", "xh"):
            v = fixed.get("x")
            index.append(pl.ds(0, 2) if v is None else (v % 2 if n == "xl" else v // 2))
        else:
            v = fixed.get(n)
            index.append(pl.ds(0, size) if v is None else v)
    return tuple(index)


def expand(axes):
    return [n for a in axes for n in (("xl", "xh") if a == "x" else (a,))]


def kept(names, axes):
    some = expand(axes)
    return tuple(n for n in names if n in some)


def remote(src, dst, send, recv, to):
    return pltpu.make_async_remote_copy(
        src_ref=src, dst_ref=dst, send_sem=send, recv_sem=recv, device_id=to, device_id_type=MESH
    )


def greeting(at):
    f = lax.axis_index("fsdp")
    s = lax.axis_index("seq")
    bar = pltpu.get_barrier_semaphore()
    peers = [(f, (s + k) % 8) for k in range(1, 8)]
    peers += [(f + 1 - 2 * (f % 2), (s + k) % 8) for k in range(8)]
    peers += [device(shifted(at, "z", k)) for k in (1, 2, 3)]
    peers += [device({**at, "x": (at["x"] + 2) % 4})]
    peers += [device({**at, "x": (at["x"] // 2 * 2 + 2) % 4 + (1 - at["x"] % 2)})]
    for p in peers:
        pl.semaphore_signal(bar, inc=1, device_id=p, device_id_type=MESH)
    return bar, len(peers)


def one_hot(rows, slots, per, size, offset, flip=False):
    shape = (slots * size, rows) if flip else (rows, slots * size)
    i = lax.broadcasted_iota(jnp.int32, shape, 1 if flip else 0)
    j = lax.broadcasted_iota(jnp.int32, shape, 0 if flip else 1)
    return (j == (i // per) * size + offset + i % per).astype(BF16)


def units(core, up, flip=False):
    i = lax.broadcasted_iota(jnp.int32, (384, 384), 1 if flip else 0)
    j = lax.broadcasted_iota(jnp.int32, (384, 384), 0 if flip else 1)
    y, r = (i % 192) // 48, i % 48
    early = y * 32 + r + (128 if up else 0)
    late = y * 16 + r - 32 + (320 if up else 256)
    return ((i // 192 == core) & (j == jnp.where(r < 32, early, late))).astype(BF16)


def nn(a, b):
    return jnp.dot(a, b, preferred_element_type=F32)


def nt(a, b):
    return lax.dot_general(a, b, (((1,), (1,)), ((), ())), preferred_element_type=F32)


def tn(a, b):
    return lax.dot_general(a, b, (((0,), (0,)), ((), ())), preferred_element_type=F32)


def norm_factor(values):
    return lax.rsqrt(jnp.mean(values * values, axis=-1, keepdims=True) + EPSILON)


def norm_back(values, factor, e):
    return factor * e - values * (factor * factor * factor * jnp.mean(e * values, axis=-1, keepdims=True))


def swap_halves(v):
    lane = lax.broadcasted_iota(jnp.int32, v.shape, 1)
    return jnp.where(lane % 64 < 32, pltpu.roll(v, 96, 1), pltpu.roll(v, 32, 1))


def digits(names, n):
    out = {}
    for name in reversed(names):
        out[name] = n % SIZES[name]
        n = n // SIZES[name]
    return out


def full_index(names, fixed, free, n):
    got = digits(free, n)
    index = []
    for name in names:
        if name in free:
            index.append(got[name])
        elif name in ("xl", "xh"):
            index.append(fixed["x"] % 2 if name == "xl" else fixed["x"] // 2)
        else:
            index.append(fixed[name])
    return tuple(index)


def count(names):
    return math.prod(SIZES[n] for n in names)


def layer_kernel(
    lens, gains, tok, cot, w_query, w_key, w_value, w_out, w_gate, w_up, w_down,
    out_o, in_o, rows_o, down_o, attn_o,
    a0, a1, a2, w0, w1, w2, g0, g1, g2, h0, h1, h2,
    xa, xat, r0, rd0, s0, d0, s0b, d0b, ks, vs, qs, ps, att, hid, dhid, dqs, cosine, sine, bias, rdn,
    v2s, cs, oacc, eacc, osum, esum, rdc, toks, out_s, in_s, lens_out, lens_in, sab, rab, *rest
):
    at = place()
    f = lax.axis_index("fsdp")
    s = lax.axis_index("seq")
    xl = at["x"] % 2
    here = at["y"] * 2 + at["c"]
    stays = at["c"] == xl
    partner = (f - at["c"] + xl, here)
    t3, t2, t1 = rest[:3], rest[3:6], rest[6:9]
    sem0s, sem0r, semds, semdr, semxs, semxr, sems, semr, semls, semlr, semcs, semcr, semps, sempr = rest[9:23]
    bem0s, bem0r, bemds, bemdr, bems, bemr, bemls, bemlr, bemcs, bemcr = rest[23:33]
    semms, semmr, semys, semyr, semzs, semzr, semws, semwr, semas, semar = rest[33:]
    attn_weights = (a0, a1, a2)
    weights = (w0, w1, w2)
    own_grads = (g0, g1, g2)
    homes = (h0, h1, h2)
    sibling = device(shifted(at, "c", 1))
    xl = at["x"] % 2
    beside = (f, at["y"] * 2 + 1 - xl)
    bar, others = greeting(at)
    row = lax.broadcasted_iota(jnp.int32, (6, 1), 0)

    def gain_column(which):
        col = jnp.zeros((6, 1), F32)
        for r in range(6):
            col = jnp.where(row == r, gains[which, r], col)
        return col

    gain_one, gain_two = gain_column(0), gain_column(1)
    for r in range(4):
        lens_out[r : r + 1] = jnp.full((1, 128), lens[0, r], jnp.int32).astype(F32)
    lens_out[4:8] = jnp.zeros((4, 128), F32)
    s0[...] = jnp.zeros_like(s0)
    d0[...] = jnp.zeros_like(d0)
    for b in range(8):
        lanes = pl.ds(b * 384, 384)
        half = pl.ds((b % 2) * 384, 384)
        s0[0, b, 0:6] = w_gate[:, lanes].astype(F32) * gain_two
        s0[1, b, 0:6] = w_up[:, lanes].astype(F32) * gain_two
        if b < 6:
            s0[2, b, 0:6] = (w_query, w_key, w_value)[b // 2][:, half].astype(F32) * gain_one
        else:
            s0[2, b, 0:6] = w_out[:, half].astype(F32)
    for b in range(2):
        d0[b, 0:24] = w_down[:, b * 384 : (b + 1) * 384].astype(F32)
    d0b[...] = d0[...].astype(BF16)
    gate_rows = s0[0].reshape(64, 384).astype(BF16)
    up_rows = s0[1].reshape(64, 384).astype(BF16)
    for core in range(2):
        rows = nn(gate_rows, units(core, False)) + nn(up_rows, units(core, True))
        s0b[core] = jnp.concatenate([rows.reshape(8, 8, 384), s0[2]], axis=1).astype(BF16)

    pl.semaphore_wait(bar, others)

    def group(k, src, dst, sends, recvs):
        me = at["c"] * 8 + s
        to, frm = (me + k) % 16, (me - k + 16) % 16
        peer = (f - at["c"] + to // 8, to % 8)
        send, recv = sends.at[k - 1], recvs.at[k - 1]
        out = remote(src.at[to // 8, to % 8], dst.at[me], send, recv, peer)
        inn = remote(src.at[to // 8, to % 8], dst.at[frm], send, recv, peer)
        return out, inn

    def first(k):
        return group(k, s0b, r0, sem0s, sem0r)

    def swap(buf, n):
        c = at["c"]
        return remote(buf.at[c], buf.at[c], semps.at[n], sempr.at[n], sibling)

    def swapped(buf, n):
        c = at["c"]
        return remote(buf.at[c], buf.at[1 - c], semps.at[n], sempr.at[n], sibling)

    def down_copy(slot):
        return remote(d0b.at[1 - xl], rd0.at[slot], semds, semdr, beside)

    def moves(n):
        src = (tok, cot, lens_out)[n]
        dst = (toks, cs.at[xl], lens_in)[n]
        return remote(src, dst, semms.at[n], semmr.at[n], partner)

    def token_out(y):
        return remote(xa.at[here], xa.at[here], semxs.at[y], semxr.at[at["y"]], (f, y * 2 + xl))

    def token_in(y):
        block = xa.at[y * 2 + at["c"]]
        return remote(block, block, semxs.at[y], semxr.at[y], (f, y * 2 + xl))

    def token_across(y):
        mine, other = xa.at[y * 2 + at["c"]], xa.at[y * 2 + 1 - at["c"]]
        send, recv = semys.at[y], semyr.at[y]
        return remote(mine, mine, send, recv, sibling), remote(other, other, send, recv, sibling)

    for k in range(1, 16):
        first(k)[0].start()
    down_copy(xl).start()

    def move():
        for n in (0, 2, 1):
            moves(n).start()
        for n in range(3):
            moves(n).wait()

    def stay():
        toks[...] = tok[...]
        cs[xl] = cot[...]
        lens_in[...] = lens_out[...]

    pl.when(jnp.logical_not(stays))(move)
    pl.when(stays)(stay)
    swap(cs, 0).start()
    inputs = toks[...].astype(F32)
    xa[here] = (inputs * norm_factor(inputs)).astype(BF16)
    for y in range(1, 4):
        pl.when(y > at["y"])(lambda y=y: token_out(y).start())
    pl.when(at["c"] == 0)(lambda: token_across(at["y"])[0].start())
    r0[at["c"] * 8 + s] = s0b[at["c"], s]
    rd0[xl] = d0b[xl]

    def rest(i, part):
        return pl.ds(0, 48) if part == 0 else pl.ds(48, ROWS[i] - 48)

    def split(i):
        return "z" if ORDERS[i][2] == "y" else "y"

    def block(i, fixed, core, rows, half=None):
        where = select(NAMES, fixed, half)
        if rows.start < 48:
            return attn_weights[i].at[where + (core,)]
        return weights[i].at[where + (pl.ds(rows.start - 48, rows.size),)]

    def put(i, first_row, value):
        where = select(NAMES, at)
        if first_row < 48:
            attn_weights[i][where + (at["c"],)] = value
        else:
            weights[i][where + (slice(first_row - 48, first_row - 48 + value.shape[0]),)] = value

    def ring(i, part, phase, k):
        order = ORDERS[i]
        axis = order[phase]
        fixed = {n: at[n] for n in ("x", "y", "z") if n not in order[:phase]}
        theirs = {**fixed, axis: (at[axis] - k + 4) % 4}
        mine, other = block(i, fixed, at["c"], rest(i, part)), block(i, theirs, at["c"], rest(i, part))
        slot = 2 * part + phase
        send, recv = sems.at[i, slot, k - 1], semr.at[i, slot, k - 1]
        to = device(shifted(at, axis, k))
        return remote(mine, mine, send, recv, to), remote(other, other, send, recv, to)

    def direct(i, part, k):
        axis = ORDERS[i][2]
        rows = pl.ds(*PARTS[part][i])
        mine = block(i, {axis: at[axis]}, at["c"], rows)
        other = block(i, {axis: (at[axis] - k + 4) % 4}, at["c"], rows)
        send, recv = semls.at[i, part, k - 1], semlr.at[i, part, k - 1]
        to = device(shifted(at, axis, k))
        return remote(mine, mine, send, recv, to), remote(other, other, send, recv, to)

    def relay(i, part, way):
        axis = ORDERS[i][2]
        half, rows = (split(i), way), pl.ds(*PARTS[part][i])
        mine = block(i, {axis: (at[axis] + (3, 1)[way]) % 4}, at["c"], rows, half)
        other = block(i, {axis: (at[axis] + 2) % 4}, at["c"], rows, half)
        send, recv = semls.at[i, part, (1, 3)[way]], semlr.at[i, part, (1, 3)[way]]
        to = device(shifted(at, axis, (1, 3)[way]))
        return remote(mine, mine, send, recv, to), remote(other, other, send, recv, to)

    def across(i, k):
        axis = ORDERS[i][2]
        where = {axis: (at[axis] + k) % 4}
        mine, other = block(i, where, at["c"], rest(i, 0)), block(i, where, 1 - at["c"], rest(i, 0))
        send, recv = semcs.at[i, k], semcr.at[i, k]
        return remote(mine, mine, send, recv, sibling), remote(other, other, send, recv, sibling)

    def start(part, phase):
        for k in (1, 3, 2):
            for i in FULL:
                ring(i, part, phase, k)[0].start()

    def arrive(part, phase):
        for k in (1, 3, 2):
            for i in FULL:
                ring(i, part, phase, k)[1].wait_recv()

    def start_last(part):
        for k in (1, 3) if part else (1, 3, 2):
            for i in PARTS[part]:
                direct(i, part, k)[0].start()

    def pass_last(part):
        for way in range(2):
            for i in PARTS[part]:
                direct(i, part, (1, 3)[way])[1].wait_recv()
                relay(i, part, way)[0].start()

    def arrive_last(part):
        for i in PARTS[part]:
            if part:
                for way in range(2):
                    relay(i, part, way)[1].wait_recv()
            else:
                for k in (1, 3, 2):
                    direct(i, part, k)[1].wait_recv()
                    across(i, (4 - k) % 4)[0].start()

    def sent(part):
        for i in PARTS[part]:
            for k in (1, 3) if part else (1, 2, 3):
                direct(i, part, k)[0].wait_send()
            if part:
                for way in range(2):
                    relay(i, part, way)[0].wait_send()

    for k in range(1, 16):
        first(k)[1].wait_recv()
    flat = r0[...].reshape(256, 384)
    piece = nn(one_hot(48, 16, 6, 16, at["c"] * 128 + 8), flat).astype(BF16)
    for i in range(3):
        put(i, 0, piece[:, i * 128 : (i + 1) * 128])
    start(0, 0)
    piece = nn(one_hot(96, 16, 6, 16, 0), flat).astype(BF16)
    put(0, 48, piece[:, :128])
    put(0, 144, piece[:64, 256:])
    put(1, 48, piece[:, 128:256])
    put(1, 144, piece[64:, 256:])
    down_copy(1 - xl).wait_recv()
    piece = nn(one_hot(48, 2, 24, 32, 0), rd0[...].reshape(64, 384)).astype(BF16)
    for b in range(3):
        lanes = slice(b * 128, (b + 1) * 128)
        put(2, 48 + 32 * b, piece[:32, lanes])
        put(2, 144 + 16 * b, piece[32:, lanes])
    start(1, 0)
    arrive(0, 0)
    start(0, 1)
    arrive(0, 1)
    start_last(0)
    for i in ATTN:
        across(i, 0)[0].start()
    arrive(1, 0)
    start(1, 1)

    ends = [lens_in[0:1, :]]
    for r in (1, 2):
        ends.append(ends[-1] + lens_in[r : r + 1, :])
    freq_lane = (lax.broadcasted_iota(jnp.int32, (1, 128), 1) % 32).astype(F32)
    freqs = jnp.exp(freq_lane * (-2.0 * math.log(ROPE_BASE) / HEAD_DIM))
    lane = lax.broadcasted_iota(jnp.int32, (128, 128), 1)

    def segment_of(index):
        return sum(jnp.where(index >= e, 1.0, 0.0) for e in ends)

    def table(u, carry):
        index = (u * 128 + lax.broadcasted_iota(jnp.int32, (128, 128), 0)).astype(F32)
        begin = jnp.zeros_like(index)
        for e in ends:
            begin = jnp.where(index >= e, e, begin)
        angle = (index - begin) * freqs
        rows = pl.ds(pl.multiple_of(u * 128, 128), 128)
        cosine[rows, :] = jnp.cos(angle)
        sine[rows, :] = jnp.where(lane % 64 < 32, -1.0, 1.0) * jnp.sin(angle)
        mine = (here * 128 + lax.broadcasted_iota(jnp.int32, (1, 128), 1)).astype(F32)
        allowed = (segment_of(index) == segment_of(mine)) & (index <= mine)
        bias[rows, :] = jnp.where(allowed, 0.0, MASKED_SCORE)
        return carry

    lax.fori_loop(0, 8, table, 0)

    arrive(1, 1)
    start_last(1)
    for u in range(1, 8):

        def clear(u=u):
            xa[u] = jnp.zeros((128, 768), BF16)

        pl.when(u > here)(clear)
    for y in range(3):

        def pass_on(y=y):
            token_in(y).wait_recv()
            token_across(y)[0].start()

        pl.when(y < at["y"])(pass_on)
    for y in range(3):
        pl.when(y < at["y"])(lambda y=y: token_across(y)[1].wait_recv())
    pl.when(at["c"] == 1)(lambda: token_across(at["y"])[1].wait_recv())

    def transpose_tokens(u, carry):
        xat[:, pl.ds(pl.multiple_of(u * 128, 128), 128)] = xa[u].T
        return carry

    lax.fori_loop(0, 8, transpose_tokens, 0)
    arrive_last(0)
    for k in range(4):
        for i in ATTN:
            across(i, k)[1].wait_recv()

    for k in range(1, 16):
        first(k)[0].wait_send()
    down_copy(xl).wait_send()
    for y in range(1, 4):
        pl.when(y > at["y"])(lambda y=y: token_out(y).wait_send())
    for y in range(3):
        pl.when(y < at["y"])(lambda y=y: token_across(y)[0].wait_send())
    pl.when(at["c"] == 0)(lambda: token_across(at["y"])[0].wait_send())

    mine = pl.ds(pl.multiple_of(here * 128, 128), 128)
    cos_mine, sin_mine = cosine[mine, :], sine[mine, :]
    left = lax.broadcasted_iota(jnp.int32, (128, 128), 1) < 64

    def attn_weight(kind, t, h):
        return attn_weights[t][kind, h].reshape(768, 128)

    def put_grad(kind, t, h, value):
        own_grads[t][kind, h] = value.reshape(2, 4, 2, 48, 128)

    def attn_full(kind):
        return jnp.concatenate([attn_weight(kind, p % 3, p // 3) for p in range(6)], axis=1)

    def stacked(v):
        zero = jnp.zeros_like(v)
        return jnp.concatenate([jnp.where(left, v, zero), jnp.where(left, zero, v)], axis=0)

    def unstacked(v):
        return jnp.concatenate([v[:64, :128], v[64:, 128:]], axis=0).T

    def pair_lanes(p):
        return pl.ds(pl.multiple_of(p * 128, 128), 128)

    def attend(t, h):
        p = t + 3 * h
        tokens_all = xa[...].reshape(1024, 768)
        w_kv = jnp.concatenate([attn_weight(1, t, h), attn_weight(2, t, h)], axis=1)
        kv = nn(tokens_all, w_kv)
        k_raw = kv[:, :128]
        k = (k_raw * cosine[...] + swap_halves(k_raw) * sine[...]).astype(BF16)
        v = kv[:, 128:].astype(BF16)
        q_raw = nn(xa[here], attn_weight(0, t, h))
        q = ((q_raw * cos_mine + swap_halves(q_raw) * sin_mine).astype(BF16) * (1.0 / math.sqrt(HEAD_DIM))).astype(BF16)
        qq = stacked(q)
        ks[p] = k
        vs[p] = v
        qs[p] = qq
        masks = bias[...]
        scores = nt(k, qq) + jnp.concatenate([masks, masks], axis=1)
        top = jnp.max(scores, axis=0, keepdims=True)
        e = jnp.exp(scores - top)
        total = jnp.sum(e, axis=0, keepdims=True)
        probs = (e * (1.0 / total)).astype(BF16)
        ps[p] = probs
        att[:, pair_lanes(p)] = unstacked(tn(v, probs)).astype(BF16)

    for t in range(3):

        def attend_third(h, carry, t=t):
            attend(t, h)
            return carry

        lax.fori_loop(0, 2, attend_third, 0)
        if t == 0:
            pass_last(1)
            start_last(2)


    hidden = toks[...].astype(F32) + nn(att[...], attn_full(3))
    hid[...] = hidden
    factor_two = norm_factor(hidden)
    v2s[at["c"]] = (hidden * factor_two).astype(BF16)
    swap(v2s, 1).start()
    oacc[...] = jnp.zeros_like(oacc)
    eacc[...] = jnp.zeros_like(eacc)
    swapped(cs, 0).wait()
    swapped(v2s, 1).wait()
    v2 = v2s[...].reshape(256, 768)
    v2t = v2.T

    def pair(a, b):
        return jnp.concatenate([a, b], axis=1)

    def gated(gate, up, d_w):
        c = cs[...].reshape(256, 768)
        sig = 1.0 / (1.0 + jnp.exp(-gate))
        silu = gate * sig
        mixed = (silu * up).astype(BF16)
        oacc[...] += nn(mixed, d_w).reshape(2, 128, 768)
        d_mixed = nt(c, d_w)
        d_gate = d_mixed * up * sig * (1.0 + gate * (1.0 - sig))
        d_up = d_mixed * silu
        return d_gate, d_up, tn(mixed, c).astype(BF16)

    def down_rows(xh, z, first_row, rows):
        def part(b, h, n):
            some = pl.ds(first_row - 48 + n * rows, rows)
            return w2[:, h, xh, z + b, some].reshape(4 * rows, 128)

        return jnp.concatenate(
            [jnp.concatenate([part(b, h, n) for h in range(2) for n in range(3)], axis=1) for b in range(2)], axis=0
        )

    def put_down(xh, z, first_row, rows, g):
        for b in range(2):
            for h in range(2):
                for n in range(3):
                    some = pl.ds(first_row + n * rows, rows)
                    lanes = slice(h * 384 + n * 128, h * 384 + (n + 1) * 128)
                    h2[:, h, xh, z + b, some] = g[b * 4 * rows : (b + 1) * 4 * rows, lanes].reshape(4, rows, 128)

    def feed_early(y, carry):
        g_w = pair(*(w0[y, b, :, :, 0:96].reshape(768, 128) for b in range(2)))
        u_w = pair(*(w1[y, b, :, :, 0:96].reshape(768, 128) for b in range(2)))
        xh, z = y // 2, (y % 2) * 2
        d_w = down_rows(xh, z, 48, 32)
        d_gate, d_up, g_d = gated(nn(v2, g_w), nn(v2, u_w), d_w)
        d_gate, d_up = d_gate.astype(BF16), d_up.astype(BF16)
        eacc[...] += (nt(d_gate, g_w) + nt(d_up, u_w)).reshape(2, 128, 768)
        g_g = nn(v2t, d_gate).astype(BF16)
        g_u = nn(v2t, d_up).astype(BF16)
        for b in range(2):
            lanes = slice(b * 128, (b + 1) * 128)
            h0[y, b, :, :, 48:144] = g_g[:, lanes].reshape(2, 4, 96, 128)
            h1[y, b, :, :, 48:144] = g_u[:, lanes].reshape(2, 4, 96, 128)
        put_down(xh, z, 48, 32, g_d)
        return carry

    def feed_late(y, carry):
        def weight(b):
            low_rows, high_rows = w0[y, b, :, :, 96:160], w1[y, b, :, :, 96:128]
            return jnp.concatenate([low_rows, high_rows], axis=2).reshape(768, 128)

        w = pair(weight(0), weight(1))
        xh, z = y // 2, (y % 2) * 2
        d_w = down_rows(xh, z, 144, 16)
        both = nn(v2, w)
        low = lax.broadcasted_iota(jnp.int32, (256, 128), 1) < 64

        def mix(a, b):
            return jnp.where(low, a, pltpu.roll(b, 64, 1)), jnp.where(low, pltpu.roll(a, 64, 1), b)

        gate, up = mix(both[:, :128], both[:, 128:])
        d_gate, d_up, g_d = gated(gate, up, d_w)
        d_both = pair(*mix(d_gate, d_up)).astype(BF16)
        eacc[...] += nt(d_both, w).reshape(2, 128, 768)
        g = nn(v2t, d_both).astype(BF16)
        for b in range(2):
            rows = g[:, b * 128 : (b + 1) * 128].reshape(2, 4, 96, 128)
            h0[y, b, :, :, 144:208] = rows[:, :, :64]
            h1[y, b, :, :, 144:176] = rows[:, :, 64:]
        put_down(xh, z, 144, 16, g_d)
        return carry

    def home(i, fixed, part=None, half=None):
        first_row, rows = (0, ROWS[i]) if part is None else PARTS[part][i]
        return homes[i].at[select(NAMES, fixed, half) + (pl.ds(first_row, rows),)]

    def share(i, k):
        where = {ORDERS[i][2]: (at[ORDERS[i][2]] + k) % 4}
        part = own_grads[i].at[select(NAMES, where) + (1 - at["c"],)]
        return remote(part, home(i, where, 0), bemcs.at[i, k], bemcr.at[i, k], sibling)

    def add_core(i, k):
        order = ORDERS[i]
        free = kept(NAMES, order[:2])
        fixed = {order[2]: (at[order[2]] + k) % 4}
        rows = pl.ds(*ATTN[i])

        def body(n, carry):
            index = full_index(NAMES, fixed, free, n)
            total = homes[i][index + (rows,)].astype(F32) + own_grads[i][index + (at["c"],)].astype(F32)
            homes[i][index + (rows,)] = total.astype(BF16)
            return carry

        lax.fori_loop(0, count(free), body, 0, unroll=4)

    def halfway(i, part, way):
        axis = ORDERS[i][2]
        half = (split(i), way)
        src = home(i, {axis: (at[axis] + 2) % 4}, part, half)
        dst = t3[i].at[(1,) + select(kept(NAMES, ORDERS[i][:2]), {}, half) + (pl.ds(*PARTS[part][i]),)]
        send, recv = bemls.at[i, part, way], bemlr.at[i, part, way]
        return remote(src, dst, send, recv, device(shifted(at, axis, (1, 3)[way])))

    def whole(i, part, way):
        axis = ORDERS[i][2]
        src = home(i, {axis: (at[axis] + (1, 3)[way]) % 4}, part)
        dst = t3[i].at[2 * way, :, :, :, pl.ds(*PARTS[part][i])] if ORDERS[i][2] != "x" else t3[i].at[
            2 * way, :, :, pl.ds(*PARTS[part][i])
        ]
        send, recv = bemls.at[i, part, 2 + way], bemlr.at[i, part, 2 + way]
        return remote(src, dst, send, recv, device(shifted(at, axis, (1, 3)[way])))

    def add_half(i, part, way):
        order = ORDERS[i]
        where = split(i)
        free = kept(NAMES, order[:2])
        turned = (where,) + tuple(m for m in free if m != where)
        fixed = {order[2]: (at[order[2]] + (1, 3)[way]) % 4}
        rows = pl.ds(*PARTS[part][i])

        def body(n, carry):
            got = digits(turned, n)
            got[where] = got[where] + way * (SIZES[where] // 2)
            n = 0
            for m in free:
                n = n * SIZES[m] + got[m]
            index = full_index(NAMES, fixed, free, n) + (rows,)
            came = t3[i][(1,) + tuple(got[m] for m in free) + (rows,)]
            homes[i][index] = (homes[i][index].astype(F32) + came.astype(F32)).astype(BF16)
            return carry

        lax.fori_loop(0, count(free) // 2, body, 0, unroll=4)

    def add_whole(i, part):
        order = ORDERS[i]
        free = kept(NAMES, order[:2])
        fixed = {order[2]: at[order[2]]}
        rows = pl.ds(*PARTS[part][i])

        def body(n, carry):
            index = full_index(NAMES, fixed, free, n) + (rows,)
            there = full_index(free, {}, free, n) + (rows,)
            total = homes[i][index].astype(F32)
            for k in (0, 2) if part else (0, 1, 2):
                total = total + t3[i][(k,) + there].astype(F32)
            homes[i][index] = total.astype(BF16)
            return carry

        lax.fori_loop(0, count(free), body, 0, unroll=4)

    def hop(i, part, left, k):
        order = ORDERS[i]
        axis = order[left - 1]
        fixed = {a: at[a] for a in order[left:]}
        rows = rest(i, part)
        src = homes[i].at[select(NAMES, {**fixed, axis: (at[axis] + k) % 4}) + (rows,)]
        if left == 1:
            dst = t1[i].at[k - 1, rows]
        else:
            dst = t2[i].at[(k - 1,) + select(kept(NAMES, order[:1]), {}) + (rows,)]
        slot = 2 * part + left - 1
        send, recv = bems.at[i, slot, k - 1], bemr.at[i, slot, k - 1]
        return remote(src, dst, send, recv, device(shifted(at, axis, k)))

    def add_ring(i, part):
        order = ORDERS[i]
        free = kept(NAMES, order[:1])
        fixed = {a: at[a] for a in order[1:]}
        rows = rest(i, part)

        def body(n, carry):
            index = full_index(NAMES, fixed, free, n) + (rows,)
            total = homes[i][index].astype(F32)
            for k in range(3):
                total = total + t2[i][(k,) + full_index(free, {}, free, n) + (rows,)].astype(F32)
            homes[i][index] = total.astype(BF16)
            return carry

        lax.fori_loop(0, count(free), body, 0)

    def hop_start(part):
        for k in (1, 3, 2):
            for i in FULL:
                hop(i, part, 2, k).start()

    def hop_on(part):
        for i in FULL:
            for k in (1, 3, 2):
                hop(i, part, 2, k).wait_recv()
            add_ring(i, part)
            for k in (1, 3, 2):
                hop(i, part, 1, k).start()

    def last(i, part):
        for k in (1, 3, 2):
            hop(i, part, 1, k).wait_recv()
        rows = rest(i, part)
        total = homes[i][select(NAMES, at) + (rows,)].astype(F32)
        for k in range(3):
            total = total + t1[i][k, rows].astype(F32)
        return total.astype(BF16)

    def hop_last(i, k):
        axis = ORDERS[i][2]
        src = home(i, {axis: (at[axis] + k) % 4}, 0)
        rows = pl.ds(*ATTN[i])
        dst = t3[i].at[(k - 1,) + select(kept(NAMES, ORDERS[i][:2]), {}) + (rows,)]
        send, recv = bemls.at[i, 0, k - 1], bemlr.at[i, 0, k - 1]
        return remote(src, dst, send, recv, device(shifted(at, axis, k)))

    def half_start(part, items=FULL):
        for way in range(2):
            for i in items:
                if i in PARTS[part]:
                    halfway(i, part, way).start()

    def half_on(part, items=FULL):
        for way in range(2):
            for i in items:
                if i in PARTS[part]:
                    halfway(i, part, way).wait_recv()
                    add_half(i, part, way)
                    whole(i, part, way).start()

    def whole_on(part):
        for i in PARTS[part]:
            if part:
                for way in range(2):
                    whole(i, part, way).wait_recv()
            else:
                for k in (1, 3, 2):
                    hop_last(i, k).wait_recv()
            add_whole(i, part)

    for i in FULL:
        for part in range(2):
            if i in FULL:
                for phase in range(2):
                    for k in (1, 2, 3):
                        ring(i, part, phase, k)[0].wait_send()
    arrive_last(1)
    feed_early(0, 0)
    pass_last(2)
    for y in range(1, 4):
        feed_early(y, 0)
    half_start(1)
    arrive_last(2)
    for y in range(4):
        feed_late(y, 0)
    sum_o = remote(oacc.at[1 - at["c"]], osum, semps.at[2], sempr.at[2], sibling)
    sum_e = remote(eacc.at[1 - at["c"]], esum, semps.at[3], sempr.at[3], sibling)
    sum_e.start()
    sum_o.start()
    half_start(2)
    half_on(1)
    sum_e.wait()

    hidden = hid[...]
    factor_two = norm_factor(hidden)
    d_hidden = cs[at["c"]].astype(F32) + norm_back(hidden, factor_two, eacc[at["c"]] + esum[...])
    dhid[...] = d_hidden
    dh = d_hidden.astype(BF16)
    d_att = nt(dh, attn_full(3)).astype(BF16)
    att_t = att[...].T
    for j in range(2):
        g_o = nn(att_t, dh[:, j * 384 : (j + 1) * 384]).astype(BF16)
        for t in range(3):
            put_grad(3, t, j, g_o[:, t * 128 : (t + 1) * 128])
    att[...] = d_att

    def attend_back(t, h):
        p = t + 3 * h
        da = stacked(att[:, pair_lanes(p)])
        k, v, qq, probs = ks[p], vs[p], qs[p], ps[p]
        d_probs = nt(v, da)
        probs_f = probs.astype(F32)
        d_sum = jnp.sum(probs_f * d_probs, axis=0, keepdims=True)
        d_scores = (probs_f * (d_probs - d_sum)).astype(BF16)
        d_v = nn(probs, da).astype(BF16)
        d_k = nn(d_scores, qq)
        d_k = (d_k * cosine[...] - swap_halves(d_k) * sine[...]).astype(BF16)
        d_q = unstacked(tn(k, d_scores)) * (1.0 / math.sqrt(HEAD_DIM))
        d_q = (d_q * cos_mine - swap_halves(d_q) * sin_mine).astype(BF16)
        ks[p] = d_k
        vs[p] = d_v
        dqs[:, pair_lanes(p)] = d_q
        g_kv = nn(xat[...], jnp.concatenate([d_k, d_v], axis=1)).astype(BF16)
        g_q = nn(xat[:, mine], d_q).astype(BF16)
        put_grad(0, t, h, g_q)
        put_grad(1, t, h, g_kv[:, :128])
        put_grad(2, t, h, g_kv[:, 128:])

    def share_on(i):
        for k in (2, 1, 3, 0):
            share(i, k).wait_recv()
            add_core(i, k)
            if k:
                hop_last(i, k).start()

    half_on(2)
    def third_back(h, carry):
        attend_back(0, h)
        return carry

    lax.fori_loop(0, 2, third_back, 0)

    def share_start(i):
        for k in (2, 1, 3, 0):
            share(i, k).start()

    share_start(0)
    attend_back(1, 0)
    share_on(0)
    attend_back(1, 1)
    share_start(1)
    attend_back(2, 0)
    share_on(1)
    attend_back(2, 1)
    share_start(2)
    whole_on(1)
    share_on(2)
    whole_on(2)
    hop_start(1)

    w_kv = jnp.concatenate([attn_full(1), attn_full(2)], axis=1)

    def tokens_back(u, carry):
        rows = pl.ds(pl.multiple_of(u * 128, 128), 128)
        d_kv = jnp.concatenate([ks[p, rows, :] for p in range(6)] + [vs[p, rows, :] for p in range(6)], axis=1)
        xa[u] = nt(d_kv, w_kv).astype(BF16)
        return carry

    lax.fori_loop(0, 8, tokens_back, 0)

    def grad_across(y):
        mine = xa.at[y * 2 + 1 - at["c"]]
        return remote(mine, rdc.at[y], semzs.at[y], semzr.at[y], sibling)

    def grad_out(y):
        return remote(xa.at[y * 2 + at["c"]], rdn.at[at["y"]], semws.at[y], semwr.at[at["y"]], (f, y * 2 + xl))

    def grad_in(y):
        return remote(xa.at[y * 2 + at["c"]], rdn.at[y], semws.at[y], semwr.at[y], (f, y * 2 + xl))

    for y in range(3):
        pl.when(y < at["y"])(lambda y=y: grad_across(y).start())
    pl.when(at["c"] == 1)(lambda: grad_across(at["y"]).start())
    for y in range(3):

        def add_across(y=y):
            grad_across(y).wait_recv()
            block = xa[y * 2 + at["c"]].astype(F32) + rdc[y].astype(F32)
            xa[y * 2 + at["c"]] = block.astype(BF16)
            grad_out(y).start()

        pl.when(y < at["y"])(add_across)
    sum_o.wait()
    out_s[...] = (hid[...] + oacc[at["c"]] + osum[...]).astype(BF16)

    def out_move():
        return remote(out_s, out_o, semms.at[3], semmr.at[3], partner)

    def out_stay():
        out_o[...] = out_s[...]

    pl.when(jnp.logical_not(stays))(lambda: out_move().start())
    pl.when(stays)(out_stay)
    esum[...] = nt(dqs[...], attn_full(0))

    hop_on(1)
    whole_on(0)
    hop_start(0)
    sum0, sum1, sum2 = last(0, 1), last(1, 1), last(2, 1)
    down = jnp.concatenate(
        [
            jnp.concatenate([sum2[a + b * n : a + b * (n + 1)] for n in range(3)], axis=1)
            for a, b in ((0, 32), (96, 16))
        ],
        axis=0,
    )
    mixed_units = jnp.concatenate([sum0[96:160], sum1[96:128]], axis=0)
    both = jnp.concatenate([sum0[0:96], sum1[0:96], mixed_units], axis=1)
    rows_mlp = nn(one_hot(96, 16, 6, 16, 0, True), both)
    d0b[...] = nn(one_hot(48, 2, 24, 32, 0, True), down).astype(BF16).reshape(2, 32, 384)
    s0b[...] = rows_mlp.astype(BF16).reshape(2, 8, 16, 384)

    def final(k):
        return group(k, s0b, r0, bem0s, bem0r)

    def final_down(slot):
        return remote(d0b.at[1 - xl], rd0.at[slot], bemds, bemdr, beside)

    for k in range(1, 16):
        final(k)[0].start()
    final_down(xl).start()
    hop_on(0)

    esum[...] += xa[here].astype(F32)

    def add_own():
        grad_across(at["y"]).wait_recv()
        esum[...] += rdc[at["y"]].astype(F32)

    pl.when(at["c"] == 0)(add_own)
    for y in range(1, 4):

        def add(y=y):
            grad_in(y).wait_recv()
            esum[...] += rdn[y].astype(F32)

        pl.when(y > at["y"])(add)
    inputs = toks[...].astype(F32)
    in_s[...] = dhid[...] + norm_back(inputs, norm_factor(inputs), esum[...])

    def in_move():
        return remote(in_s, in_o, semms.at[4], semmr.at[4], partner)

    def in_stay():
        in_o[...] = in_s[...]

    pl.when(jnp.logical_not(stays))(lambda: in_move().start())
    pl.when(stays)(in_stay)
    attn = jnp.concatenate([last(i, 0) for i in range(3)], axis=1)
    rows = nn(one_hot(48, 8, 6, 16, 0, True), attn)
    sab[...] = rows.astype(BF16).reshape(8, 16, 384)

    def final_attn(k):
        to, frm = (s + k) % 8, (s - k + 8) % 8
        out = remote(sab.at[to], rab.at[s], semas.at[k - 1], semar.at[k - 1], (f, to))
        inn = remote(sab.at[to], rab.at[frm], semas.at[k - 1], semar.at[k - 1], (f, to))
        return out, inn

    for k in range(1, 8):
        final_attn(k)[0].start()
    rab[s] = sab[s]
    r0[at["c"] * 8 + s] = s0b[at["c"], s]
    rd0[xl] = d0b[xl]
    for k in range(1, 16):
        final(k)[1].wait_recv()
    final_down(1 - xl).wait_recv()
    rows_o[...] = r0[...]
    down_o[...] = rd0[...]
    for k in range(1, 8):
        final_attn(k)[1].wait_recv()
    attn_o[...] = rab[...]
    for k in range(1, 16):
        final(k)[0].wait_send()
    for k in range(1, 8):
        final_attn(k)[0].wait_send()
    final_down(xl).wait_send()
    for y in range(3):

        def across_sent(y=y):
            grad_across(y).wait_send()
            grad_out(y).wait_send()

        pl.when(y < at["y"])(across_sent)
    pl.when(at["c"] == 1)(lambda: grad_across(at["y"]).wait_send())

    def moved():
        out_move().wait()
        in_move().wait()

    pl.when(jnp.logical_not(stays))(moved)
    for part in range(3):
        sent(part)
    for i in ATTN:
        for k in range(4):
            across(i, k)[0].wait_send()
            share(i, k).wait_send()
    for i in ATTN:
        for k in (1, 2, 3):
            hop_last(i, k).wait_send()
    for part in (1, 2):
        for i in PARTS[part]:
            for way in range(2):
                halfway(i, part, way).wait_send()
                whole(i, part, way).wait_send()
    for part in range(2):
        for i in FULL:
            for left in (2, 1):
                for k in (1, 2, 3):
                    hop(i, part, left, k).wait_send()


def finish_kernel(gains, w_query, w_key, w_value, w_gate, w_up, rows_i, down_i, attn_i, out_i, in_i,
                  out_o, in_o, ga1_o, gq_o, gk_o, gv_o, go_o, ga2_o, gg_o, gu_o, gd_o, s0):
    out_o[...] = out_i[...]
    in_o[...] = in_i[...]
    row = lax.broadcasted_iota(jnp.int32, (6, 1), 0)

    def gain_column(which):
        col = jnp.zeros((6, 1), F32)
        for r in range(6):
            col = jnp.where(row == r, gains[which, r], col)
        return col

    def as_row(col):
        lane = lax.broadcasted_iota(jnp.int32, (6, 6), 1)
        side = lax.broadcasted_iota(jnp.int32, (6, 6), 0)
        return jnp.sum(jnp.where(lane == side, col, 0.0), axis=0, keepdims=True)

    gain_one, gain_two = gain_column(0), gain_column(1)
    got = rows_i[...].reshape(2, 8, 16, 384)
    halves = [got[core, :, :8].reshape(64, 384) for core in range(2)]
    for which in range(2):
        natural = nn(halves[0], units(0, which == 1, True)) + nn(halves[1], units(1, which == 1, True))
        s0[which] = natural.reshape(8, 8, 384)
    s0[2] = attn_i[:, 0:8, :].astype(F32)
    down = down_i[...].astype(F32)
    gain_sum_one = jnp.zeros((6, 1), F32)
    gain_sum_two = jnp.zeros((6, 1), F32)
    for b in range(8):
        lanes = pl.ds(b * 384, 384)
        half = pl.ds((b % 2) * 384, 384)
        h_gate, h_up, h_attn = s0[0, b, 0:6], s0[1, b, 0:6], s0[2, b, 0:6]
        gg_o[:, lanes] = h_gate * gain_two
        gu_o[:, lanes] = h_up * gain_two
        gain_sum_two += jnp.sum(h_gate * w_gate[:, lanes].astype(F32), axis=1, keepdims=True)
        gain_sum_two += jnp.sum(h_up * w_up[:, lanes].astype(F32), axis=1, keepdims=True)
        if b < 6:
            (gq_o, gk_o, gv_o)[b // 2][:, half] = h_attn * gain_one
            raw = (w_query, w_key, w_value)[b // 2][:, half].astype(F32)
            gain_sum_one += jnp.sum(h_attn * raw, axis=1, keepdims=True)
        else:
            go_o[:, half] = h_attn
    for b in range(2):
        gd_o[:, b * 384 : (b + 1) * 384] = down[b, 0:24]
    ga1_o[...] = as_row(gain_sum_one)
    ga2_o[...] = as_row(gain_sum_two)


VMEM_SPEC = pl.BlockSpec(memory_space=pltpu.VMEM)
SMEM_SPEC = pl.BlockSpec(memory_space=pltpu.SMEM)
DMA = pltpu.SemaphoreType.DMA


def layer(lens, gains, *arrays):
    outs = [((128, 768), BF16), ((128, 768), F32), ((16, 16, 384), BF16), ((2, 32, 384), BF16), ((8, 16, 384), BF16)]
    sizes = tuple(SIZES[n] for n in NAMES)
    scratch = [(sizes + (2, 48, 128), BF16) for _ in ROWS] + [(sizes + (r - 48, 128), BF16) for r in ROWS]
    scratch += [(sizes + (2, 48, 128), BF16) for _ in ROWS]
    scratch += [(sizes + (r, 128), BF16) for r in ROWS]
    scratch += [
        ((8, 128, 768), BF16), ((768, 1024), BF16), ((16, 16, 384), BF16), ((2, 32, 384), BF16),
        ((3, 8, 8, 384), F32), ((2, 32, 384), F32), ((2, 8, 16, 384), BF16), ((2, 32, 384), BF16),
        ((6, 1024, 128), BF16), ((6, 1024, 128), BF16), ((6, 256, 128), BF16), ((6, 1024, 256), BF16),
        ((128, 768), BF16), ((128, 768), F32), ((128, 768), F32), ((128, 768), BF16),
        ((1024, 128), F32), ((1024, 128), F32), ((1024, 128), F32), ((4, 128, 768), BF16),
        ((2, 128, 768), BF16), ((2, 128, 768), BF16), ((2, 128, 768), F32), ((2, 128, 768), F32),
        ((128, 768), F32), ((128, 768), F32), ((4, 128, 768), BF16), ((128, 768), BF16), ((128, 768), BF16), ((128, 768), F32),
        ((8, 128), F32), ((8, 128), F32), ((8, 16, 384), BF16), ((8, 16, 384), BF16),
    ]
    for rings in (2, 1, 0):
        for i in range(3):
            left = tuple(SIZES[n] for n in kept(NAMES, ORDERS[i][:rings]))
            scratch.append(((3,) + left + (ROWS[i], 128), BF16))
    copies = [
        DMA((15,)), DMA((15,)), DMA, DMA, DMA((4,)), DMA((4,)),
        DMA((3, 4, 3)), DMA((3, 4, 3)), DMA((3, 3, 4)), DMA((3, 3, 4)), DMA((3, 4)), DMA((3, 4)), DMA((4,)), DMA((4,)),
        DMA((15,)), DMA((15,)), DMA, DMA,
        DMA((3, 4, 3)), DMA((3, 4, 3)), DMA((3, 3, 4)), DMA((3, 3, 4)), DMA((3, 4)), DMA((3, 4)),
        DMA((5,)), DMA((5,)), DMA((4,)), DMA((4,)), DMA((4,)), DMA((4,)), DMA((4,)), DMA((4,)), DMA((7,)), DMA((7,)),
    ]
    return pl.pallas_call(
        layer_kernel,
        out_shape=[jax.ShapeDtypeStruct(shape, kind) for shape, kind in outs],
        in_specs=[SMEM_SPEC] * 2 + [VMEM_SPEC] * 9,
        out_specs=[VMEM_SPEC] * len(outs),
        scratch_shapes=[pltpu.VMEM(shape, kind) for shape, kind in scratch] + copies,
        compiler_params=pltpu.CompilerParams(collective_id=0, has_side_effects=True, vmem_limit_bytes=VMEM_LIMIT),
        name="layer",
    )(lens, gains, *arrays)


def finish(gains, *arrays):
    outs = [
        ((128, 768), BF16), ((128, 768), F32), ((1, 6), F32),
        ((6, 768), F32), ((6, 768), F32), ((6, 768), F32), ((6, 768), F32),
        ((1, 6), F32), ((6, 3072), F32), ((6, 3072), F32), ((24, 768), F32),
    ]
    return pl.pallas_call(
        finish_kernel,
        out_shape=[jax.ShapeDtypeStruct(shape, kind) for shape, kind in outs],
        in_specs=[SMEM_SPEC] + [VMEM_SPEC] * 10,
        out_specs=[VMEM_SPEC] * len(outs),
        scratch_shapes=[pltpu.VMEM((3, 8, 8, 384), F32)],
        name="finish",
    )(gains, *arrays)


def per_device(tokens, doc_lengths, attn_gain, w_query, w_key, w_value, w_out, mlp_gain, w_gate, w_up, w_down, cotangent):
    gains = jnp.stack([attn_gain, mlp_gain]).astype(F32)
    layer_out, input_grad, rows, down, rows_attn = layer(
        doc_lengths, gains, tokens[0], cotangent[0], w_query, w_key, w_value, w_out, w_gate, w_up, w_down
    )
    out = finish(gains, w_query, w_key, w_value, w_gate, w_up, rows, down, rows_attn, layer_out, input_grad)
    return (out[0][None], out[1][None], out[2][0]) + tuple(out[3:7]) + (out[7][0],) + tuple(out[8:])


def solution(mesh):
    rows = P(("fsdp", "seq"), None)
    gain = P(("fsdp", "seq"))
    toks = P("fsdp", "seq", None)
    return jax.shard_map(
        per_device,
        mesh=mesh,
        in_specs=(toks, P("fsdp", None), gain, rows, rows, rows, rows, gain, rows, rows, rows, toks),
        out_specs=(toks, toks, gain, rows, rows, rows, rows, gain, rows, rows, rows),
        check_vma=False,
    )
```

```python
import math

import jax
import jax.numpy as jnp
from jax import lax
from jax.experimental import pallas as pl
from jax.experimental.pallas import tpu as pltpu
from jax.sharding import PartitionSpec as P

HEADS = 12
HEAD_DIM = 64
EPSILON = 1e-05
ROPE_BASE = 10000.0
MASKED_SCORE = -1e30
VMEM_LIMIT = 62 * 2**20
MESH = pl.DeviceIdType.MESH
BF16 = jnp.bfloat16
F32 = jnp.float32

NAMES = ("y", "xl", "xh", "z")
SIZES = {"y": 4, "xl": 2, "xh": 2, "z": 4, "c": 2}
ORDERS = (("y", "z", "x"), ("z", "x", "y"), ("x", "y", "z"))
ROWS = (208, 160, 208)
FULL = (1, 0, 2)
ATTN = {0: (0, 48), 1: (0, 48), 2: (0, 48)}
EARLY = {0: (48, 96), 1: (48, 96), 2: (48, 96)}
LATE = {0: (144, 64), 1: (144, 16), 2: (144, 64)}
PARTS = (ATTN, EARLY, LATE)


def place():
    f = lax.axis_index("fsdp")
    s = lax.axis_index("seq")
    return {"x": (f // 8) * 2 + s % 2, "y": s // 2, "z": (f // 2) % 4, "c": f % 2}


def device(at):
    return ((at["x"] // 2) * 8 + at["z"] * 2 + at["c"], at["y"] * 2 + at["x"] % 2)


def shifted(at, axis, k):
    return {**at, axis: (at[axis] + k) % SIZES.get(axis, 4)}


def select(names, fixed, half=None):
    index = []
    for n in names:
        size = SIZES[n]
        if half is not None and n == half[0]:
            index.append(pl.ds(half[1] * (size // 2), size // 2))
        elif n in ("xl", "xh"):
            v = fixed.get("x")
            index.append(pl.ds(0, 2) if v is None else (v % 2 if n == "xl" else v // 2))
        else:
            v = fixed.get(n)
            index.append(pl.ds(0, size) if v is None else v)
    return tuple(index)


def expand(axes):
    return [n for a in axes for n in (("xl", "xh") if a == "x" else (a,))]


def kept(names, axes):
    some = expand(axes)
    return tuple(n for n in names if n in some)


def remote(src, dst, send, recv, to):
    return pltpu.make_async_remote_copy(
        src_ref=src, dst_ref=dst, send_sem=send, recv_sem=recv, device_id=to, device_id_type=MESH
    )


def greeting(at):
    f = lax.axis_index("fsdp")
    s = lax.axis_index("seq")
    bar = pltpu.get_barrier_semaphore()
    peers = [(f, (s + k) % 8) for k in range(1, 8)]
    peers += [(f + 1 - 2 * (f % 2), (s + k) % 8) for k in range(8)]
    peers += [device(shifted(at, "z", k)) for k in (1, 2, 3)]
    peers += [device({**at, "x": (at["x"] + 2) % 4})]
    peers += [device({**at, "x": (at["x"] // 2 * 2 + 2) % 4 + (1 - at["x"] % 2)})]
    for p in peers:
        pl.semaphore_signal(bar, inc=1, device_id=p, device_id_type=MESH)
    return bar, len(peers)


def one_hot(rows, slots, per, size, offset, flip=False):
    shape = (slots * size, rows) if flip else (rows, slots * size)
    i = lax.broadcasted_iota(jnp.int32, shape, 1 if flip else 0)
    j = lax.broadcasted_iota(jnp.int32, shape, 0 if flip else 1)
    return (j == (i // per) * size + offset + i % per).astype(BF16)


def units(core, up, flip=False):
    i = lax.broadcasted_iota(jnp.int32, (384, 384), 1 if flip else 0)
    j = lax.broadcasted_iota(jnp.int32, (384, 384), 0 if flip else 1)
    y, r = (i % 192) // 48, i % 48
    early = y * 32 + r + (128 if up else 0)
    late = y * 16 + r - 32 + (320 if up else 256)
    return ((i // 192 == core) & (j == jnp.where(r < 32, early, late))).astype(BF16)


def as_column(row):
    lane = lax.broadcasted_iota(jnp.int32, (6, 6), 1)
    side = lax.broadcasted_iota(jnp.int32, (6, 6), 0)
    return jnp.sum(jnp.where(lane == side, row.astype(F32), 0.0), axis=1, keepdims=True)


def nn(a, b):
    return jnp.dot(a, b, preferred_element_type=F32)


def nt(a, b):
    return lax.dot_general(a, b, (((1,), (1,)), ((), ())), preferred_element_type=F32)


def tn(a, b):
    return lax.dot_general(a, b, (((0,), (0,)), ((), ())), preferred_element_type=F32)


def norm_factor(values):
    return lax.rsqrt(jnp.mean(values * values, axis=-1, keepdims=True) + EPSILON)


def norm_back(values, factor, e):
    return factor * e - values * (factor * factor * factor * jnp.mean(e * values, axis=-1, keepdims=True))


def swap_halves(v):
    lane = lax.broadcasted_iota(jnp.int32, v.shape, 1)
    return jnp.where(lane % 64 < 32, pltpu.roll(v, 96, 1), pltpu.roll(v, 32, 1))


def digits(names, n):
    out = {}
    for name in reversed(names):
        out[name] = n % SIZES[name]
        n = n // SIZES[name]
    return out


def full_index(names, fixed, free, n):
    got = digits(free, n)
    index = []
    for name in names:
        if name in free:
            index.append(got[name])
        elif name in ("xl", "xh"):
            index.append(fixed["x"] % 2 if name == "xl" else fixed["x"] // 2)
        else:
            index.append(fixed[name])
    return tuple(index)


def count(names):
    return math.prod(SIZES[n] for n in names)


def layer_kernel(
    lens, gain_a, gain_m, tok, cot, w_query, w_key, w_value, w_out, w_gate, w_up, w_down,
    out_o, in_o, rows_o, down_o, attn_o,
    a0, a1, a2, w0, w1, w2, g0, g1, g2, h0, h1, h2,
    xa, xat, r0, rd0, s0, d0, s0b, d0b, ks, vs, qs, ps, att, hid, dhid, dqs, cosine, sine, bias, rdn,
    v2s, cs, oacc, eacc, osum, esum, rdc, toks, out_s, in_s, lens_out, lens_in, sab, rab, *rest
):
    at = place()
    f = lax.axis_index("fsdp")
    s = lax.axis_index("seq")
    xl = at["x"] % 2
    here = at["y"] * 2 + at["c"]
    stays = at["c"] == xl
    partner = (f - at["c"] + xl, here)
    t3, t2, t1 = rest[:3], rest[3:6], rest[6:9]
    sem0s, sem0r, semds, semdr, semxs, semxr, sems, semr, semls, semlr, semcs, semcr, semps, sempr = rest[9:23]
    bem0s, bem0r, bemds, bemdr, bems, bemr, bemls, bemlr, bemcs, bemcr = rest[23:33]
    semms, semmr, semys, semyr, semzs, semzr, semws, semwr, semas, semar = rest[33:]
    attn_weights = (a0, a1, a2)
    weights = (w0, w1, w2)
    own_grads = (g0, g1, g2)
    homes = (h0, h1, h2)
    sibling = device(shifted(at, "c", 1))
    xl = at["x"] % 2
    beside = (f, at["y"] * 2 + 1 - xl)
    bar, others = greeting(at)
    gain_one, gain_two = as_column(gain_a[...]), as_column(gain_m[...])
    for r in range(4):
        lens_out[r : r + 1] = jnp.full((1, 128), lens[0, r], jnp.int32).astype(F32)
    lens_out[4:8] = jnp.zeros((4, 128), F32)
    s0[...] = jnp.zeros_like(s0)
    d0[...] = jnp.zeros_like(d0)
    for b in range(8):
        lanes = pl.ds(b * 384, 384)
        half = pl.ds((b % 2) * 384, 384)
        s0[0, b, 0:6] = w_gate[:, lanes].astype(F32) * gain_two
        s0[1, b, 0:6] = w_up[:, lanes].astype(F32) * gain_two
        if b < 6:
            s0[2, b, 0:6] = (w_query, w_key, w_value)[b // 2][:, half].astype(F32) * gain_one
        else:
            s0[2, b, 0:6] = w_out[:, half].astype(F32)
    for b in range(2):
        d0[b, 0:24] = w_down[:, b * 384 : (b + 1) * 384].astype(F32)
    d0b[...] = d0[...].astype(BF16)
    gate_rows = s0[0].reshape(64, 384).astype(BF16)
    up_rows = s0[1].reshape(64, 384).astype(BF16)
    for core in range(2):
        rows = nn(gate_rows, units(core, False)) + nn(up_rows, units(core, True))
        s0b[core] = jnp.concatenate([rows.reshape(8, 8, 384), s0[2]], axis=1).astype(BF16)

    pl.semaphore_wait(bar, others)

    def group(k, src, dst, sends, recvs):
        me = at["c"] * 8 + s
        to, frm = (me + k) % 16, (me - k + 16) % 16
        peer = (f - at["c"] + to // 8, to % 8)
        send, recv = sends.at[k - 1], recvs.at[k - 1]
        out = remote(src.at[to // 8, to % 8], dst.at[me], send, recv, peer)
        inn = remote(src.at[to // 8, to % 8], dst.at[frm], send, recv, peer)
        return out, inn

    def first(k):
        return group(k, s0b, r0, sem0s, sem0r)

    def swap(buf, n):
        c = at["c"]
        return remote(buf.at[c], buf.at[c], semps.at[n], sempr.at[n], sibling)

    def swapped(buf, n):
        c = at["c"]
        return remote(buf.at[c], buf.at[1 - c], semps.at[n], sempr.at[n], sibling)

    def down_copy(slot):
        return remote(d0b.at[1 - xl], rd0.at[slot], semds, semdr, beside)

    def moves(n):
        src = (tok, cot, lens_out)[n]
        dst = (toks, cs.at[xl], lens_in)[n]
        return remote(src, dst, semms.at[n], semmr.at[n], partner)

    def token_out(y):
        return remote(xa.at[here], xa.at[here], semxs.at[y], semxr.at[at["y"]], (f, y * 2 + xl))

    def token_in(y):
        block = xa.at[y * 2 + at["c"]]
        return remote(block, block, semxs.at[y], semxr.at[y], (f, y * 2 + xl))

    def token_across(y):
        mine, other = xa.at[y * 2 + at["c"]], xa.at[y * 2 + 1 - at["c"]]
        send, recv = semys.at[y], semyr.at[y]
        return remote(mine, mine, send, recv, sibling), remote(other, other, send, recv, sibling)

    for k in range(1, 16):
        first(k)[0].start()
    down_copy(xl).start()

    def move():
        for n in (0, 2):
            moves(n).start()

    def stay():
        toks[...] = tok[...]
        cs[xl] = cot[...]
        lens_in[...] = lens_out[...]

    pl.when(jnp.logical_not(stays))(move)
    pl.when(stays)(stay)
    r0[at["c"] * 8 + s] = s0b[at["c"], s]
    rd0[xl] = d0b[xl]

    def rest(i, part):
        return pl.ds(0, 48) if part == 0 else pl.ds(48, ROWS[i] - 48)

    def split(i):
        return "z" if ORDERS[i][2] == "y" else "y"

    def block(i, fixed, core, rows, half=None):
        where = select(NAMES, fixed, half)
        if rows.start < 48:
            return attn_weights[i].at[where + (core,)]
        return weights[i].at[where + (pl.ds(rows.start - 48, rows.size),)]

    def put(i, first_row, value):
        where = select(NAMES, at)
        if first_row < 48:
            attn_weights[i][where + (at["c"],)] = value
        else:
            weights[i][where + (slice(first_row - 48, first_row - 48 + value.shape[0]),)] = value

    def ring(i, part, phase, k):
        order = ORDERS[i]
        axis = order[phase]
        fixed = {n: at[n] for n in ("x", "y", "z") if n not in order[:phase]}
        theirs = {**fixed, axis: (at[axis] - k + 4) % 4}
        rows = pl.ds(*PARTS[part][i])
        mine, other = block(i, fixed, at["c"], rows), block(i, theirs, at["c"], rows)
        slot = 2 * part + phase
        send, recv = sems.at[i, slot, k - 1], semr.at[i, slot, k - 1]
        to = device(shifted(at, axis, k))
        return remote(mine, mine, send, recv, to), remote(other, other, send, recv, to)

    def direct(i, part, k):
        axis = ORDERS[i][2]
        rows = pl.ds(*PARTS[part][i])
        mine = block(i, {axis: at[axis]}, at["c"], rows)
        other = block(i, {axis: (at[axis] - k + 4) % 4}, at["c"], rows)
        send, recv = semls.at[i, part, k - 1], semlr.at[i, part, k - 1]
        to = device(shifted(at, axis, k))
        return remote(mine, mine, send, recv, to), remote(other, other, send, recv, to)

    def relay(i, part, way):
        axis = ORDERS[i][2]
        half, rows = (split(i), way), pl.ds(*PARTS[part][i])
        mine = block(i, {axis: (at[axis] + (3, 1)[way]) % 4}, at["c"], rows, half)
        other = block(i, {axis: (at[axis] + 2) % 4}, at["c"], rows, half)
        send, recv = semls.at[i, part, (1, 3)[way]], semlr.at[i, part, (1, 3)[way]]
        to = device(shifted(at, axis, (1, 3)[way]))
        return remote(mine, mine, send, recv, to), remote(other, other, send, recv, to)

    def across(i, k):
        axis = ORDERS[i][2]
        where = {axis: (at[axis] + k) % 4}
        mine, other = block(i, where, at["c"], rest(i, 0)), block(i, where, 1 - at["c"], rest(i, 0))
        send, recv = semcs.at[i, k], semcr.at[i, k]
        return remote(mine, mine, send, recv, sibling), remote(other, other, send, recv, sibling)

    def start(part, phase):
        for k in (1, 3, 2):
            for i in FULL:
                ring(i, part, phase, k)[0].start()

    def arrive(part, phase):
        for k in (1, 3, 2):
            for i in FULL:
                ring(i, part, phase, k)[1].wait_recv()

    def start_last(part):
        for k in (1, 3) if part else (1, 3, 2):
            for i in PARTS[part]:
                direct(i, part, k)[0].start()

    def pass_last(part):
        for way in range(2):
            for i in PARTS[part]:
                direct(i, part, (1, 3)[way])[1].wait_recv()
                relay(i, part, way)[0].start()

    def arrive_last(part):
        for i in PARTS[part]:
            if part:
                for way in range(2):
                    relay(i, part, way)[1].wait_recv()
            else:
                for k in (1, 3, 2):
                    direct(i, part, k)[1].wait_recv()
                    across(i, (4 - k) % 4)[0].start()

    def sent(part):
        for i in PARTS[part]:
            for k in (1, 3) if part else (1, 2, 3):
                direct(i, part, k)[0].wait_send()
            if part:
                for way in range(2):
                    relay(i, part, way)[0].wait_send()

    for k in range(1, 16):
        first(k)[1].wait_recv()
    flat = r0[...].reshape(256, 384)
    piece = nn(one_hot(48, 16, 6, 16, at["c"] * 128 + 8), flat).astype(BF16)
    for i in range(3):
        put(i, 0, piece[:, i * 128 : (i + 1) * 128])
    start(0, 0)
    piece = nn(one_hot(96, 16, 6, 16, 0), flat).astype(BF16)
    put(0, 48, piece[:, :128])
    put(0, 144, piece[:64, 256:])
    put(1, 48, piece[:, 128:256])
    put(1, 144, piece[64:80, 256:])
    put(2, 192, piece[80:, 256:])
    down_copy(1 - xl).wait_recv()
    piece = nn(one_hot(48, 2, 24, 32, 0), rd0[...].reshape(64, 384)).astype(BF16)
    for b in range(3):
        lanes = slice(b * 128, (b + 1) * 128)
        put(2, 48 + 32 * b, piece[:32, lanes])
        put(2, 144 + 16 * b, piece[32:, lanes])
    start(1, 0)
    start(2, 0)

    def arrived():
        for n in (0, 2):
            moves(n).wait()
        moves(1).start()

    pl.when(jnp.logical_not(stays))(arrived)
    inputs = toks[...].astype(F32)
    xa[here] = (inputs * norm_factor(inputs)).astype(BF16)
    for y in range(1, 4):
        pl.when(y > at["y"])(lambda y=y: token_out(y).start())
    pl.when(at["c"] == 0)(lambda: token_across(at["y"])[0].start())
    arrive(0, 0)
    start(0, 1)
    arrive(1, 0)
    start(1, 1)
    arrive(0, 1)
    start_last(0)
    for i in ATTN:
        across(i, 0)[0].start()
    arrive(1, 1)
    start_last(1)
    arrive(2, 0)
    start(2, 1)

    ends = [lens_in[0:1, :]]
    for r in (1, 2):
        ends.append(ends[-1] + lens_in[r : r + 1, :])
    freq_lane = (lax.broadcasted_iota(jnp.int32, (1, 128), 1) % 32).astype(F32)
    freqs = jnp.exp(freq_lane * (-2.0 * math.log(ROPE_BASE) / HEAD_DIM))
    lane = lax.broadcasted_iota(jnp.int32, (128, 128), 1)

    def segment_of(index):
        return sum(jnp.where(index >= e, 1.0, 0.0) for e in ends)

    def table(u, carry):
        index = (u * 128 + lax.broadcasted_iota(jnp.int32, (128, 128), 0)).astype(F32)
        begin = jnp.zeros_like(index)
        for e in ends:
            begin = jnp.where(index >= e, e, begin)
        angle = (index - begin) * freqs
        rows = pl.ds(pl.multiple_of(u * 128, 128), 128)
        cosine[rows, :] = jnp.cos(angle)
        sine[rows, :] = jnp.where(lane % 64 < 32, -1.0, 1.0) * jnp.sin(angle)
        mine = (here * 128 + lax.broadcasted_iota(jnp.int32, (1, 128), 1)).astype(F32)
        allowed = (segment_of(index) == segment_of(mine)) & (index <= mine)
        bias[rows, :] = jnp.where(allowed, 0.0, MASKED_SCORE)
        return carry

    lax.fori_loop(0, 8, table, 0)


    for u in range(1, 8):

        def clear(u=u):
            xa[u] = jnp.zeros((128, 768), BF16)

        pl.when(u > here)(clear)
    for y in range(3):

        def pass_on(y=y):
            token_in(y).wait_recv()
            token_across(y)[0].start()

        pl.when(y < at["y"])(pass_on)
    for y in range(3):
        pl.when(y < at["y"])(lambda y=y: token_across(y)[1].wait_recv())
    pl.when(at["c"] == 1)(lambda: token_across(at["y"])[1].wait_recv())

    def transpose_tokens(u, carry):
        xat[:, pl.ds(pl.multiple_of(u * 128, 128), 128)] = xa[u].T
        return carry

    lax.fori_loop(0, 8, transpose_tokens, 0)
    arrive_last(0)
    for k in range(4):
        for i in ATTN:
            across(i, k)[1].wait_recv()

    for k in range(1, 16):
        first(k)[0].wait_send()
    down_copy(xl).wait_send()
    for y in range(1, 4):
        pl.when(y > at["y"])(lambda y=y: token_out(y).wait_send())
    for y in range(3):
        pl.when(y < at["y"])(lambda y=y: token_across(y)[0].wait_send())
    pl.when(at["c"] == 0)(lambda: token_across(at["y"])[0].wait_send())

    mine = pl.ds(pl.multiple_of(here * 128, 128), 128)
    cos_mine, sin_mine = cosine[mine, :], sine[mine, :]
    left = lax.broadcasted_iota(jnp.int32, (128, 128), 1) < 64

    def attn_weight(kind, t, h):
        return attn_weights[t][kind, h].reshape(768, 128)

    def put_grad(kind, t, h, value):
        own_grads[t][kind, h] = value.reshape(2, 4, 2, 48, 128)

    def attn_full(kind):
        return jnp.concatenate([attn_weight(kind, p % 3, p // 3) for p in range(6)], axis=1)

    def stacked(v):
        zero = jnp.zeros_like(v)
        return jnp.concatenate([jnp.where(left, v, zero), jnp.where(left, zero, v)], axis=0)

    def unstacked(v):
        return jnp.concatenate([v[:64, :128], v[64:, 128:]], axis=0).T

    def pair_lanes(p):
        return pl.ds(pl.multiple_of(p * 128, 128), 128)

    def attend(t, h):
        p = t + 3 * h
        tokens_all = xa[...].reshape(1024, 768)
        w_kv = jnp.concatenate([attn_weight(1, t, h), attn_weight(2, t, h)], axis=1)
        kv = nn(tokens_all, w_kv)
        k_raw = kv[:, :128]
        k = (k_raw * cosine[...] + swap_halves(k_raw) * sine[...]).astype(BF16)
        v = kv[:, 128:].astype(BF16)
        q_raw = nn(xa[here], attn_weight(0, t, h))
        q = ((q_raw * cos_mine + swap_halves(q_raw) * sin_mine).astype(BF16) * (1.0 / math.sqrt(HEAD_DIM))).astype(BF16)
        qq = stacked(q)
        ks[p] = k
        vs[p] = v
        qs[p] = qq
        masks = bias[...]
        scores = nt(k, qq) + jnp.concatenate([masks, masks], axis=1)
        top = jnp.max(scores, axis=0, keepdims=True)
        e = jnp.exp(scores - top)
        total = jnp.sum(e, axis=0, keepdims=True)
        probs = (e * (1.0 / total)).astype(BF16)
        ps[p] = probs
        att[:, pair_lanes(p)] = unstacked(tn(v, probs)).astype(BF16)

    for t in range(3):

        def attend_third(h, carry, t=t):
            attend(t, h)
            return carry

        lax.fori_loop(0, 2, attend_third, 0)
        if t == 0:
            pass_last(1)
        if t == 1:
            arrive(2, 1)
            start_last(2)


    hidden = toks[...].astype(F32) + nn(att[...], attn_full(3))
    hid[...] = hidden
    factor_two = norm_factor(hidden)
    v2s[at["c"]] = (hidden * factor_two).astype(BF16)
    swap(v2s, 1).start()
    pl.when(jnp.logical_not(stays))(lambda: moves(1).wait())
    swap(cs, 0).start()
    oacc[...] = jnp.zeros_like(oacc)
    eacc[...] = jnp.zeros_like(eacc)
    swapped(cs, 0).wait()
    swapped(v2s, 1).wait()
    v2 = v2s[...].reshape(256, 768)
    v2t = v2.T

    def pair(a, b):
        return jnp.concatenate([a, b], axis=1)

    def gated(gate, up, d_w):
        c = cs[...].reshape(256, 768)
        sig = 1.0 / (1.0 + jnp.exp(-gate))
        silu = gate * sig
        mixed = (silu * up).astype(BF16)
        oacc[...] += nn(mixed, d_w).reshape(2, 128, 768)
        d_mixed = nt(c, d_w)
        d_gate = d_mixed * up * sig * (1.0 + gate * (1.0 - sig))
        d_up = d_mixed * silu
        return d_gate, d_up, tn(mixed, c).astype(BF16)

    def down_rows(xh, z, first_row, rows):
        def part(b, h, n):
            some = pl.ds(first_row - 48 + n * rows, rows)
            return w2[:, h, xh, z + b, some].reshape(4 * rows, 128)

        return jnp.concatenate(
            [jnp.concatenate([part(b, h, n) for h in range(2) for n in range(3)], axis=1) for b in range(2)], axis=0
        )

    def put_down(xh, z, first_row, rows, g):
        for b in range(2):
            for h in range(2):
                for n in range(3):
                    some = pl.ds(first_row + n * rows, rows)
                    lanes = slice(h * 384 + n * 128, h * 384 + (n + 1) * 128)
                    h2[:, h, xh, z + b, some] = g[b * 4 * rows : (b + 1) * 4 * rows, lanes].reshape(4, rows, 128)

    def feed_early(y, carry):
        g_w = pair(*(w0[y, b, :, :, 0:96].reshape(768, 128) for b in range(2)))
        u_w = pair(*(w1[y, b, :, :, 0:96].reshape(768, 128) for b in range(2)))
        xh, z = y // 2, (y % 2) * 2
        d_w = down_rows(xh, z, 48, 32)
        d_gate, d_up, g_d = gated(nn(v2, g_w), nn(v2, u_w), d_w)
        d_gate, d_up = d_gate.astype(BF16), d_up.astype(BF16)
        eacc[...] += (nt(d_gate, g_w) + nt(d_up, u_w)).reshape(2, 128, 768)
        g_g = nn(v2t, d_gate).astype(BF16)
        g_u = nn(v2t, d_up).astype(BF16)
        for b in range(2):
            lanes = slice(b * 128, (b + 1) * 128)
            h0[y, b, :, :, 48:144] = g_g[:, lanes].reshape(2, 4, 96, 128)
            h1[y, b, :, :, 48:144] = g_u[:, lanes].reshape(2, 4, 96, 128)
        put_down(xh, z, 48, 32, g_d)
        return carry

    def feed_late(y, carry):
        def weight(b):
            rows = (w0[y, b, :, :, 96:160], w1[y, b, :, :, 96:112], w2[y, b, :, :, 144:160])
            return jnp.concatenate(rows, axis=2).reshape(768, 128)

        w = pair(weight(0), weight(1))
        xh, z = y // 2, (y % 2) * 2
        d_w = down_rows(xh, z, 144, 16)
        both = nn(v2, w)
        low = lax.broadcasted_iota(jnp.int32, (256, 128), 1) < 64

        def mix(a, b):
            return jnp.where(low, a, pltpu.roll(b, 64, 1)), jnp.where(low, pltpu.roll(a, 64, 1), b)

        gate, up = mix(both[:, :128], both[:, 128:])
        d_gate, d_up, g_d = gated(gate, up, d_w)
        d_both = pair(*mix(d_gate, d_up)).astype(BF16)
        eacc[...] += nt(d_both, w).reshape(2, 128, 768)
        g = nn(v2t, d_both).astype(BF16)
        for b in range(2):
            rows = g[:, b * 128 : (b + 1) * 128].reshape(2, 4, 96, 128)
            h0[y, b, :, :, 144:208] = rows[:, :, :64]
            h1[y, b, :, :, 144:160] = rows[:, :, 64:80]
            h2[y, b, :, :, 192:208] = rows[:, :, 80:]
        put_down(xh, z, 144, 16, g_d)
        return carry

    def home(i, fixed, part=None, half=None):
        first_row, rows = (0, ROWS[i]) if part is None else PARTS[part][i]
        return homes[i].at[select(NAMES, fixed, half) + (pl.ds(first_row, rows),)]

    def share(i, k):
        where = {ORDERS[i][2]: (at[ORDERS[i][2]] + k) % 4}
        part = own_grads[i].at[select(NAMES, where) + (1 - at["c"],)]
        return remote(part, home(i, where, 0), bemcs.at[i, k], bemcr.at[i, k], sibling)

    def add_core(i, k):
        order = ORDERS[i]
        free = kept(NAMES, order[:2])
        fixed = {order[2]: (at[order[2]] + k) % 4}
        rows = pl.ds(*ATTN[i])

        def body(n, carry):
            index = full_index(NAMES, fixed, free, n)
            total = homes[i][index + (rows,)].astype(F32) + own_grads[i][index + (at["c"],)].astype(F32)
            homes[i][index + (rows,)] = total.astype(BF16)
            return carry

        lax.fori_loop(0, count(free), body, 0, unroll=4)

    def halfway(i, part, way):
        axis = ORDERS[i][2]
        half = (split(i), way)
        src = home(i, {axis: (at[axis] + 2) % 4}, part, half)
        dst = t3[i].at[(1,) + select(kept(NAMES, ORDERS[i][:2]), {}, half) + (pl.ds(*PARTS[part][i]),)]
        send, recv = bemls.at[i, part, way], bemlr.at[i, part, way]
        return remote(src, dst, send, recv, device(shifted(at, axis, (1, 3)[way])))

    def whole(i, part, way):
        axis = ORDERS[i][2]
        src = home(i, {axis: (at[axis] + (1, 3)[way]) % 4}, part)
        dst = t3[i].at[2 * way, :, :, :, pl.ds(*PARTS[part][i])] if ORDERS[i][2] != "x" else t3[i].at[
            2 * way, :, :, pl.ds(*PARTS[part][i])
        ]
        send, recv = bemls.at[i, part, 2 + way], bemlr.at[i, part, 2 + way]
        return remote(src, dst, send, recv, device(shifted(at, axis, (1, 3)[way])))

    def add_half(i, part, way):
        order = ORDERS[i]
        where = split(i)
        free = kept(NAMES, order[:2])
        turned = (where,) + tuple(m for m in free if m != where)
        fixed = {order[2]: (at[order[2]] + (1, 3)[way]) % 4}
        rows = pl.ds(*PARTS[part][i])

        def body(n, carry):
            got = digits(turned, n)
            got[where] = got[where] + way * (SIZES[where] // 2)
            n = 0
            for m in free:
                n = n * SIZES[m] + got[m]
            index = full_index(NAMES, fixed, free, n) + (rows,)
            came = t3[i][(1,) + tuple(got[m] for m in free) + (rows,)]
            homes[i][index] = (homes[i][index].astype(F32) + came.astype(F32)).astype(BF16)
            return carry

        lax.fori_loop(0, count(free) // 2, body, 0, unroll=4)

    def add_whole(i, part):
        order = ORDERS[i]
        free = kept(NAMES, order[:2])
        fixed = {order[2]: at[order[2]]}
        rows = pl.ds(*PARTS[part][i])

        def body(n, carry):
            index = full_index(NAMES, fixed, free, n) + (rows,)
            there = full_index(free, {}, free, n) + (rows,)
            total = homes[i][index].astype(F32)
            for k in (0, 2) if part else (0, 1, 2):
                total = total + t3[i][(k,) + there].astype(F32)
            homes[i][index] = total.astype(BF16)
            return carry

        lax.fori_loop(0, count(free), body, 0, unroll=4)

    def hop(i, part, left, k):
        order = ORDERS[i]
        axis = order[left - 1]
        fixed = {a: at[a] for a in order[left:]}
        rows = rest(i, part)
        src = homes[i].at[select(NAMES, {**fixed, axis: (at[axis] + k) % 4}) + (rows,)]
        if left == 1:
            dst = t1[i].at[k - 1, rows]
        else:
            dst = t2[i].at[(k - 1,) + select(kept(NAMES, order[:1]), {}) + (rows,)]
        slot = 2 * part + left - 1
        send, recv = bems.at[i, slot, k - 1], bemr.at[i, slot, k - 1]
        return remote(src, dst, send, recv, device(shifted(at, axis, k)))

    def add_ring(i, part):
        order = ORDERS[i]
        free = kept(NAMES, order[:1])
        fixed = {a: at[a] for a in order[1:]}
        rows = rest(i, part)

        def body(n, carry):
            index = full_index(NAMES, fixed, free, n) + (rows,)
            total = homes[i][index].astype(F32)
            for k in range(3):
                total = total + t2[i][(k,) + full_index(free, {}, free, n) + (rows,)].astype(F32)
            homes[i][index] = total.astype(BF16)
            return carry

        lax.fori_loop(0, count(free), body, 0)

    def hop_start(part):
        for k in (1, 3, 2):
            for i in FULL:
                hop(i, part, 2, k).start()

    def hop_on(part):
        for i in FULL:
            for k in (1, 3, 2):
                hop(i, part, 2, k).wait_recv()
            add_ring(i, part)
            for k in (1, 3, 2):
                hop(i, part, 1, k).start()

    def last(i, part):
        for k in (1, 3, 2):
            hop(i, part, 1, k).wait_recv()
        rows = rest(i, part)
        total = homes[i][select(NAMES, at) + (rows,)].astype(F32)
        for k in range(3):
            total = total + t1[i][k, rows].astype(F32)
        return total.astype(BF16)

    def hop_last(i, k):
        axis = ORDERS[i][2]
        src = home(i, {axis: (at[axis] + k) % 4}, 0)
        rows = pl.ds(*ATTN[i])
        dst = t3[i].at[(k - 1,) + select(kept(NAMES, ORDERS[i][:2]), {}) + (rows,)]
        send, recv = bemls.at[i, 0, k - 1], bemlr.at[i, 0, k - 1]
        return remote(src, dst, send, recv, device(shifted(at, axis, k)))

    def half_start(part, items=FULL):
        for way in range(2):
            for i in items:
                if i in PARTS[part]:
                    halfway(i, part, way).start()

    def half_on(part, items=FULL):
        for way in range(2):
            for i in items:
                if i in PARTS[part]:
                    halfway(i, part, way).wait_recv()
                    add_half(i, part, way)
                    whole(i, part, way).start()

    def whole_on(part):
        for i in PARTS[part]:
            if part:
                for way in range(2):
                    whole(i, part, way).wait_recv()
            else:
                for k in (1, 3, 2):
                    hop_last(i, k).wait_recv()
            add_whole(i, part)

    for i in FULL:
        for part in range(3):
            for phase in range(2):
                for k in (1, 2, 3):
                    ring(i, part, phase, k)[0].wait_send()
    arrive_last(1)
    feed_early(0, 0)
    pass_last(2)
    for y in range(1, 4):
        feed_early(y, 0)
    half_start(1)
    arrive_last(2)
    for y in range(4):
        feed_late(y, 0)
    sum_o = remote(oacc.at[1 - at["c"]], osum, semps.at[2], sempr.at[2], sibling)
    sum_e = remote(eacc.at[1 - at["c"]], esum, semps.at[3], sempr.at[3], sibling)
    sum_e.start()
    sum_o.start()
    half_start(2)
    half_on(1)
    sum_e.wait()

    hidden = hid[...]
    factor_two = norm_factor(hidden)
    d_hidden = cs[at["c"]].astype(F32) + norm_back(hidden, factor_two, eacc[at["c"]] + esum[...])
    dhid[...] = d_hidden
    dh = d_hidden.astype(BF16)
    d_att = nt(dh, attn_full(3)).astype(BF16)
    att_t = att[...].T
    for j in range(2):
        g_o = nn(att_t, dh[:, j * 384 : (j + 1) * 384]).astype(BF16)
        for t in range(3):
            put_grad(3, t, j, g_o[:, t * 128 : (t + 1) * 128])
    att[...] = d_att

    def attend_back(t, h):
        p = t + 3 * h
        da = stacked(att[:, pair_lanes(p)])
        k, v, qq, probs = ks[p], vs[p], qs[p], ps[p]
        d_probs = nt(v, da)
        probs_f = probs.astype(F32)
        d_sum = jnp.sum(probs_f * d_probs, axis=0, keepdims=True)
        d_scores = (probs_f * (d_probs - d_sum)).astype(BF16)
        d_v = nn(probs, da).astype(BF16)
        d_k = nn(d_scores, qq)
        d_k = (d_k * cosine[...] - swap_halves(d_k) * sine[...]).astype(BF16)
        d_q = unstacked(tn(k, d_scores)) * (1.0 / math.sqrt(HEAD_DIM))
        d_q = (d_q * cos_mine - swap_halves(d_q) * sin_mine).astype(BF16)
        ks[p] = d_k
        vs[p] = d_v
        dqs[:, pair_lanes(p)] = d_q
        g_kv = nn(xat[...], jnp.concatenate([d_k, d_v], axis=1)).astype(BF16)
        g_q = nn(xat[:, mine], d_q).astype(BF16)
        put_grad(0, t, h, g_q)
        put_grad(1, t, h, g_kv[:, :128])
        put_grad(2, t, h, g_kv[:, 128:])

    def share_on(i):
        for k in (2, 1, 3, 0):
            share(i, k).wait_recv()
            add_core(i, k)
            if k:
                hop_last(i, k).start()

    half_on(2)
    def third_back(h, carry):
        attend_back(0, h)
        return carry

    attend_back(0, 0)
    attend_back(0, 1)

    def share_start(i):
        for k in (2, 1, 3, 0):
            share(i, k).start()

    share_start(0)
    attend_back(1, 0)
    share_on(0)
    attend_back(1, 1)
    share_start(1)
    attend_back(2, 0)
    share_on(1)
    attend_back(2, 1)
    share_start(2)
    whole_on(1)
    share_on(2)
    whole_on(2)
    hop_start(1)

    w_kv = jnp.concatenate([attn_full(1), attn_full(2)], axis=1)

    def tokens_back(u, carry):
        rows = pl.ds(pl.multiple_of(u * 128, 128), 128)
        d_kv = jnp.concatenate([ks[p, rows, :] for p in range(6)] + [vs[p, rows, :] for p in range(6)], axis=1)
        xa[u] = nt(d_kv, w_kv).astype(BF16)
        return carry

    lax.fori_loop(0, 8, tokens_back, 0)

    def grad_across(y):
        mine = xa.at[y * 2 + 1 - at["c"]]
        return remote(mine, rdc.at[y], semzs.at[y], semzr.at[y], sibling)

    def grad_out(y):
        return remote(xa.at[y * 2 + at["c"]], rdn.at[at["y"]], semws.at[y], semwr.at[at["y"]], (f, y * 2 + xl))

    def grad_in(y):
        return remote(xa.at[y * 2 + at["c"]], rdn.at[y], semws.at[y], semwr.at[y], (f, y * 2 + xl))

    for y in range(3):
        pl.when(y < at["y"])(lambda y=y: grad_across(y).start())
    pl.when(at["c"] == 1)(lambda: grad_across(at["y"]).start())
    for y in range(3):

        def add_across(y=y):
            grad_across(y).wait_recv()
            block = xa[y * 2 + at["c"]].astype(F32) + rdc[y].astype(F32)
            xa[y * 2 + at["c"]] = block.astype(BF16)
            grad_out(y).start()

        pl.when(y < at["y"])(add_across)
    sum_o.wait()
    out_s[...] = (hid[...] + oacc[at["c"]] + osum[...]).astype(BF16)

    def out_move():
        return remote(out_s, out_o, semms.at[3], semmr.at[3], partner)

    def out_stay():
        out_o[...] = out_s[...]

    pl.when(jnp.logical_not(stays))(lambda: out_move().start())
    pl.when(stays)(out_stay)
    esum[...] = nt(dqs[...], attn_full(0))

    hop_on(1)
    whole_on(0)
    hop_start(0)
    sum0, sum1, sum2 = last(0, 1), last(1, 1), last(2, 1)
    down = jnp.concatenate(
        [
            jnp.concatenate([sum2[a + b * n : a + b * (n + 1)] for n in range(3)], axis=1)
            for a, b in ((0, 32), (96, 16))
        ],
        axis=0,
    )
    mixed_units = jnp.concatenate([sum0[96:160], sum1[96:112], sum2[144:160]], axis=0)
    both = jnp.concatenate([sum0[0:96], sum1[0:96], mixed_units], axis=1)
    rows_mlp = nn(one_hot(96, 16, 6, 16, 0, True), both)
    d0b[...] = nn(one_hot(48, 2, 24, 32, 0, True), down).astype(BF16).reshape(2, 32, 384)
    s0b[...] = rows_mlp.astype(BF16).reshape(2, 8, 16, 384)

    def final(k):
        return group(k, s0b, r0, bem0s, bem0r)

    def final_down(slot):
        return remote(d0b.at[1 - xl], rd0.at[slot], bemds, bemdr, beside)

    for k in range(1, 16):
        final(k)[0].start()
    final_down(xl).start()
    hop_on(0)

    esum[...] += xa[here].astype(F32)

    def add_own():
        grad_across(at["y"]).wait_recv()
        esum[...] += rdc[at["y"]].astype(F32)

    pl.when(at["c"] == 0)(add_own)
    for y in range(1, 4):

        def add(y=y):
            grad_in(y).wait_recv()
            esum[...] += rdn[y].astype(F32)

        pl.when(y > at["y"])(add)
    inputs = toks[...].astype(F32)
    in_s[...] = dhid[...] + norm_back(inputs, norm_factor(inputs), esum[...])

    def in_move():
        return remote(in_s, in_o, semms.at[4], semmr.at[4], partner)

    def in_stay():
        in_o[...] = in_s[...]

    pl.when(jnp.logical_not(stays))(lambda: in_move().start())
    pl.when(stays)(in_stay)
    attn = jnp.concatenate([last(i, 0) for i in range(3)], axis=1)
    rows = nn(one_hot(48, 8, 6, 16, 0, True), attn)
    sab[...] = rows.astype(BF16).reshape(8, 16, 384)

    def final_attn(k):
        to, frm = (s + k) % 8, (s - k + 8) % 8
        out = remote(sab.at[to], rab.at[s], semas.at[k - 1], semar.at[k - 1], (f, to))
        inn = remote(sab.at[to], rab.at[frm], semas.at[k - 1], semar.at[k - 1], (f, to))
        return out, inn

    for k in range(1, 8):
        final_attn(k)[0].start()
    rab[s] = sab[s]
    r0[at["c"] * 8 + s] = s0b[at["c"], s]
    rd0[xl] = d0b[xl]
    for k in range(1, 16):
        final(k)[1].wait_recv()
    final_down(1 - xl).wait_recv()
    rows_o[...] = r0[...]
    down_o[...] = rd0[...]
    for k in range(1, 8):
        final_attn(k)[1].wait_recv()
    attn_o[...] = rab[...]
    for k in range(1, 16):
        final(k)[0].wait_send()
    for k in range(1, 8):
        final_attn(k)[0].wait_send()
    final_down(xl).wait_send()
    for y in range(3):

        def across_sent(y=y):
            grad_across(y).wait_send()
            grad_out(y).wait_send()

        pl.when(y < at["y"])(across_sent)
    pl.when(at["c"] == 1)(lambda: grad_across(at["y"]).wait_send())

    def moved():
        out_move().wait()
        in_move().wait()

    pl.when(jnp.logical_not(stays))(moved)
    for part in range(3):
        sent(part)
    for i in ATTN:
        for k in range(4):
            across(i, k)[0].wait_send()
            share(i, k).wait_send()
    for i in ATTN:
        for k in (1, 2, 3):
            hop_last(i, k).wait_send()
    for part in (1, 2):
        for i in PARTS[part]:
            for way in range(2):
                halfway(i, part, way).wait_send()
                whole(i, part, way).wait_send()
    for part in range(2):
        for i in FULL:
            for left in (2, 1):
                for k in (1, 2, 3):
                    hop(i, part, left, k).wait_send()


def finish_kernel(gain_a, gain_m, w_query, w_key, w_value, w_gate, w_up, rows_i, down_i, attn_i, out_i, in_i,
                  out_o, in_o, ga1_o, gq_o, gk_o, gv_o, go_o, ga2_o, gg_o, gu_o, gd_o, s0):
    out_o[...] = out_i[...]
    in_o[...] = in_i[...]
    def as_row(col):
        lane = lax.broadcasted_iota(jnp.int32, (6, 6), 1)
        side = lax.broadcasted_iota(jnp.int32, (6, 6), 0)
        return jnp.sum(jnp.where(lane == side, col, 0.0), axis=0, keepdims=True)

    gain_one, gain_two = as_column(gain_a[...]), as_column(gain_m[...])
    got = rows_i[...].reshape(2, 8, 16, 384)
    halves = [got[core, :, :8].reshape(64, 384) for core in range(2)]
    for which in range(2):
        natural = nn(halves[0], units(0, which == 1, True)) + nn(halves[1], units(1, which == 1, True))
        s0[which] = natural.reshape(8, 8, 384)
    s0[2] = attn_i[:, 0:8, :].astype(F32)
    down = down_i[...].astype(F32)
    gain_sum_one = jnp.zeros((6, 1), F32)
    gain_sum_two = jnp.zeros((6, 1), F32)
    for b in range(8):
        lanes = pl.ds(b * 384, 384)
        half = pl.ds((b % 2) * 384, 384)
        h_gate, h_up, h_attn = s0[0, b, 0:6], s0[1, b, 0:6], s0[2, b, 0:6]
        gg_o[:, lanes] = h_gate * gain_two
        gu_o[:, lanes] = h_up * gain_two
        gain_sum_two += jnp.sum(h_gate * w_gate[:, lanes].astype(F32), axis=1, keepdims=True)
        gain_sum_two += jnp.sum(h_up * w_up[:, lanes].astype(F32), axis=1, keepdims=True)
        if b < 6:
            (gq_o, gk_o, gv_o)[b // 2][:, half] = h_attn * gain_one
            raw = (w_query, w_key, w_value)[b // 2][:, half].astype(F32)
            gain_sum_one += jnp.sum(h_attn * raw, axis=1, keepdims=True)
        else:
            go_o[:, half] = h_attn
    for b in range(2):
        gd_o[:, b * 384 : (b + 1) * 384] = down[b, 0:24]
    ga1_o[...] = as_row(gain_sum_one)
    ga2_o[...] = as_row(gain_sum_two)


VMEM_SPEC = pl.BlockSpec(memory_space=pltpu.VMEM)
SMEM_SPEC = pl.BlockSpec(memory_space=pltpu.SMEM)
DMA = pltpu.SemaphoreType.DMA


def layer(lens, *arrays):
    outs = [((128, 768), BF16), ((128, 768), F32), ((16, 16, 384), BF16), ((2, 32, 384), BF16), ((8, 16, 384), BF16)]
    sizes = tuple(SIZES[n] for n in NAMES)
    scratch = [(sizes + (2, 48, 128), BF16) for _ in ROWS] + [(sizes + (r - 48, 128), BF16) for r in ROWS]
    scratch += [(sizes + (2, 48, 128), BF16) for _ in ROWS]
    scratch += [(sizes + (r, 128), BF16) for r in ROWS]
    scratch += [
        ((8, 128, 768), BF16), ((768, 1024), BF16), ((16, 16, 384), BF16), ((2, 32, 384), BF16),
        ((3, 8, 8, 384), F32), ((2, 32, 384), F32), ((2, 8, 16, 384), BF16), ((2, 32, 384), BF16),
        ((6, 1024, 128), BF16), ((6, 1024, 128), BF16), ((6, 256, 128), BF16), ((6, 1024, 256), BF16),
        ((128, 768), BF16), ((128, 768), F32), ((128, 768), F32), ((128, 768), BF16),
        ((1024, 128), F32), ((1024, 128), F32), ((1024, 128), F32), ((4, 128, 768), BF16),
        ((2, 128, 768), BF16), ((2, 128, 768), BF16), ((2, 128, 768), F32), ((2, 128, 768), F32),
        ((128, 768), F32), ((128, 768), F32), ((4, 128, 768), BF16), ((128, 768), BF16), ((128, 768), BF16), ((128, 768), F32),
        ((8, 128), F32), ((8, 128), F32), ((8, 16, 384), BF16), ((8, 16, 384), BF16),
    ]
    for rings in (2, 1, 0):
        for i in range(3):
            left = tuple(SIZES[n] for n in kept(NAMES, ORDERS[i][:rings]))
            scratch.append(((3,) + left + (ROWS[i], 128), BF16))
    copies = [
        DMA((15,)), DMA((15,)), DMA, DMA, DMA((4,)), DMA((4,)),
        DMA((3, 6, 3)), DMA((3, 6, 3)), DMA((3, 3, 4)), DMA((3, 3, 4)), DMA((3, 4)), DMA((3, 4)), DMA((4,)), DMA((4,)),
        DMA((15,)), DMA((15,)), DMA, DMA,
        DMA((3, 4, 3)), DMA((3, 4, 3)), DMA((3, 3, 4)), DMA((3, 3, 4)), DMA((3, 4)), DMA((3, 4)),
        DMA((5,)), DMA((5,)), DMA((4,)), DMA((4,)), DMA((4,)), DMA((4,)), DMA((4,)), DMA((4,)), DMA((7,)), DMA((7,)),
    ]
    return pl.pallas_call(
        layer_kernel,
        out_shape=[jax.ShapeDtypeStruct(shape, kind) for shape, kind in outs],
        in_specs=[SMEM_SPEC] + [VMEM_SPEC] * 11,
        out_specs=[VMEM_SPEC] * len(outs),
        scratch_shapes=[pltpu.VMEM(shape, kind) for shape, kind in scratch] + copies,
        compiler_params=pltpu.CompilerParams(collective_id=0, has_side_effects=True, vmem_limit_bytes=VMEM_LIMIT),
        name="layer",
    )(lens, *arrays)


def finish(*arrays):
    outs = [
        ((128, 768), BF16), ((128, 768), F32), ((1, 6), F32),
        ((6, 768), F32), ((6, 768), F32), ((6, 768), F32), ((6, 768), F32),
        ((1, 6), F32), ((6, 3072), F32), ((6, 3072), F32), ((24, 768), F32),
    ]
    return pl.pallas_call(
        finish_kernel,
        out_shape=[jax.ShapeDtypeStruct(shape, kind) for shape, kind in outs],
        in_specs=[VMEM_SPEC] * 12,
        out_specs=[VMEM_SPEC] * len(outs),
        scratch_shapes=[pltpu.VMEM((3, 8, 8, 384), F32)],
        name="finish",
    )(*arrays)


def per_device(tokens, doc_lengths, attn_gain, w_query, w_key, w_value, w_out, mlp_gain, w_gate, w_up, w_down, cotangent):
    gains = (attn_gain.reshape(1, 6), mlp_gain.reshape(1, 6))
    layer_out, input_grad, rows, down, rows_attn = layer(
        doc_lengths, *gains, tokens[0], cotangent[0], w_query, w_key, w_value, w_out, w_gate, w_up, w_down
    )
    out = finish(*gains, w_query, w_key, w_value, w_gate, w_up, rows, down, rows_attn, layer_out, input_grad)
    return (out[0][None], out[1][None], out[2][0]) + tuple(out[3:7]) + (out[7][0],) + tuple(out[8:])


def solution(mesh):
    rows = P(("fsdp", "seq"), None)
    gain = P(("fsdp", "seq"))
    toks = P("fsdp", "seq", None)
    return jax.shard_map(
        per_device,
        mesh=mesh,
        in_specs=(toks, P("fsdp", None), gain, rows, rows, rows, rows, gain, rows, rows, rows, toks),
        out_specs=(toks, toks, gain, rows, rows, rows, rows, gain, rows, rows, rows),
        check_vma=False,
    )
```

```python
import math

import jax
import jax.numpy as jnp
from jax import lax
from jax.experimental import pallas as pl
from jax.experimental.pallas import tpu as pltpu
from jax.sharding import PartitionSpec as P

HEADS = 12
HEAD_DIM = 64
EPSILON = 1e-05
ROPE_BASE = 10000.0
MASKED_SCORE = -1e30
VMEM_LIMIT = 62 * 2**20
MESH = pl.DeviceIdType.MESH
BF16 = jnp.bfloat16
F32 = jnp.float32

NAMES = ("y", "xl", "xh", "z")
SIZES = {"y": 4, "xl": 2, "xh": 2, "z": 4, "c": 2}
ORDERS = (("y", "z", "x"), ("z", "x", "y"), ("x", "y", "z"))
ROWS = (192, 192, 192)
FULL = (1, 0, 2)
ATTN = {0: (0, 48), 1: (0, 48), 2: (0, 48)}
EARLY = {0: (48, 96), 1: (48, 96), 2: (48, 96)}
LATE = {0: (144, 48), 1: (144, 48), 2: (144, 48)}
PARTS = (ATTN, EARLY, LATE)


def place():
    f = lax.axis_index("fsdp")
    s = lax.axis_index("seq")
    return {"x": (f // 8) * 2 + s % 2, "y": s // 2, "z": (f // 2) % 4, "c": f % 2}


def device(at):
    return ((at["x"] // 2) * 8 + at["z"] * 2 + at["c"], at["y"] * 2 + at["x"] % 2)


def shifted(at, axis, k):
    return {**at, axis: (at[axis] + k) % SIZES.get(axis, 4)}


def select(names, fixed, half=None):
    index = []
    for n in names:
        size = SIZES[n]
        if half is not None and n == half[0]:
            index.append(pl.ds(half[1] * (size // 2), size // 2))
        elif n in ("xl", "xh"):
            v = fixed.get("x")
            index.append(pl.ds(0, 2) if v is None else (v % 2 if n == "xl" else v // 2))
        else:
            v = fixed.get(n)
            index.append(pl.ds(0, size) if v is None else v)
    return tuple(index)


def expand(axes):
    return [n for a in axes for n in (("xl", "xh") if a == "x" else (a,))]


def kept(names, axes):
    some = expand(axes)
    return tuple(n for n in names if n in some)


def remote(src, dst, send, recv, to):
    return pltpu.make_async_remote_copy(
        src_ref=src, dst_ref=dst, send_sem=send, recv_sem=recv, device_id=to, device_id_type=MESH
    )


def greeting(at):
    f = lax.axis_index("fsdp")
    s = lax.axis_index("seq")
    bar = pltpu.get_barrier_semaphore()
    peers = [(f, (s + k) % 8) for k in range(1, 8)]
    peers += [(f + 1 - 2 * (f % 2), (s + k) % 8) for k in range(8)]
    peers += [device(shifted(at, "z", k)) for k in (1, 2, 3)]
    peers += [device({**at, "x": (at["x"] + 2) % 4})]
    peers += [device({**at, "x": (at["x"] // 2 * 2 + 2) % 4 + (1 - at["x"] % 2)})]
    for p in peers:
        pl.semaphore_signal(bar, inc=1, device_id=p, device_id_type=MESH)
    return bar, len(peers)


def one_hot(rows, slots, per, size, offset, flip=False):
    shape = (slots * size, rows) if flip else (rows, slots * size)
    i = lax.broadcasted_iota(jnp.int32, shape, 1 if flip else 0)
    j = lax.broadcasted_iota(jnp.int32, shape, 0 if flip else 1)
    return (j == (i // per) * size + offset + i % per).astype(BF16)


def units(core, up, flip=False):
    i = lax.broadcasted_iota(jnp.int32, (384, 384), 1 if flip else 0)
    j = lax.broadcasted_iota(jnp.int32, (384, 384), 0 if flip else 1)
    y, r = (i % 192) // 48, i % 48
    early = y * 32 + r + (128 if up else 0)
    late = y * 16 + r - 32 + (320 if up else 256)
    return ((i // 192 == core) & (j == jnp.where(r < 32, early, late))).astype(BF16)


def as_column(row):
    lane = lax.broadcasted_iota(jnp.int32, (6, 6), 1)
    side = lax.broadcasted_iota(jnp.int32, (6, 6), 0)
    return jnp.sum(jnp.where(lane == side, row.astype(F32), 0.0), axis=1, keepdims=True)


def nn(a, b):
    return jnp.dot(a, b, preferred_element_type=F32)


def nt(a, b):
    return lax.dot_general(a, b, (((1,), (1,)), ((), ())), preferred_element_type=F32)


def tn(a, b):
    return lax.dot_general(a, b, (((0,), (0,)), ((), ())), preferred_element_type=F32)


def norm_factor(values):
    return lax.rsqrt(jnp.mean(values * values, axis=-1, keepdims=True) + EPSILON)


def norm_back(values, factor, e):
    return factor * e - values * (factor * factor * factor * jnp.mean(e * values, axis=-1, keepdims=True))


def swap_halves(v):
    lane = lax.broadcasted_iota(jnp.int32, v.shape, 1)
    return jnp.where(lane % 64 < 32, pltpu.roll(v, 96, 1), pltpu.roll(v, 32, 1))


def digits(names, n):
    out = {}
    for name in reversed(names):
        out[name] = n % SIZES[name]
        n = n // SIZES[name]
    return out


def full_index(names, fixed, free, n):
    got = digits(free, n)
    index = []
    for name in names:
        if name in free:
            index.append(got[name])
        elif name in ("xl", "xh"):
            index.append(fixed["x"] % 2 if name == "xl" else fixed["x"] // 2)
        else:
            index.append(fixed[name])
    return tuple(index)


def count(names):
    return math.prod(SIZES[n] for n in names)


def layer_kernel(
    lens, gain_a, gain_m, tok, cot, w_query, w_key, w_value, w_out, w_gate, w_up, w_down,
    out_o, in_o, rows_o, down_o, attn_o,
    a0, a1, a2, w0, w1, w2, g0, g1, g2, h0, h1, h2,
    xa, xat, r0, rd0, s0, d0, s0b, d0b, ks, vs, qs, ps, att, hid, dhid, dqs, cosine, sine, bias, rdn,
    v2s, cs, oacc, eacc, osum, esum, rdc, toks, out_s, in_s, lens_out, lens_in, sab, rab, *rest
):
    at = place()
    f = lax.axis_index("fsdp")
    s = lax.axis_index("seq")
    xl = at["x"] % 2
    here = at["y"] * 2 + at["c"]
    stays = at["c"] == xl
    partner = (f - at["c"] + xl, here)
    t3, t2, t1 = rest[:3], rest[3:6], rest[6:9]
    sem0s, sem0r, semds, semdr, semxs, semxr, sems, semr, semls, semlr, semcs, semcr, semps, sempr = rest[9:23]
    bem0s, bem0r, bemds, bemdr, bems, bemr, bemls, bemlr, bemcs, bemcr = rest[23:33]
    semms, semmr, semys, semyr, semzs, semzr, semws, semwr, semas, semar = rest[33:]
    attn_weights = (a0, a1, a2)
    weights = (w0, w1, w2)
    own_grads = (g0, g1, g2)
    homes = (h0, h1, h2)
    sibling = device(shifted(at, "c", 1))
    xl = at["x"] % 2
    beside = (f, at["y"] * 2 + 1 - xl)
    bar, others = greeting(at)
    gain_one, gain_two = as_column(gain_a[...]), as_column(gain_m[...])
    for r in range(4):
        lens_out[r : r + 1] = jnp.full((1, 128), lens[0, r], jnp.int32).astype(F32)
    lens_out[4:8] = jnp.zeros((4, 128), F32)
    s0[...] = jnp.zeros_like(s0)
    d0[...] = jnp.zeros_like(d0)
    for b in range(8):
        lanes = pl.ds(b * 384, 384)
        half = pl.ds((b % 2) * 384, 384)
        s0[0, b, 0:6] = w_gate[:, lanes].astype(F32) * gain_two
        s0[1, b, 0:6] = w_up[:, lanes].astype(F32) * gain_two
        if b < 6:
            s0[2, b, 0:6] = (w_query, w_key, w_value)[b // 2][:, half].astype(F32) * gain_one
        else:
            s0[2, b, 0:6] = w_out[:, half].astype(F32)
    for b in range(2):
        d0[b, 0:24] = w_down[:, b * 384 : (b + 1) * 384].astype(F32)
    d0b[...] = d0[...].astype(BF16)
    gate_rows = s0[0].reshape(64, 384).astype(BF16)
    up_rows = s0[1].reshape(64, 384).astype(BF16)
    for core in range(2):
        rows = nn(gate_rows, units(core, False)) + nn(up_rows, units(core, True))
        s0b[core] = jnp.concatenate([rows.reshape(8, 8, 384), s0[2]], axis=1).astype(BF16)

    pl.semaphore_wait(bar, others)

    def group(k, src, dst, sends, recvs):
        me = at["c"] * 8 + s
        to, frm = (me + k) % 16, (me - k + 16) % 16
        peer = (f - at["c"] + to // 8, to % 8)
        send, recv = sends.at[k - 1], recvs.at[k - 1]
        out = remote(src.at[to // 8, to % 8], dst.at[me], send, recv, peer)
        inn = remote(src.at[to // 8, to % 8], dst.at[frm], send, recv, peer)
        return out, inn

    def first(k):
        return group(k, s0b, r0, sem0s, sem0r)

    def swap(buf, n):
        c = at["c"]
        return remote(buf.at[c], buf.at[c], semps.at[n], sempr.at[n], sibling)

    def swapped(buf, n):
        c = at["c"]
        return remote(buf.at[c], buf.at[1 - c], semps.at[n], sempr.at[n], sibling)

    def down_copy(slot):
        return remote(d0b.at[1 - xl], rd0.at[slot], semds, semdr, beside)

    def moves(n):
        src = (tok, cot, lens_out)[n]
        dst = (toks, cs.at[xl], lens_in)[n]
        return remote(src, dst, semms.at[n], semmr.at[n], partner)

    def token_out(y):
        return remote(xa.at[here], xa.at[here], semxs.at[y], semxr.at[at["y"]], (f, y * 2 + xl))

    def token_in(y):
        block = xa.at[y * 2 + at["c"]]
        return remote(block, block, semxs.at[y], semxr.at[y], (f, y * 2 + xl))

    def token_across(y):
        mine, other = xa.at[y * 2 + at["c"]], xa.at[y * 2 + 1 - at["c"]]
        send, recv = semys.at[y], semyr.at[y]
        return remote(mine, mine, send, recv, sibling), remote(other, other, send, recv, sibling)

    for k in range(1, 16):
        first(k)[0].start()
    down_copy(xl).start()

    def move():
        for n in (0, 2):
            moves(n).start()

    def stay():
        toks[...] = tok[...]
        cs[xl] = cot[...]
        lens_in[...] = lens_out[...]

    pl.when(jnp.logical_not(stays))(move)
    pl.when(stays)(stay)
    r0[at["c"] * 8 + s] = s0b[at["c"], s]
    rd0[xl] = d0b[xl]

    def rest(i, part):
        return pl.ds(0, 48) if part == 0 else pl.ds(48, ROWS[i] - 48)

    def split(i):
        return "z" if ORDERS[i][2] == "y" else "y"

    def block(i, fixed, core, rows, half=None):
        where = select(NAMES, fixed, half)
        if rows.start < 48:
            return attn_weights[i].at[where + (core,)]
        return weights[i].at[where + (pl.ds(rows.start - 48, rows.size),)]

    def put(i, first_row, value):
        where = select(NAMES, at)
        if first_row < 48:
            attn_weights[i][where + (at["c"],)] = value
        else:
            weights[i][where + (slice(first_row - 48, first_row - 48 + value.shape[0]),)] = value

    def ring(i, part, phase, k):
        order = ORDERS[i]
        axis = order[phase]
        fixed = {n: at[n] for n in ("x", "y", "z") if n not in order[:phase]}
        theirs = {**fixed, axis: (at[axis] - k + 4) % 4}
        rows = pl.ds(*PARTS[part][i])
        mine, other = block(i, fixed, at["c"], rows), block(i, theirs, at["c"], rows)
        slot = 2 * part + phase
        send, recv = sems.at[i, slot, k - 1], semr.at[i, slot, k - 1]
        to = device(shifted(at, axis, k))
        return remote(mine, mine, send, recv, to), remote(other, other, send, recv, to)

    def direct(i, part, k):
        axis = ORDERS[i][2]
        rows = pl.ds(*PARTS[part][i])
        mine = block(i, {axis: at[axis]}, at["c"], rows)
        other = block(i, {axis: (at[axis] - k + 4) % 4}, at["c"], rows)
        send, recv = semls.at[i, part, k - 1], semlr.at[i, part, k - 1]
        to = device(shifted(at, axis, k))
        return remote(mine, mine, send, recv, to), remote(other, other, send, recv, to)

    def relay(i, part, way):
        axis = ORDERS[i][2]
        half, rows = (split(i), way), pl.ds(*PARTS[part][i])
        mine = block(i, {axis: (at[axis] + (3, 1)[way]) % 4}, at["c"], rows, half)
        other = block(i, {axis: (at[axis] + 2) % 4}, at["c"], rows, half)
        send, recv = semls.at[i, part, (1, 3)[way]], semlr.at[i, part, (1, 3)[way]]
        to = device(shifted(at, axis, (1, 3)[way]))
        return remote(mine, mine, send, recv, to), remote(other, other, send, recv, to)

    def across(i, k):
        axis = ORDERS[i][2]
        where = {axis: (at[axis] + k) % 4}
        mine, other = block(i, where, at["c"], rest(i, 0)), block(i, where, 1 - at["c"], rest(i, 0))
        send, recv = semcs.at[i, k], semcr.at[i, k]
        return remote(mine, mine, send, recv, sibling), remote(other, other, send, recv, sibling)

    def start(part, phase):
        for k in (1, 3, 2):
            for i in FULL:
                ring(i, part, phase, k)[0].start()

    def arrive(part, phase):
        for k in (1, 3, 2):
            for i in FULL:
                ring(i, part, phase, k)[1].wait_recv()

    def start_last(part):
        for k in (1, 3) if part else (1, 3, 2):
            for i in PARTS[part]:
                direct(i, part, k)[0].start()

    def pass_last(part):
        for way in range(2):
            for i in PARTS[part]:
                direct(i, part, (1, 3)[way])[1].wait_recv()
                relay(i, part, way)[0].start()

    def arrive_last(part):
        for i in PARTS[part]:
            if part:
                for way in range(2):
                    relay(i, part, way)[1].wait_recv()
            else:
                for k in (1, 3, 2):
                    direct(i, part, k)[1].wait_recv()
                    across(i, (4 - k) % 4)[0].start()

    def sent(part):
        for i in PARTS[part]:
            for k in (1, 3) if part else (1, 2, 3):
                direct(i, part, k)[0].wait_send()
            if part:
                for way in range(2):
                    relay(i, part, way)[0].wait_send()

    for k in range(1, 16):
        first(k)[1].wait_recv()
    flat = r0[...].reshape(256, 384)
    piece = nn(one_hot(48, 16, 6, 16, at["c"] * 128 + 8), flat).astype(BF16)
    for i in range(3):
        put(i, 0, piece[:, i * 128 : (i + 1) * 128])
    start(0, 0)
    piece = nn(one_hot(96, 16, 6, 16, 0), flat).astype(BF16)
    put(0, 48, piece[:, :128])
    put(0, 144, piece[:48, 256:])
    put(1, 48, piece[:, 128:256])
    put(1, 144, piece[48:96, 256:])
    down_copy(1 - xl).wait_recv()
    piece = nn(one_hot(48, 2, 24, 32, 0), rd0[...].reshape(64, 384)).astype(BF16)
    for b in range(3):
        lanes = slice(b * 128, (b + 1) * 128)
        put(2, 48 + 32 * b, piece[:32, lanes])
        put(2, 144 + 16 * b, piece[32:, lanes])
    start(1, 0)
    start(2, 0)

    def arrived():
        for n in (0, 2):
            moves(n).wait()
        moves(1).start()

    pl.when(jnp.logical_not(stays))(arrived)
    inputs = toks[...].astype(F32)
    xa[here] = (inputs * norm_factor(inputs)).astype(BF16)
    for y in range(1, 4):
        pl.when(y > at["y"])(lambda y=y: token_out(y).start())
    pl.when(at["c"] == 0)(lambda: token_across(at["y"])[0].start())
    arrive(0, 0)
    start(0, 1)
    arrive(1, 0)
    start(1, 1)
    arrive(0, 1)
    start_last(0)
    for i in ATTN:
        across(i, 0)[0].start()
    arrive(1, 1)
    start_last(1)
    arrive(2, 0)
    start(2, 1)

    ends = [lens_in[0:1, :]]
    for r in (1, 2):
        ends.append(ends[-1] + lens_in[r : r + 1, :])
    freq_lane = (lax.broadcasted_iota(jnp.int32, (1, 128), 1) % 32).astype(F32)
    freqs = jnp.exp(freq_lane * (-2.0 * math.log(ROPE_BASE) / HEAD_DIM))
    lane = lax.broadcasted_iota(jnp.int32, (128, 128), 1)

    def segment_of(index):
        return sum(jnp.where(index >= e, 1.0, 0.0) for e in ends)

    def table(u, carry):
        index = (u * 128 + lax.broadcasted_iota(jnp.int32, (128, 128), 0)).astype(F32)
        begin = jnp.zeros_like(index)
        for e in ends:
            begin = jnp.where(index >= e, e, begin)
        angle = (index - begin) * freqs
        rows = pl.ds(pl.multiple_of(u * 128, 128), 128)
        cosine[rows, :] = jnp.cos(angle)
        sine[rows, :] = jnp.where(lane % 64 < 32, -1.0, 1.0) * jnp.sin(angle)
        mine = (here * 128 + lax.broadcasted_iota(jnp.int32, (1, 128), 1)).astype(F32)
        allowed = (segment_of(index) == segment_of(mine)) & (index <= mine)
        bias[rows, :] = jnp.where(allowed, 0.0, MASKED_SCORE)
        return carry

    lax.fori_loop(0, 8, table, 0)


    for u in range(1, 8):

        def clear(u=u):
            xa[u] = jnp.zeros((128, 768), BF16)

        pl.when(u > here)(clear)
    for y in range(3):

        def pass_on(y=y):
            token_in(y).wait_recv()
            token_across(y)[0].start()

        pl.when(y < at["y"])(pass_on)
    for y in range(3):
        pl.when(y < at["y"])(lambda y=y: token_across(y)[1].wait_recv())
    pl.when(at["c"] == 1)(lambda: token_across(at["y"])[1].wait_recv())

    def transpose_tokens(u, carry):
        xat[:, pl.ds(pl.multiple_of(u * 128, 128), 128)] = xa[u].T
        return carry

    lax.fori_loop(0, 8, transpose_tokens, 0)
    arrive_last(0)
    for k in range(4):
        for i in ATTN:
            across(i, k)[1].wait_recv()

    for k in range(1, 16):
        first(k)[0].wait_send()
    down_copy(xl).wait_send()
    for y in range(1, 4):
        pl.when(y > at["y"])(lambda y=y: token_out(y).wait_send())
    for y in range(3):
        pl.when(y < at["y"])(lambda y=y: token_across(y)[0].wait_send())
    pl.when(at["c"] == 0)(lambda: token_across(at["y"])[0].wait_send())

    mine = pl.ds(pl.multiple_of(here * 128, 128), 128)
    cos_mine, sin_mine = cosine[mine, :], sine[mine, :]
    left = lax.broadcasted_iota(jnp.int32, (128, 128), 1) < 64

    def attn_weight(kind, t, h):
        return attn_weights[t][kind, h].reshape(768, 128)

    def put_grad(kind, t, h, value):
        own_grads[t][kind, h] = value.reshape(2, 4, 2, 48, 128)

    def attn_full(kind):
        return jnp.concatenate([attn_weight(kind, p % 3, p // 3) for p in range(6)], axis=1)

    def stacked(v):
        zero = jnp.zeros_like(v)
        return jnp.concatenate([jnp.where(left, v, zero), jnp.where(left, zero, v)], axis=0)

    def unstacked(v):
        return jnp.concatenate([v[:64, :128], v[64:, 128:]], axis=0).T

    def pair_lanes(p):
        return pl.ds(pl.multiple_of(p * 128, 128), 128)

    def attend(t, h):
        p = t + 3 * h
        tokens_all = xa[...].reshape(1024, 768)
        w_kv = jnp.concatenate([attn_weight(1, t, h), attn_weight(2, t, h)], axis=1)
        kv = nn(tokens_all, w_kv)
        k_raw = kv[:, :128]
        k = (k_raw * cosine[...] + swap_halves(k_raw) * sine[...]).astype(BF16)
        v = kv[:, 128:].astype(BF16)
        q_raw = nn(xa[here], attn_weight(0, t, h))
        q = ((q_raw * cos_mine + swap_halves(q_raw) * sin_mine).astype(BF16) * (1.0 / math.sqrt(HEAD_DIM))).astype(BF16)
        qq = stacked(q)
        ks[p] = k
        vs[p] = v
        qs[p] = qq
        masks = bias[...]
        scores = nt(k, qq) + jnp.concatenate([masks, masks], axis=1)
        top = jnp.max(scores, axis=0, keepdims=True)
        e = jnp.exp(scores - top)
        total = jnp.sum(e, axis=0, keepdims=True)
        probs = (e * (1.0 / total)).astype(BF16)
        ps[p] = probs
        att[:, pair_lanes(p)] = unstacked(tn(v, probs)).astype(BF16)

    for t in range(3):

        def attend_third(h, carry, t=t):
            attend(t, h)
            return carry

        lax.fori_loop(0, 2, attend_third, 0)
        if t == 0:
            pass_last(1)
        if t == 1:
            arrive(2, 1)
            start_last(2)


    hidden = toks[...].astype(F32) + nn(att[...], attn_full(3))
    hid[...] = hidden
    factor_two = norm_factor(hidden)
    v2s[at["c"]] = (hidden * factor_two).astype(BF16)
    swap(v2s, 1).start()
    pl.when(jnp.logical_not(stays))(lambda: moves(1).wait())
    swap(cs, 0).start()
    oacc[...] = jnp.zeros_like(oacc)
    eacc[...] = jnp.zeros_like(eacc)
    swapped(cs, 0).wait()
    swapped(v2s, 1).wait()
    v2 = v2s[...].reshape(256, 768)
    v2t = v2.T

    def pair(a, b):
        return jnp.concatenate([a, b], axis=1)

    def gated(gate, up, d_w):
        c = cs[...].reshape(256, 768)
        sig = 1.0 / (1.0 + jnp.exp(-gate))
        silu = gate * sig
        mixed = (silu * up).astype(BF16)
        oacc[...] += nn(mixed, d_w).reshape(2, 128, 768)
        d_mixed = nt(c, d_w)
        d_gate = d_mixed * up * sig * (1.0 + gate * (1.0 - sig))
        d_up = d_mixed * silu
        return d_gate, d_up, tn(mixed, c).astype(BF16)

    def down_rows(xh, z, first_row, rows):
        def part(b, h, n):
            some = pl.ds(first_row - 48 + n * rows, rows)
            return w2[:, h, xh, z + b, some].reshape(4 * rows, 128)

        return jnp.concatenate(
            [jnp.concatenate([part(b, h, n) for h in range(2) for n in range(3)], axis=1) for b in range(2)], axis=0
        )

    def put_down(xh, z, first_row, rows, g):
        for b in range(2):
            for h in range(2):
                for n in range(3):
                    some = pl.ds(first_row + n * rows, rows)
                    lanes = slice(h * 384 + n * 128, h * 384 + (n + 1) * 128)
                    h2[:, h, xh, z + b, some] = g[b * 4 * rows : (b + 1) * 4 * rows, lanes].reshape(4, rows, 128)

    def feed_early(y, carry):
        g_w = pair(*(w0[y, b, :, :, 0:96].reshape(768, 128) for b in range(2)))
        u_w = pair(*(w1[y, b, :, :, 0:96].reshape(768, 128) for b in range(2)))
        xh, z = y // 2, (y % 2) * 2
        d_w = down_rows(xh, z, 48, 32)
        d_gate, d_up, g_d = gated(nn(v2, g_w), nn(v2, u_w), d_w)
        d_gate, d_up = d_gate.astype(BF16), d_up.astype(BF16)
        eacc[...] += (nt(d_gate, g_w) + nt(d_up, u_w)).reshape(2, 128, 768)
        g_g = nn(v2t, d_gate).astype(BF16)
        g_u = nn(v2t, d_up).astype(BF16)
        for b in range(2):
            lanes = slice(b * 128, (b + 1) * 128)
            h0[y, b, :, :, 48:144] = g_g[:, lanes].reshape(2, 4, 96, 128)
            h1[y, b, :, :, 48:144] = g_u[:, lanes].reshape(2, 4, 96, 128)
        put_down(xh, z, 48, 32, g_d)
        return carry

    def feed_late(y, carry):
        def weight(b):
            rows = (w0[y, b, :, :, 96:144], w1[y, b, :, :, 96:144])
            return jnp.concatenate(rows, axis=2).reshape(768, 128)

        w = pair(weight(0), weight(1))
        xh, z = y // 2, (y % 2) * 2
        d_w = down_rows(xh, z, 144, 16)
        both = nn(v2, w)
        low = lax.broadcasted_iota(jnp.int32, (256, 128), 1) < 64

        def mix(a, b):
            return jnp.where(low, a, pltpu.roll(b, 64, 1)), jnp.where(low, pltpu.roll(a, 64, 1), b)

        gate, up = mix(both[:, :128], both[:, 128:])
        d_gate, d_up, g_d = gated(gate, up, d_w)
        d_both = pair(*mix(d_gate, d_up)).astype(BF16)
        eacc[...] += nt(d_both, w).reshape(2, 128, 768)
        g = nn(v2t, d_both).astype(BF16)
        for b in range(2):
            rows = g[:, b * 128 : (b + 1) * 128].reshape(2, 4, 96, 128)
            h0[y, b, :, :, 144:192] = rows[:, :, :48]
            h1[y, b, :, :, 144:192] = rows[:, :, 48:96]
        put_down(xh, z, 144, 16, g_d)
        return carry

    def home(i, fixed, part=None, half=None):
        first_row, rows = (0, ROWS[i]) if part is None else PARTS[part][i]
        return homes[i].at[select(NAMES, fixed, half) + (pl.ds(first_row, rows),)]

    def share(i, k):
        where = {ORDERS[i][2]: (at[ORDERS[i][2]] + k) % 4}
        part = own_grads[i].at[select(NAMES, where) + (1 - at["c"],)]
        return remote(part, home(i, where, 0), bemcs.at[i, k], bemcr.at[i, k], sibling)

    def add_core(i, k):
        order = ORDERS[i]
        free = kept(NAMES, order[:2])
        fixed = {order[2]: (at[order[2]] + k) % 4}
        rows = pl.ds(*ATTN[i])

        def body(n, carry):
            index = full_index(NAMES, fixed, free, n)
            total = homes[i][index + (rows,)].astype(F32) + own_grads[i][index + (at["c"],)].astype(F32)
            homes[i][index + (rows,)] = total.astype(BF16)
            return carry

        lax.fori_loop(0, count(free), body, 0, unroll=4)

    def halfway(i, part, way):
        axis = ORDERS[i][2]
        half = (split(i), way)
        src = home(i, {axis: (at[axis] + 2) % 4}, part, half)
        dst = t3[i].at[(1,) + select(kept(NAMES, ORDERS[i][:2]), {}, half) + (pl.ds(*PARTS[part][i]),)]
        send, recv = bemls.at[i, part, way], bemlr.at[i, part, way]
        return remote(src, dst, send, recv, device(shifted(at, axis, (1, 3)[way])))

    def whole(i, part, way):
        axis = ORDERS[i][2]
        src = home(i, {axis: (at[axis] + (1, 3)[way]) % 4}, part)
        dst = t3[i].at[2 * way, :, :, :, pl.ds(*PARTS[part][i])] if ORDERS[i][2] != "x" else t3[i].at[
            2 * way, :, :, pl.ds(*PARTS[part][i])
        ]
        send, recv = bemls.at[i, part, 2 + way], bemlr.at[i, part, 2 + way]
        return remote(src, dst, send, recv, device(shifted(at, axis, (1, 3)[way])))

    def add_half(i, part, way):
        order = ORDERS[i]
        where = split(i)
        free = kept(NAMES, order[:2])
        turned = (where,) + tuple(m for m in free if m != where)
        fixed = {order[2]: (at[order[2]] + (1, 3)[way]) % 4}
        rows = pl.ds(*PARTS[part][i])

        def body(n, carry):
            got = digits(turned, n)
            got[where] = got[where] + way * (SIZES[where] // 2)
            n = 0
            for m in free:
                n = n * SIZES[m] + got[m]
            index = full_index(NAMES, fixed, free, n) + (rows,)
            came = t3[i][(1,) + tuple(got[m] for m in free) + (rows,)]
            homes[i][index] = (homes[i][index].astype(F32) + came.astype(F32)).astype(BF16)
            return carry

        lax.fori_loop(0, count(free) // 2, body, 0, unroll=4)

    def add_whole(i, part):
        order = ORDERS[i]
        free = kept(NAMES, order[:2])
        fixed = {order[2]: at[order[2]]}
        rows = pl.ds(*PARTS[part][i])

        def body(n, carry):
            index = full_index(NAMES, fixed, free, n) + (rows,)
            there = full_index(free, {}, free, n) + (rows,)
            total = homes[i][index].astype(F32)
            for k in (0, 2) if part else (0, 1, 2):
                total = total + t3[i][(k,) + there].astype(F32)
            homes[i][index] = total.astype(BF16)
            return carry

        lax.fori_loop(0, count(free), body, 0, unroll=4)

    def hop(i, part, left, k):
        order = ORDERS[i]
        axis = order[left - 1]
        fixed = {a: at[a] for a in order[left:]}
        rows = rest(i, part)
        src = homes[i].at[select(NAMES, {**fixed, axis: (at[axis] + k) % 4}) + (rows,)]
        if left == 1:
            dst = t1[i].at[k - 1, rows]
        else:
            dst = t2[i].at[(k - 1,) + select(kept(NAMES, order[:1]), {}) + (rows,)]
        slot = 2 * part + left - 1
        send, recv = bems.at[i, slot, k - 1], bemr.at[i, slot, k - 1]
        return remote(src, dst, send, recv, device(shifted(at, axis, k)))

    def add_ring(i, part):
        order = ORDERS[i]
        free = kept(NAMES, order[:1])
        fixed = {a: at[a] for a in order[1:]}
        rows = rest(i, part)

        def body(n, carry):
            index = full_index(NAMES, fixed, free, n) + (rows,)
            total = homes[i][index].astype(F32)
            for k in range(3):
                total = total + t2[i][(k,) + full_index(free, {}, free, n) + (rows,)].astype(F32)
            homes[i][index] = total.astype(BF16)
            return carry

        lax.fori_loop(0, count(free), body, 0)

    def hop_start(part):
        for k in (1, 3, 2):
            for i in FULL:
                hop(i, part, 2, k).start()

    def hop_on(part):
        for i in FULL:
            for k in (1, 3, 2):
                hop(i, part, 2, k).wait_recv()
            add_ring(i, part)
            for k in (1, 3, 2):
                hop(i, part, 1, k).start()

    def last(i, part):
        for k in (1, 3, 2):
            hop(i, part, 1, k).wait_recv()
        rows = rest(i, part)
        total = homes[i][select(NAMES, at) + (rows,)].astype(F32)
        for k in range(3):
            total = total + t1[i][k, rows].astype(F32)
        return total.astype(BF16)

    def hop_last(i, k):
        axis = ORDERS[i][2]
        src = home(i, {axis: (at[axis] + k) % 4}, 0)
        rows = pl.ds(*ATTN[i])
        dst = t3[i].at[(k - 1,) + select(kept(NAMES, ORDERS[i][:2]), {}) + (rows,)]
        send, recv = bemls.at[i, 0, k - 1], bemlr.at[i, 0, k - 1]
        return remote(src, dst, send, recv, device(shifted(at, axis, k)))

    def half_start(part, items=FULL):
        for way in range(2):
            for i in items:
                if i in PARTS[part]:
                    halfway(i, part, way).start()

    def half_on(part, items=FULL):
        for way in range(2):
            for i in items:
                if i in PARTS[part]:
                    halfway(i, part, way).wait_recv()
                    add_half(i, part, way)
                    whole(i, part, way).start()

    def whole_on(part):
        for i in PARTS[part]:
            if part:
                for way in range(2):
                    whole(i, part, way).wait_recv()
            else:
                for k in (1, 3, 2):
                    hop_last(i, k).wait_recv()
            add_whole(i, part)

    for i in FULL:
        for part in range(3):
            for phase in range(2):
                for k in (1, 2, 3):
                    ring(i, part, phase, k)[0].wait_send()
    arrive_last(1)
    feed_early(0, 0)
    pass_last(2)
    for y in range(1, 4):
        feed_early(y, 0)
    half_start(1)
    arrive_last(2)
    for y in range(4):
        feed_late(y, 0)
    sum_o = remote(oacc.at[1 - at["c"]], osum, semps.at[2], sempr.at[2], sibling)
    sum_e = remote(eacc.at[1 - at["c"]], esum, semps.at[3], sempr.at[3], sibling)
    sum_e.start()
    sum_o.start()
    half_start(2)
    half_on(1)
    sum_e.wait()

    hidden = hid[...]
    factor_two = norm_factor(hidden)
    d_hidden = cs[at["c"]].astype(F32) + norm_back(hidden, factor_two, eacc[at["c"]] + esum[...])
    dhid[...] = d_hidden
    dh = d_hidden.astype(BF16)
    d_att = nt(dh, attn_full(3)).astype(BF16)
    att_t = att[...].T
    for j in range(2):
        g_o = nn(att_t, dh[:, j * 384 : (j + 1) * 384]).astype(BF16)
        for t in range(3):
            put_grad(3, t, j, g_o[:, t * 128 : (t + 1) * 128])
    att[...] = d_att

    def attend_back(t, h):
        p = t + 3 * h
        da = stacked(att[:, pair_lanes(p)])
        k, v, qq, probs = ks[p], vs[p], qs[p], ps[p]
        d_probs = nt(v, da)
        probs_f = probs.astype(F32)
        d_sum = jnp.sum(probs_f * d_probs, axis=0, keepdims=True)
        d_scores = (probs_f * (d_probs - d_sum)).astype(BF16)
        d_v = nn(probs, da).astype(BF16)
        d_k = nn(d_scores, qq)
        d_k = (d_k * cosine[...] - swap_halves(d_k) * sine[...]).astype(BF16)
        d_q = unstacked(tn(k, d_scores)) * (1.0 / math.sqrt(HEAD_DIM))
        d_q = (d_q * cos_mine - swap_halves(d_q) * sin_mine).astype(BF16)
        ks[p] = d_k
        vs[p] = d_v
        dqs[:, pair_lanes(p)] = d_q
        g_kv = nn(xat[...], jnp.concatenate([d_k, d_v], axis=1)).astype(BF16)
        g_q = nn(xat[:, mine], d_q).astype(BF16)
        put_grad(0, t, h, g_q)
        put_grad(1, t, h, g_kv[:, :128])
        put_grad(2, t, h, g_kv[:, 128:])

    def share_on(i):
        for k in (2, 1, 3, 0):
            share(i, k).wait_recv()
            add_core(i, k)
            if k:
                hop_last(i, k).start()

    half_on(2)
    def third_back(h, carry):
        attend_back(0, h)
        return carry

    attend_back(0, 0)
    attend_back(0, 1)

    def share_start(i):
        for k in (2, 1, 3, 0):
            share(i, k).start()

    share_start(0)
    attend_back(1, 0)
    share_on(0)
    attend_back(1, 1)
    share_start(1)
    attend_back(2, 0)
    share_on(1)
    attend_back(2, 1)
    share_start(2)
    whole_on(1)
    share_on(2)
    whole_on(2)
    hop_start(1)

    w_kv = jnp.concatenate([attn_full(1), attn_full(2)], axis=1)

    def tokens_back(u, carry):
        rows = pl.ds(pl.multiple_of(u * 128, 128), 128)
        d_kv = jnp.concatenate([ks[p, rows, :] for p in range(6)] + [vs[p, rows, :] for p in range(6)], axis=1)
        xa[u] = nt(d_kv, w_kv).astype(BF16)
        return carry

    lax.fori_loop(0, 8, tokens_back, 0)

    def grad_across(y):
        mine = xa.at[y * 2 + 1 - at["c"]]
        return remote(mine, rdc.at[y], semzs.at[y], semzr.at[y], sibling)

    def grad_out(y):
        return remote(xa.at[y * 2 + at["c"]], rdn.at[at["y"]], semws.at[y], semwr.at[at["y"]], (f, y * 2 + xl))

    def grad_in(y):
        return remote(xa.at[y * 2 + at["c"]], rdn.at[y], semws.at[y], semwr.at[y], (f, y * 2 + xl))

    for y in range(3):
        pl.when(y < at["y"])(lambda y=y: grad_across(y).start())
    pl.when(at["c"] == 1)(lambda: grad_across(at["y"]).start())
    for y in range(3):

        def add_across(y=y):
            grad_across(y).wait_recv()
            block = xa[y * 2 + at["c"]].astype(F32) + rdc[y].astype(F32)
            xa[y * 2 + at["c"]] = block.astype(BF16)
            grad_out(y).start()

        pl.when(y < at["y"])(add_across)
    sum_o.wait()
    out_s[...] = (hid[...] + oacc[at["c"]] + osum[...]).astype(BF16)

    def out_move():
        return remote(out_s, out_o, semms.at[3], semmr.at[3], partner)

    def out_stay():
        out_o[...] = out_s[...]

    pl.when(jnp.logical_not(stays))(lambda: out_move().start())
    pl.when(stays)(out_stay)
    esum[...] = nt(dqs[...], attn_full(0))

    hop_on(1)
    whole_on(0)
    hop_start(0)
    sum0, sum1, sum2 = last(0, 1), last(1, 1), last(2, 1)
    down = jnp.concatenate(
        [
            jnp.concatenate([sum2[a + b * n : a + b * (n + 1)] for n in range(3)], axis=1)
            for a, b in ((0, 32), (96, 16))
        ],
        axis=0,
    )
    mixed_units = jnp.concatenate([sum0[96:144], sum1[96:144]], axis=0)
    both = jnp.concatenate([sum0[0:96], sum1[0:96], mixed_units], axis=1)
    rows_mlp = nn(one_hot(96, 16, 6, 16, 0, True), both)
    d0b[...] = nn(one_hot(48, 2, 24, 32, 0, True), down).astype(BF16).reshape(2, 32, 384)
    s0b[...] = rows_mlp.astype(BF16).reshape(2, 8, 16, 384)

    def final(k):
        return group(k, s0b, r0, bem0s, bem0r)

    def final_down(slot):
        return remote(d0b.at[1 - xl], rd0.at[slot], bemds, bemdr, beside)

    for k in range(1, 16):
        final(k)[0].start()
    final_down(xl).start()
    hop_on(0)

    esum[...] += xa[here].astype(F32)

    def add_own():
        grad_across(at["y"]).wait_recv()
        esum[...] += rdc[at["y"]].astype(F32)

    pl.when(at["c"] == 0)(add_own)
    for y in range(1, 4):

        def add(y=y):
            grad_in(y).wait_recv()
            esum[...] += rdn[y].astype(F32)

        pl.when(y > at["y"])(add)
    inputs = toks[...].astype(F32)
    in_s[...] = dhid[...] + norm_back(inputs, norm_factor(inputs), esum[...])

    def in_move():
        return remote(in_s, in_o, semms.at[4], semmr.at[4], partner)

    def in_stay():
        in_o[...] = in_s[...]

    pl.when(jnp.logical_not(stays))(lambda: in_move().start())
    pl.when(stays)(in_stay)
    attn = jnp.concatenate([last(i, 0) for i in range(3)], axis=1)
    rows = nn(one_hot(48, 8, 6, 16, 0, True), attn)
    sab[...] = rows.astype(BF16).reshape(8, 16, 384)

    def final_attn(k):
        to, frm = (s + k) % 8, (s - k + 8) % 8
        out = remote(sab.at[to], rab.at[s], semas.at[k - 1], semar.at[k - 1], (f, to))
        inn = remote(sab.at[to], rab.at[frm], semas.at[k - 1], semar.at[k - 1], (f, to))
        return out, inn

    for k in range(1, 8):
        final_attn(k)[0].start()
    rab[s] = sab[s]
    r0[at["c"] * 8 + s] = s0b[at["c"], s]
    rd0[xl] = d0b[xl]
    for k in range(1, 16):
        final(k)[1].wait_recv()
    final_down(1 - xl).wait_recv()
    rows_o[...] = r0[...]
    down_o[...] = rd0[...]
    for k in range(1, 8):
        final_attn(k)[1].wait_recv()
    attn_o[...] = rab[...]
    for k in range(1, 16):
        final(k)[0].wait_send()
    for k in range(1, 8):
        final_attn(k)[0].wait_send()
    final_down(xl).wait_send()
    for y in range(3):

        def across_sent(y=y):
            grad_across(y).wait_send()
            grad_out(y).wait_send()

        pl.when(y < at["y"])(across_sent)
    pl.when(at["c"] == 1)(lambda: grad_across(at["y"]).wait_send())

    def moved():
        out_move().wait()
        in_move().wait()

    pl.when(jnp.logical_not(stays))(moved)
    for part in range(3):
        sent(part)
    for i in ATTN:
        for k in range(4):
            across(i, k)[0].wait_send()
            share(i, k).wait_send()
    for i in ATTN:
        for k in (1, 2, 3):
            hop_last(i, k).wait_send()
    for part in (1, 2):
        for i in PARTS[part]:
            for way in range(2):
                halfway(i, part, way).wait_send()
                whole(i, part, way).wait_send()
    for part in range(2):
        for i in FULL:
            for left in (2, 1):
                for k in (1, 2, 3):
                    hop(i, part, left, k).wait_send()


def finish_kernel(gain_a, gain_m, w_query, w_key, w_value, w_gate, w_up, rows_i, down_i, attn_i, out_i, in_i,
                  out_o, in_o, ga1_o, gq_o, gk_o, gv_o, go_o, ga2_o, gg_o, gu_o, gd_o, s0):
    out_o[...] = out_i[...]
    in_o[...] = in_i[...]
    def as_row(col):
        lane = lax.broadcasted_iota(jnp.int32, (6, 6), 1)
        side = lax.broadcasted_iota(jnp.int32, (6, 6), 0)
        return jnp.sum(jnp.where(lane == side, col, 0.0), axis=0, keepdims=True)

    gain_one, gain_two = as_column(gain_a[...]), as_column(gain_m[...])
    got = rows_i[...].reshape(2, 8, 16, 384)
    halves = [got[core, :, :8].reshape(64, 384) for core in range(2)]
    for which in range(2):
        natural = nn(halves[0], units(0, which == 1, True)) + nn(halves[1], units(1, which == 1, True))
        s0[which] = natural.reshape(8, 8, 384)
    s0[2] = attn_i[:, 0:8, :].astype(F32)
    down = down_i[...].astype(F32)
    gain_sum_one = jnp.zeros((6, 1), F32)
    gain_sum_two = jnp.zeros((6, 1), F32)
    for b in range(8):
        lanes = pl.ds(b * 384, 384)
        half = pl.ds((b % 2) * 384, 384)
        h_gate, h_up, h_attn = s0[0, b, 0:6], s0[1, b, 0:6], s0[2, b, 0:6]
        gg_o[:, lanes] = h_gate * gain_two
        gu_o[:, lanes] = h_up * gain_two
        gain_sum_two += jnp.sum(h_gate * w_gate[:, lanes].astype(F32), axis=1, keepdims=True)
        gain_sum_two += jnp.sum(h_up * w_up[:, lanes].astype(F32), axis=1, keepdims=True)
        if b < 6:
            (gq_o, gk_o, gv_o)[b // 2][:, half] = h_attn * gain_one
            raw = (w_query, w_key, w_value)[b // 2][:, half].astype(F32)
            gain_sum_one += jnp.sum(h_attn * raw, axis=1, keepdims=True)
        else:
            go_o[:, half] = h_attn
    for b in range(2):
        gd_o[:, b * 384 : (b + 1) * 384] = down[b, 0:24]
    ga1_o[...] = as_row(gain_sum_one)
    ga2_o[...] = as_row(gain_sum_two)


VMEM_SPEC = pl.BlockSpec(memory_space=pltpu.VMEM)
SMEM_SPEC = pl.BlockSpec(memory_space=pltpu.SMEM)
DMA = pltpu.SemaphoreType.DMA


def layer(lens, *arrays):
    outs = [((128, 768), BF16), ((128, 768), F32), ((16, 16, 384), BF16), ((2, 32, 384), BF16), ((8, 16, 384), BF16)]
    sizes = tuple(SIZES[n] for n in NAMES)
    scratch = [(sizes + (2, 48, 128), BF16) for _ in ROWS] + [(sizes + (r - 48, 128), BF16) for r in ROWS]
    scratch += [(sizes + (2, 48, 128), BF16) for _ in ROWS]
    scratch += [(sizes + (r, 128), BF16) for r in ROWS]
    scratch += [
        ((8, 128, 768), BF16), ((768, 1024), BF16), ((16, 16, 384), BF16), ((2, 32, 384), BF16),
        ((3, 8, 8, 384), F32), ((2, 32, 384), F32), ((2, 8, 16, 384), BF16), ((2, 32, 384), BF16),
        ((6, 1024, 128), BF16), ((6, 1024, 128), BF16), ((6, 256, 128), BF16), ((6, 1024, 256), BF16),
        ((128, 768), BF16), ((128, 768), F32), ((128, 768), F32), ((128, 768), BF16),
        ((1024, 128), F32), ((1024, 128), F32), ((1024, 128), F32), ((4, 128, 768), BF16),
        ((2, 128, 768), BF16), ((2, 128, 768), BF16), ((2, 128, 768), F32), ((2, 128, 768), F32),
        ((128, 768), F32), ((128, 768), F32), ((4, 128, 768), BF16), ((128, 768), BF16), ((128, 768), BF16), ((128, 768), F32),
        ((8, 128), F32), ((8, 128), F32), ((8, 16, 384), BF16), ((8, 16, 384), BF16),
    ]
    for rings in (2, 1, 0):
        for i in range(3):
            left = tuple(SIZES[n] for n in kept(NAMES, ORDERS[i][:rings]))
            scratch.append(((3,) + left + (ROWS[i], 128), BF16))
    copies = [
        DMA((15,)), DMA((15,)), DMA, DMA, DMA((4,)), DMA((4,)),
        DMA((3, 6, 3)), DMA((3, 6, 3)), DMA((3, 3, 4)), DMA((3, 3, 4)), DMA((3, 4)), DMA((3, 4)), DMA((4,)), DMA((4,)),
        DMA((15,)), DMA((15,)), DMA, DMA,
        DMA((3, 4, 3)), DMA((3, 4, 3)), DMA((3, 3, 4)), DMA((3, 3, 4)), DMA((3, 4)), DMA((3, 4)),
        DMA((5,)), DMA((5,)), DMA((4,)), DMA((4,)), DMA((4,)), DMA((4,)), DMA((4,)), DMA((4,)), DMA((7,)), DMA((7,)),
    ]
    return pl.pallas_call(
        layer_kernel,
        out_shape=[jax.ShapeDtypeStruct(shape, kind) for shape, kind in outs],
        in_specs=[SMEM_SPEC] + [VMEM_SPEC] * 11,
        out_specs=[VMEM_SPEC] * len(outs),
        scratch_shapes=[pltpu.VMEM(shape, kind) for shape, kind in scratch] + copies,
        compiler_params=pltpu.CompilerParams(collective_id=0, has_side_effects=True, vmem_limit_bytes=VMEM_LIMIT),
        name="layer",
    )(lens, *arrays)


def finish(*arrays):
    outs = [
        ((128, 768), BF16), ((128, 768), F32), ((1, 6), F32),
        ((6, 768), F32), ((6, 768), F32), ((6, 768), F32), ((6, 768), F32),
        ((1, 6), F32), ((6, 3072), F32), ((6, 3072), F32), ((24, 768), F32),
    ]
    return pl.pallas_call(
        finish_kernel,
        out_shape=[jax.ShapeDtypeStruct(shape, kind) for shape, kind in outs],
        in_specs=[VMEM_SPEC] * 12,
        out_specs=[VMEM_SPEC] * len(outs),
        scratch_shapes=[pltpu.VMEM((3, 8, 8, 384), F32)],
        name="finish",
    )(*arrays)


def per_device(tokens, doc_lengths, attn_gain, w_query, w_key, w_value, w_out, mlp_gain, w_gate, w_up, w_down, cotangent):
    gains = (attn_gain.reshape(1, 6), mlp_gain.reshape(1, 6))
    layer_out, input_grad, rows, down, rows_attn = layer(
        doc_lengths, *gains, tokens[0], cotangent[0], w_query, w_key, w_value, w_out, w_gate, w_up, w_down
    )
    out = finish(*gains, w_query, w_key, w_value, w_gate, w_up, rows, down, rows_attn, layer_out, input_grad)
    return (out[0][None], out[1][None], out[2][0]) + tuple(out[3:7]) + (out[7][0],) + tuple(out[8:])


def solution(mesh):
    rows = P(("fsdp", "seq"), None)
    gain = P(("fsdp", "seq"))
    toks = P("fsdp", "seq", None)
    return jax.shard_map(
        per_device,
        mesh=mesh,
        in_specs=(toks, P("fsdp", None), gain, rows, rows, rows, rows, gain, rows, rows, rows, toks),
        out_specs=(toks, toks, gain, rows, rows, rows, rows, gain, rows, rows, rows),
        check_vma=False,
    )
```
